256 devices in a mesh: blk: 16 (over z, core), uly: 16 (over y, x).
Axes of the slice: x: 4, y: 4, z: 8, core: 2. Of those that a mesh axis runs over, the one named last changes fastest.
Arguments:
- query: bfloat16 [2048, 6144], P('blk', 'uly'), may hold values from -21 to 21
- key: bfloat16 [2048, 6144], P('blk', 'uly'), may hold values from -3 to 3
- value: bfloat16 [2048, 6144], P('blk', 'uly'), may hold values from -6 to 6
- grad_out: bfloat16 [2048, 6144], P('blk', 'uly'), may hold values from -6 to 6
- tile_mask: int32 [48, 16, 16], replicated, may hold values from 0 to 1, as said below
- tile_order: int32 [16], replicated, may hold values from 0 to 15, each once
Outputs:
- grad_query: bfloat16 [2048, 6144], P(('blk', 'uly'))
- grad_key: bfloat16 [2048, 6144], P(('blk', 'uly'))
- grad_value: bfloat16 [2048, 6144], P(('blk', 'uly'))
The draws below stay inside these ranges and needn't reach their ends.
Inputs may be any that keep to these rules, and one draw needn't show every extreme that they name: `tile_mask`: every head keeps the diagonal tiles (a tile with itself); rows of tiles keep different shares.
All inputs are finite; a program needn't handle non-finite values.
Results may differ from the reference program's by a relative error of at most 0.007.
Values may be sent and summed in bfloat16 or wider, within the bound.
A program may use at most 64 MiB of HBM per device.

```python
import jax
import jax.numpy as jnp
from jax import lax

H = 48
DH = 128
TILE = 128
S = 2048
TILES = 16


def keys_common(key, spread):
    base = jax.random.uniform(key, (S, H * DH), jnp.float32, -spread, spread)
    picked = (jnp.arange(S) % 64 == 6)[:, None]
    return jnp.where(picked, base, base)


def draw_key(key, part):
    result = keys_common(key, 1.7)
    return result.astype(jnp.bfloat16)


def draw_query(key, part):
    own_key = jax.random.fold_in(key, 3)
    result = jnp.clip(jax.random.normal(own_key, (S, H * DH), jnp.float32), -6.0, 6.0)
    return result.astype(jnp.bfloat16)


def draw_tile_mask(key, part):
    key = jax.random.fold_in(key, 7)
    rate_key, value_key = jax.random.split(key)
    rates = jax.random.randint(rate_key, (H, TILES, 1), 1, 16)
    values = jax.random.randint(value_key, (H, TILES, TILES), 0, 100)
    diagonal = (jnp.arange(TILES)[:, None] == jnp.arange(TILES)[None, :])[None, :, :]
    return jnp.where((values < rates) | diagonal, 1, 0).astype(jnp.int32)


def level_of(key, dims, pieces, low, top_value):
    loudness = 1.0
    for position, blocks in pieces:
        draws = jax.random.uniform(jax.random.fold_in(jax.random.fold_in(key, 6), position), (blocks,), jnp.float32, low / len(pieces), top_value / len(pieces))
        loudness = loudness * jnp.repeat(jnp.exp(draws), dims[position] // blocks).reshape((-1,) + (1,) * (len(dims) - 1 - position))
    return loudness


def bell_draw(stream_key, dims, scale, most, shards=(), kind=jnp.bfloat16):
    entries = jax.random.normal(stream_key, dims, jnp.float32) * scale
    if len(shards) > 0:
        entries = level_of(stream_key, dims, shards, -0.22, 0.18) * entries
    return jnp.clip(entries, min=-most, max=most).astype(kind)


def setup_inputs(seed: int = 0) -> dict:
    keys = jax.random.split(jax.random.key(seed), 7)
    query = draw_query(jax.random.fold_in(keys[6], 71), 0)
    key = draw_key(jax.random.fold_in(keys[6], 71), 0)
    value = bell_draw(keys[2], (S, H * DH), 1.0, 6.0, ((0, 16), (1, 16)))
    grad_out = bell_draw(keys[3], (S, H * DH), 1.0, 6.0, ((0, 16), (1, 16)))
    tile_mask = draw_tile_mask(jax.random.fold_in(keys[6], 71), 0)
    tile_order = jax.random.permutation(keys[5], TILES).astype(jnp.int32)
    return {"query": query, "key": key, "value": value, "grad_out": grad_out, "tile_mask": tile_mask, "tile_order": tile_order}


def reference(query, key, value, grad_out, tile_mask, tile_order):
    factor = DH ** -0.5
    queries = query.reshape(S, H, DH)
    keys_all = key.reshape(S, H, DH)
    values_all = value.reshape(S, H, DH)
    cotangent = grad_out.reshape(S, H, DH)
    identity = tile_order[jnp.arange(S, dtype=jnp.int32) // TILE]

    def one_head(head):
        head_mask = tile_mask[head]
        allowed = head_mask[identity][:, identity] > 0
        q_head = queries[:, head]
        k_head = keys_all[:, head]
        v_head = values_all[:, head]
        g_head = cotangent[:, head]
        scores = jnp.dot(q_head, k_head.T, preferred_element_type=jnp.float32) * factor
        largest = jnp.max(jnp.where(allowed, scores, -jnp.inf), axis=1)
        total = jnp.sum(jnp.where(allowed, jnp.exp(scores - largest[:, None]), 0.0), axis=1)
        lse = largest + jnp.log(total)
        prob = jnp.where(allowed, jnp.exp(scores - lse[:, None]), 0.0)
        prob_b = prob.astype(jnp.bfloat16)
        output = jnp.dot(prob_b, v_head, preferred_element_type=jnp.float32)
        delta = jnp.sum(g_head.astype(jnp.float32) * output, axis=1)
        dprob = jnp.dot(g_head, v_head.T, preferred_element_type=jnp.float32)
        dscore = (prob * (dprob - delta[:, None]) * factor).astype(jnp.bfloat16)
        grad_q = jnp.dot(dscore, k_head, preferred_element_type=jnp.float32).astype(jnp.bfloat16)
        grad_k = jnp.dot(dscore.T, q_head, preferred_element_type=jnp.float32).astype(jnp.bfloat16)
        grad_v = jnp.dot(prob_b.T, g_head, preferred_element_type=jnp.float32).astype(jnp.bfloat16)
        return grad_q, grad_k, grad_v

    grads = lax.map(one_head, jnp.arange(H, dtype=jnp.int32))
    result = [jnp.transpose(piece, (1, 0, 2)).reshape(S, H * DH) for piece in grads]
    return result[0], result[1], result[2]
```

```python
import functools

import jax
import jax.numpy as jnp
from jax import lax
from jax.experimental import pallas as pl
from jax.experimental.pallas import tpu as pltpu
from jax.sharding import PartitionSpec as P

H = 48
DH = 128
TILE = 128
NZ = 8
NU = 16
SLOTS = 2
WIDE = 6
COUNT = 32
MESH = pl.DeviceIdType.MESH
FACTOR = DH ** -0.5
LOG2E = 1.4426950408889634
F32 = jnp.float32
BF16 = jnp.bfloat16


def nt(a, b):
    return lax.dot_general(a, b, (((1,), (1,)), ((), ())), preferred_element_type=F32)


def nn(a, b):
    return lax.dot_general(a, b, (((1,), (0,)), ((), ())), preferred_element_type=F32)


def lift(u):
    x, y = lax.rem(u, 4), lax.div(u, 4)
    return lax.rem(2 * x + 4 * lax.rem(y, 2) + lax.div(y, 2), NZ)


def beside(u):
    x, y = lax.rem(u, 4), lax.div(u, 4)
    other = y + 1 - 2 * lax.rem(y, 2)
    return 4 * y + lax.rem(x + 1, 4), 4 * other + x, 4 * y + lax.rem(x + 3, 4)


def hosted(z, u):
    rel = lax.rem(z - lift(u) + NZ, NZ)
    yes = jnp.logical_or(rel == 0, jnp.logical_or(rel == 3, rel == 6))
    return yes, lax.div(rel, 3)


def remote(src, dst, send, recv, there):
    return pltpu.make_async_remote_copy(
        src_ref=src, dst_ref=dst, send_sem=send, recv_sem=recv,
        device_id=there, device_id_type=MESH,
    )


def arrived(ref, sem):
    pltpu.make_async_copy(ref, ref, sem).wait()


def place():
    blk = lax.axis_index("blk")
    u = lax.axis_index("uly")
    z = lax.div(blk, 2)
    c = lax.rem(blk, 2)
    yes, mine = hosted(z, u)
    return blk, u, z, c, jnp.logical_and(yes, c == lax.rem(mine, 2)), mine


def collect(
    q_in, k_in, v_in, g_in, mask_in, order_ref, kv, qg, picked,
    mask, passing, in_send, kv_sem, qg_sem, mask_sem, pass_sem, pass_send,
):
    blk, u, z, c, is_host, mine = place()
    via = beside(u)
    served = (via[2], via[1], via[0])
    barrier = pltpu.get_barrier_semaphore()

    def greet(there):
        pl.semaphore_signal(barrier, inc=1, device_id=there, device_id_type=MESH)

    get_mask = pltpu.make_async_copy(mask_in, mask, mask_sem)

    @pl.when(is_host)
    def _():
        get_mask.start()

        def greet_line(n, carry):
            greet((lax.rem(blk + n, 2 * NZ), u))
            return carry

        lax.fori_loop(1, 2 * NZ, greet_line, 0)

    for line in served:
        greet((blk, line))

    pl.semaphore_wait(barrier, 3 + 3 - is_host.astype(jnp.int32))

    def inputs(l):
        host = lax.rem(lift(u) + 3 * l, NZ)
        r = lax.rem(z - host + NZ, NZ)
        cols = pl.ds(l * DH, DH)
        there = (2 * host + l % 2, u)
        home = (
            (k_in, kv.at[c, r, 0], kv_sem),
            (v_in, kv.at[c, r, 1], kv_sem),
            (q_in, qg.at[c, r, 0], qg_sem),
            (g_in, qg.at[c, r, 1], qg_sem),
        )
        home = [(src.at[:, cols], dst, sem) for src, dst, sem in home]
        straight = [(src, dst, in_send, sem, there) for src, dst, sem in home]
        around = [
            (home[n + 1][0], passing.at[n, l], in_send, pass_sem.at[n, l], (blk, via[n]))
            for n in range(3)
        ] + straight[:1]
        return host, home, straight, around

    for l in range(3):
        host, home, straight, around = inputs(l)

        @pl.when(host != z)
        def _():
            for move in around:
                remote(*move).start()

        @pl.when(jnp.logical_and(host == z, c != l % 2))
        def _():
            for move in straight:
                remote(*move).start()

        @pl.when(jnp.logical_and(host == z, c == l % 2))
        def _():
            for move in home:
                pltpu.make_async_copy(*move).start()

    @pl.when(is_host)
    def _():
        row = lax.broadcasted_iota(jnp.int32, (16, 16), 0)
        lane = lax.broadcasted_iota(jnp.int32, (16, 16), 1)
        ident = jnp.zeros((16, 16), jnp.int32)
        for j in range(16):
            ident = jnp.where(row == j, order_ref[2 * lax.rem(z + j % NZ, NZ) + j // NZ], ident)
        hot = jnp.where(lane == ident, 1.0, 0.0).astype(BF16)
        wide = lax.broadcasted_iota(jnp.int32, (16, 128), 1)
        hot_wide = jnp.where(wide == ident[:, :1], 1.0, 0.0).astype(BF16)
        get_mask.wait()
        flat = jnp.where(mask[...] > 0, 1.0, 0.0).reshape(256, H).astype(BF16)
        head = lax.broadcasted_iota(jnp.int32, (H, 128), 0) == 3 * u + mine
        picked_out = nn(flat, jnp.where(head, 1.0, 0.0).astype(BF16))
        tall = lax.broadcasted_iota(jnp.int32, (16, 16, 128), 1)
        across = lax.broadcasted_iota(jnp.int32, (16, 16, 128), 2)
        table = jnp.where(tall == across, picked_out.reshape(16, 16, 128), 0.0)
        table = jnp.sum(table, axis=1).astype(BF16)
        by_query = nn(hot, table).astype(BF16)
        allowed = nt(by_query, hot_wide)
        before = jnp.where(row < lane, 1.0, 0.0).astype(BF16)
        rank = nn(allowed.astype(BF16), before)
        listed = jnp.where(wide == COUNT, jnp.sum(allowed, axis=1, keepdims=True), 0.0)
        for n in range(16):
            here = jnp.logical_and(allowed > 0.5, jnp.abs(rank - n) < 0.5)
            one = jnp.sum(jnp.where(here, lane.astype(F32), 0.0), axis=1, keepdims=True)
            listed = jnp.where(wide == n, one, listed)
        picked[...] = listed.astype(jnp.int32)

    def passed(n, l):
        host = lax.rem(lift(served[n]) + 3 * l, NZ)
        r = lax.rem(z - host + NZ, NZ)
        dst, sem = (
            (kv.at[c, r, 1], kv_sem),
            (qg.at[c, r, 0], qg_sem),
            (qg.at[c, r, 1], qg_sem),
        )[n]
        there = (2 * host + l % 2, served[n])
        return host != z, remote(passing.at[n, l], dst, pass_send.at[n, l], sem, there)

    for l in range(3):
        for n in range(3):
            on, move = passed(n, l)

            @pl.when(on)
            def _():
                arrived(passing.at[n, l], pass_sem.at[n, l])
                move.start()

    @pl.when(is_host)
    def _():
        arrived(kv, kv_sem)
        arrived(qg, qg_sem)
        arrived(kv.at[0, pl.ds(0, 4)], in_send)

    @pl.when(jnp.logical_not(is_host))
    def _():
        arrived(kv.at[0, pl.ds(0, 6)], in_send)

    for l in range(3):
        for n in range(3):
            on, move = passed(n, l)
            pl.when(on)(move.wait_send)


def gradients(
    kv, qg, picked_in, dq_out, kv_out,
    picked, item_row, item_base, e_buf, d_buf, top_buf, row_top, row_sum, row_mix, dq_acc, acc, sem,
):
    blk, u, z, c, is_host, mine = place()

    @pl.when(is_host)
    def _():
        get = pltpu.make_async_copy(picked_in, picked, sem)
        get.start()
        acc[...] = jnp.zeros_like(acc)
        dq_acc[...] = jnp.zeros_like(dq_acc)
        row_top[...] = jnp.full_like(row_top, -1e30)
        row_sum[...] = jnp.zeros_like(row_sum)
        row_mix[...] = jnp.zeros_like(row_mix)
        get.wait()

        items = jnp.int32(0)
        for r in range(16):
            groups = lax.div(picked[r, COUNT] + SLOTS - 1, SLOTS)

            def add(b, n, r=r):
                item_row[n] = r
                item_base[n] = b * SLOTS
                return n + 1

            items = lax.fori_loop(0, groups, add, items)
        for m in range(WIDE - 1):
            item_row[items + m] = 0
            item_base[items + m] = 16
        rounds = lax.div(items + WIDE - 1, WIDE)

        def tiles(ref, r, base, part):
            return jnp.concatenate(
                [ref[picked[r, base + m], part] for m in range(SLOTS)], axis=0
            )

        def weigh(t, carry):
            for w in range(WIDE):
                i = t * WIDE + w
                r = item_row[i]
                base = item_base[i]
                scores = nt(tiles(kv, r, base, 0), qg[r, 0]) * (FACTOR * LOG2E)
                scores = jnp.concatenate(
                    [
                        scores[128 * m:128 * m + 128]
                        + jnp.where(base + m < picked[r, COUNT], 0.0, -1e30)
                        for m in range(SLOTS)
                    ],
                    axis=0,
                )
                top = jnp.max(scores, axis=0, keepdims=True)
                e = jnp.exp2(scores - top)
                dprob = nt(tiles(kv, r, base, 1), qg[r, 1])
                e_buf[i] = e
                d_buf[i] = dprob
                top_buf[i] = top
                total = jnp.sum(e, axis=0, keepdims=True)
                mixed = jnp.sum(e * dprob, axis=0, keepdims=True)
                old = row_top[r]
                new = jnp.maximum(old, top)
                keep = jnp.exp2(old - new)
                part = jnp.exp2(top - new)
                row_top[r] = new
                row_sum[r] = row_sum[r] * keep + total * part
                row_mix[r] = row_mix[r] * keep + mixed * part
            return carry

        lax.fori_loop(0, rounds, weigh, 0)

        def spread(t, carry):
            for w in range(WIDE):
                i = t * WIDE + w
                r = item_row[i]
                base = item_base[i]
                whole = 1.0 / row_sum[r]
                prob = e_buf[i] * (jnp.exp2(top_buf[i] - row_top[r]) * whole)
                dscore = (prob * (d_buf[i] - row_mix[r] * whole)).astype(BF16)
                dk = nn(dscore, qg[r, 0])
                dv = nn(prob.astype(BF16), qg[r, 1])
                dq_acc[r] += lax.dot_general(
                    dscore, tiles(kv, r, base, 0), (((0,), (0,)), ((), ())),
                    preferred_element_type=F32,
                )
                for m in range(SLOTS):
                    j = picked[r, base + m]
                    acc[j, 0] += dk[128 * m:128 * m + 128]
                    acc[j, 1] += dv[128 * m:128 * m + 128]
            return carry

        lax.fori_loop(0, rounds, spread, 0)
        dq_out[...] = (dq_acc[...] * FACTOR).astype(BF16)

        def stage(j, carry):
            dk = acc[j, 0] * FACTOR
            dv = acc[j, 1]
            for n in range(NU):
                piece = jnp.concatenate([dk[8 * n:8 * n + 8], dv[8 * n:8 * n + 8]], axis=0)
                kv_out[NU * lax.div(j, NZ) + n, lax.rem(j, NZ)] = piece.astype(BF16)
            return carry

        lax.fori_loop(0, 16, stage, 0)


def give_back(
    dq_in, kv_out, out_q, out_k, out_v, r_q, r_kv, t_q, f_q, f_kv,
    p1q_send, p1k_send, rq_sem, rkv_sem, p2q_send, p2k_send, fq_sem, fkv_sem,
):
    blk, u, z, c, is_host, mine = place()
    seat = mine * 2 + lax.rem(lax.div(u, 4), 2)
    barrier = pltpu.get_barrier_semaphore()

    def greet(there):
        pl.semaphore_signal(barrier, inc=1, device_id=there, device_id_type=MESH)

    def greet_line(r, carry):
        greet((2 * lax.rem(z + r, NZ) + c, u))
        return carry

    def greet_plane(n, carry):
        greet((blk, lax.rem(u + n, NU)))
        return carry

    for l in range(3):
        at_line = (2 * lax.rem(lift(u) + 3 * l, NZ) + l % 2, u)
        pl.when(at_line[0] != blk)(functools.partial(greet, at_line))
        up = lax.rem(z - 3 * l + 2 * NZ, NZ)
        for half in range(2):
            x = lax.div(lax.rem(up - lax.rem(up, 2) - 4 * half + NZ, NZ), 2)
            line = 4 * (2 * lax.rem(up, 2) + half) + x
            away = jnp.logical_or(line != u, c != l % 2)
            pl.when(away)(functools.partial(greet, (2 * z + l % 2, line)))
    lax.fori_loop(1, NZ, greet_line, 0)
    lax.fori_loop(1, NU, greet_plane, 0)
    pl.semaphore_wait(barrier, 7 + 15 + (15 + 31) * is_host.astype(jnp.int32))

    @pl.when(is_host)
    def _():
        def send_k(n):
            part = pl.ds(4 * n, 4)
            for side in range(2):

                def one(i, carry):
                    to = lax.rem(u + i, NU)
                    remote(
                        kv_out.at[NU * side + to, part], r_kv.at[seat, part],
                        p1k_send.at[n], rkv_sem.at[n], (2 * z + side, to),
                    ).start()
                    return carry

                lax.fori_loop(1, NU, one, 0)

                @pl.when(c != side)
                def _():
                    one(0, 0)

                @pl.when(c == side)
                def _():
                    pltpu.make_async_copy(
                        kv_out.at[NU * side + u, part], r_kv.at[seat, part], rkv_sem.at[n]
                    ).start()

        def send_q(n, carry):
            there = lax.rem(blk + n, 2 * NZ)
            r = lax.rem(lax.div(there, 2) - z + NZ, NZ)
            tile = NZ * lax.rem(there, 2) + r
            remote(dq_in.at[tile], r_q.at[mine], p1q_send, rq_sem, (there, u)).start()
            return carry

        send_k(0)
        lax.fori_loop(1, 2 * NZ, send_q, 0)
        pltpu.make_async_copy(dq_in.at[NZ * c], r_q.at[mine], rq_sem).start()
        send_k(1)

    arrived(r_q, rq_sem)
    heads = [r_q[l].astype(F32) for l in range(3)]
    for i in range(NU):
        rows = slice(8 * i, 8 * i + 8)
        t_q[i, :16] = jnp.concatenate([heads[0][rows], heads[1][rows]], axis=0).astype(BF16)
        t_q[i, 16:] = jnp.concatenate([heads[2][rows], heads[2][rows]], axis=0).astype(BF16)

    def pass_q(i, carry):
        to = lax.rem(u + i, NU)
        remote(t_q.at[to], f_q.at[u], p2q_send, fq_sem, (blk, to)).start()
        return carry

    lax.fori_loop(1, NU, pass_q, 0)
    pltpu.make_async_copy(t_q.at[u], f_q.at[u], fq_sem).start()

    def pass_k(r, carry):
        there = (2 * lax.rem(z + r, NZ) + c, u)
        remote(r_kv.at[:, r], f_kv.at[z], p2k_send, fkv_sem, there).start()
        return carry

    arrived(r_kv.at[:, pl.ds(0, 4)], rkv_sem.at[0])
    lax.fori_loop(1, 4, pass_k, 0)
    pltpu.make_async_copy(r_kv.at[:, 0], f_kv.at[z], fkv_sem).start()
    arrived(r_kv.at[:, pl.ds(4, 4)], rkv_sem.at[1])
    lax.fori_loop(4, NZ, pass_k, 0)

    @pl.when(is_host)
    def _():
        arrived(dq_in.at[pl.ds(0, 15)], p1q_send)
        for n in range(2):
            arrived(kv_out.at[pl.ds(0, 31), pl.ds(4 * n, 4)], p1k_send.at[n])

    arrived(t_q.at[pl.ds(0, NU - 1)], p2q_send)
    arrived(r_kv.at[:, pl.ds(0, NZ - 1)], p2k_send)
    def columns(head):
        return slice(head * DH, head * DH + DH)

    arrived(f_q, fq_sem)
    for n in range(NU):
        first = f_q[n, :16].astype(F32)
        out_q[:, columns(3 * n)] = first[:8].astype(BF16)
        out_q[:, columns(3 * n + 1)] = first[8:].astype(BF16)
        out_q[:, columns(3 * n + 2)] = f_q[n, 16:].astype(F32)[:8].astype(BF16)
    arrived(f_kv, fkv_sem)
    for d in range(NZ):
        for l in range(3):
            for half in range(2):
                both = f_kv[d, 2 * l + half].astype(F32)
                up = (d - 3 * l) % NZ
                x = (up - up % 2 - 4 * half) % NZ // 2
                head = 3 * (4 * (2 * (up % 2) + half) + x) + l
                out_k[:, columns(head)] = both[:8].astype(BF16)
                out_v[:, columns(head)] = both[8:].astype(BF16)


def local(query, key, value, grad_out, tile_mask, tile_order):
    anywhere = pl.BlockSpec(memory_space=pl.ANY)
    vmem = pl.BlockSpec(memory_space=pltpu.VMEM)
    smem = pl.BlockSpec(memory_space=pltpu.SMEM)
    dma = pltpu.SemaphoreType.DMA
    shape = jax.ShapeDtypeStruct
    most = 16 * 16 // SLOTS + WIDE
    operands = (query, key, value, grad_out, jnp.transpose(tile_mask, (1, 2, 0)), tile_order)
    kv, qg, picked = pl.pallas_call(
        collect,
        out_shape=(
            shape((2, NZ, 2, 128, 128), BF16),
            shape((2, NZ, 2, 128, 128), BF16),
            shape((16, 128), jnp.int32),
        ),
        in_specs=[anywhere] * 5 + [smem],
        out_specs=(vmem, vmem, vmem),
        scratch_shapes=[
            pltpu.VMEM((16, 16, H), jnp.int32),
            pltpu.VMEM((3, 3, 128, 128), BF16),
            dma, dma, dma, dma, dma((3, 3)), dma((3, 3)),
        ],
        compiler_params=pltpu.CompilerParams(
            collective_id=0, has_side_effects=True, vmem_limit_bytes=16 * 1024 * 1024
        ),
    )(*[pltpu.with_memory_space_constraint(a, pltpu.HBM) for a in operands])
    dq, kv_out = pl.pallas_call(
        gradients,
        out_shape=(
            shape((16, 128, 128), BF16),
            shape((2 * NU, NZ, 16, 128), BF16),
        ),
        in_specs=[vmem, vmem, anywhere],
        out_specs=(vmem, vmem),
        scratch_shapes=[
            pltpu.SMEM((16, 128), jnp.int32),
            pltpu.SMEM((most,), jnp.int32),
            pltpu.SMEM((most,), jnp.int32),
            pltpu.VMEM((most, 128 * SLOTS, 128), F32),
            pltpu.VMEM((most, 128 * SLOTS, 128), F32),
            pltpu.VMEM((most, 1, 128), F32),
            pltpu.VMEM((16, 1, 128), F32),
            pltpu.VMEM((16, 1, 128), F32),
            pltpu.VMEM((16, 1, 128), F32),
            pltpu.VMEM((16, 128, 128), F32),
            pltpu.VMEM((16, 2, 128, 128), F32),
            dma,
        ],
        compiler_params=pltpu.CompilerParams(vmem_limit_bytes=48 * 1024 * 1024),
    )(kv.reshape(16, 2, 128, 128), qg.reshape(16, 2, 128, 128), picked)
    out = shape((8, H * DH), BF16)
    return pl.pallas_call(
        give_back,
        out_shape=(out, out, out),
        in_specs=[vmem] * 2,
        out_specs=(vmem, vmem, vmem),
        scratch_shapes=[
            pltpu.VMEM((3, 128, 128), BF16),
            pltpu.VMEM((6, NZ, 16, 128), BF16),
            pltpu.VMEM((NU, 32, 128), BF16),
            pltpu.VMEM((NU, 32, 128), BF16),
            pltpu.VMEM((NZ, 6, 16, 128), BF16),
            dma, dma((2,)), dma, dma((2,)), dma, dma, dma, dma,
        ],
        compiler_params=pltpu.CompilerParams(
            collective_id=1, has_side_effects=True, vmem_limit_bytes=16 * 1024 * 1024
        ),
    )(dq, kv_out)


def solution(mesh):
    placed = (P("blk", "uly"), P("blk", "uly"), P("blk", "uly"), P("blk", "uly"), P(), P())
    return jax.shard_map(
        local,
        mesh=mesh,
        in_specs=placed,
        out_specs=(P(("blk", "uly"), None), P(("blk", "uly"), None), P(("blk", "uly"), None)),
        check_vma=False,
    )
```

```python
import functools

import jax
import jax.numpy as jnp
from jax import lax
from jax.experimental import pallas as pl
from jax.experimental.pallas import tpu as pltpu
from jax.sharding import PartitionSpec as P

H = 48
DH = 128
TILE = 128
NZ = 8
NU = 16
SLOTS = 2
WIDE = 6
COUNT = 32
MESH = pl.DeviceIdType.MESH
FACTOR = DH ** -0.5
LOG2E = 1.4426950408889634
F32 = jnp.float32
BF16 = jnp.bfloat16


def nt(a, b):
    return lax.dot_general(a, b, (((1,), (1,)), ((), ())), preferred_element_type=F32)


def nn(a, b):
    return lax.dot_general(a, b, (((1,), (0,)), ((), ())), preferred_element_type=F32)


def lift(u):
    x, y = lax.rem(u, 4), lax.div(u, 4)
    return lax.rem(2 * x + 4 * lax.rem(y, 2) + lax.div(y, 2), NZ)


def beside(u):
    x, y = lax.rem(u, 4), lax.div(u, 4)
    other = y + 1 - 2 * lax.rem(y, 2)
    return 4 * y + lax.rem(x + 1, 4), 4 * other + x, 4 * y + lax.rem(x + 3, 4)


def hosted(z, u):
    rel = lax.rem(z - lift(u) + NZ, NZ)
    yes = jnp.logical_or(rel == 0, jnp.logical_or(rel == 3, rel == 6))
    return yes, lax.div(rel, 3)


def remote(src, dst, send, recv, there):
    return pltpu.make_async_remote_copy(
        src_ref=src, dst_ref=dst, send_sem=send, recv_sem=recv,
        device_id=there, device_id_type=MESH,
    )


def arrived(ref, sem):
    pltpu.make_async_copy(ref, ref, sem).wait()


def place():
    blk = lax.axis_index("blk")
    u = lax.axis_index("uly")
    z = lax.div(blk, 2)
    c = lax.rem(blk, 2)
    yes, mine = hosted(z, u)
    return blk, u, z, c, jnp.logical_and(yes, c == lax.rem(mine, 2)), mine


def collect(
    q_in, k_in, v_in, g_in, mask_in, order_ref, kv, qg, picked,
    mask, passing, in_send, kv_sem, qg_sem, mask_sem, pass_sem, pass_send,
):
    blk, u, z, c, is_host, mine = place()
    via = beside(u)
    served = (via[2], via[1], via[0])
    barrier = pltpu.get_barrier_semaphore()

    def greet(there):
        pl.semaphore_signal(barrier, inc=1, device_id=there, device_id_type=MESH)

    get_mask = pltpu.make_async_copy(mask_in, mask, mask_sem)

    @pl.when(is_host)
    def _():
        get_mask.start()

        def greet_line(n, carry):
            greet((lax.rem(blk + n, 2 * NZ), u))
            return carry

        lax.fori_loop(1, 2 * NZ, greet_line, 0)

    for line in served:
        greet((blk, line))

    pl.semaphore_wait(barrier, 3 + 3 - is_host.astype(jnp.int32))

    def inputs(l):
        host = lax.rem(lift(u) + 3 * l, NZ)
        r = lax.rem(z - host + NZ, NZ)
        cols = pl.ds(pl.multiple_of(l * DH, DH), DH)
        there = (2 * host + lax.rem(l, 2), u)
        home = (
            (k_in, kv.at[c, r, 0], kv_sem),
            (v_in, kv.at[c, r, 1], kv_sem),
            (q_in, qg.at[c, r, 0], qg_sem),
            (g_in, qg.at[c, r, 1], qg_sem),
        )
        home = [(src.at[:, cols], dst, sem) for src, dst, sem in home]
        straight = [(src, dst, in_send, sem, there) for src, dst, sem in home]
        around = [
            (home[n + 1][0], passing.at[n, l], in_send, pass_sem.at[n, l], (blk, via[n]))
            for n in range(3)
        ] + straight[:1]
        return host, home, straight, around

    def nth(n, line):
        return lax.rem(z + line + n, 3)

    for n in range(3):
        l = nth(n, u)
        host, home, straight, around = inputs(l)

        @pl.when(host != z)
        def _():
            for move in around:
                remote(*move).start()

        @pl.when(jnp.logical_and(host == z, c != lax.rem(l, 2)))
        def _():
            for move in straight:
                remote(*move).start()

        @pl.when(jnp.logical_and(host == z, c == lax.rem(l, 2)))
        def _():
            for move in home:
                pltpu.make_async_copy(*move).start()

    @pl.when(is_host)
    def _():
        row = lax.broadcasted_iota(jnp.int32, (16, 16), 0)
        lane = lax.broadcasted_iota(jnp.int32, (16, 16), 1)
        ident = jnp.zeros((16, 16), jnp.int32)
        for j in range(16):
            ident = jnp.where(row == j, order_ref[2 * lax.rem(z + j % NZ, NZ) + j // NZ], ident)
        hot = jnp.where(lane == ident, 1.0, 0.0).astype(BF16)
        wide = lax.broadcasted_iota(jnp.int32, (16, 128), 1)
        hot_wide = jnp.where(wide == ident[:, :1], 1.0, 0.0).astype(BF16)
        get_mask.wait()
        flat = jnp.where(mask[...] > 0, 1.0, 0.0).reshape(256, H).astype(BF16)
        head = lax.broadcasted_iota(jnp.int32, (H, 128), 0) == 3 * u + mine
        picked_out = nn(flat, jnp.where(head, 1.0, 0.0).astype(BF16))
        tall = lax.broadcasted_iota(jnp.int32, (16, 16, 128), 1)
        across = lax.broadcasted_iota(jnp.int32, (16, 16, 128), 2)
        table = jnp.where(tall == across, picked_out.reshape(16, 16, 128), 0.0)
        table = jnp.sum(table, axis=1).astype(BF16)
        by_query = nn(hot, table).astype(BF16)
        allowed = nt(by_query, hot_wide)
        before = jnp.where(row < lane, 1.0, 0.0).astype(BF16)
        rank = nn(allowed.astype(BF16), before)
        listed = jnp.where(wide == COUNT, jnp.sum(allowed, axis=1, keepdims=True), 0.0)
        for n in range(16):
            here = jnp.logical_and(allowed > 0.5, jnp.abs(rank - n) < 0.5)
            one = jnp.sum(jnp.where(here, lane.astype(F32), 0.0), axis=1, keepdims=True)
            listed = jnp.where(wide == n, one, listed)
        picked[...] = listed.astype(jnp.int32)

    def passed(n, l):
        host = lax.rem(lift(served[n]) + 3 * l, NZ)
        r = lax.rem(z - host + NZ, NZ)
        dst, sem = (
            (kv.at[c, r, 1], kv_sem),
            (qg.at[c, r, 0], qg_sem),
            (qg.at[c, r, 1], qg_sem),
        )[n]
        there = (2 * host + lax.rem(l, 2), served[n])
        return host != z, remote(passing.at[n, l], dst, pass_send.at[n, l], sem, there)

    for i in range(3):
        for n in range(3):
            l = nth(i, served[n])
            on, move = passed(n, l)

            @pl.when(on)
            def _():
                arrived(passing.at[n, l], pass_sem.at[n, l])
                move.start()

    @pl.when(is_host)
    def _():
        arrived(kv, kv_sem)
        arrived(qg, qg_sem)
        arrived(kv.at[0, pl.ds(0, 4)], in_send)

    @pl.when(jnp.logical_not(is_host))
    def _():
        arrived(kv.at[0, pl.ds(0, 6)], in_send)

    for l in range(3):
        for n in range(3):
            on, move = passed(n, l)
            pl.when(on)(move.wait_send)


def gradients(
    kv, qg, picked_in, dq_out, acc,
    picked, item_row, item_base, e_buf, d_buf, top_buf, row_top, row_sum, row_mix, dq_acc, sem,
):
    blk, u, z, c, is_host, mine = place()

    @pl.when(is_host)
    def _():
        get = pltpu.make_async_copy(picked_in, picked, sem)
        get.start()
        acc[...] = jnp.zeros_like(acc)
        dq_acc[...] = jnp.zeros_like(dq_acc)
        row_top[...] = jnp.full_like(row_top, -1e30)
        row_sum[...] = jnp.zeros_like(row_sum)
        row_mix[...] = jnp.zeros_like(row_mix)
        get.wait()

        items = jnp.int32(0)
        for r in range(16):
            groups = lax.div(picked[r, COUNT] + SLOTS - 1, SLOTS)

            def add(b, n, r=r):
                item_row[n] = r
                item_base[n] = b * SLOTS
                return n + 1

            items = lax.fori_loop(0, groups, add, items)
        for m in range(WIDE - 1):
            item_row[items + m] = 0
            item_base[items + m] = 16
        rounds = lax.div(items + WIDE - 1, WIDE)

        def tiles(ref, r, base, part):
            return jnp.concatenate(
                [ref[picked[r, base + m], part] for m in range(SLOTS)], axis=0
            )

        def weigh(t, carry):
            for w in range(WIDE):
                i = t * WIDE + w
                r = item_row[i]
                base = item_base[i]
                scores = nt(tiles(kv, r, base, 0), qg[r, 0]) * (FACTOR * LOG2E)
                scores = jnp.concatenate(
                    [
                        scores[128 * m:128 * m + 128]
                        + jnp.where(base + m < picked[r, COUNT], 0.0, -1e30)
                        for m in range(SLOTS)
                    ],
                    axis=0,
                )
                top = jnp.max(scores, axis=0, keepdims=True)
                e = jnp.exp2(scores - top)
                dprob = nt(tiles(kv, r, base, 1), qg[r, 1])
                e_buf[i] = e
                d_buf[i] = dprob
                top_buf[i] = top
                total = jnp.sum(e, axis=0, keepdims=True)
                mixed = jnp.sum(e * dprob, axis=0, keepdims=True)
                old = row_top[r]
                new = jnp.maximum(old, top)
                keep = jnp.exp2(old - new)
                part = jnp.exp2(top - new)
                row_top[r] = new
                row_sum[r] = row_sum[r] * keep + total * part
                row_mix[r] = row_mix[r] * keep + mixed * part
            return carry

        lax.fori_loop(0, rounds, weigh, 0)

        def spread(t, carry):
            for w in range(WIDE):
                i = t * WIDE + w
                r = item_row[i]
                base = item_base[i]
                whole = 1.0 / row_sum[r]
                prob = e_buf[i] * (jnp.exp2(top_buf[i] - row_top[r]) * whole)
                dscore = (prob * (d_buf[i] - row_mix[r] * whole)).astype(BF16)
                dk = nn(dscore, qg[r, 0])
                dv = nn(prob.astype(BF16), qg[r, 1])
                dq_acc[r] += lax.dot_general(
                    dscore, tiles(kv, r, base, 0), (((0,), (0,)), ((), ())),
                    preferred_element_type=F32,
                )
                for m in range(SLOTS):
                    j = picked[r, base + m]
                    acc[j, 0] += dk[128 * m:128 * m + 128]
                    acc[j, 1] += dv[128 * m:128 * m + 128]
            return carry

        lax.fori_loop(0, rounds, spread, 0)
        dq_out[...] = (dq_acc[...] * FACTOR).astype(BF16)


def give_back(
    dq_in, acc, f_q, f_kv, kv_out, r_q, r_kv, t_q,
    p1q_send, p1k_send, rq_sem, rkv_sem, p2q_send, p2k_send, fq_sem, fkv_sem,
):
    blk, u, z, c, is_host, mine = place()
    seat = mine * 2 + lax.rem(lax.div(u, 4), 2)
    barrier = pltpu.get_barrier_semaphore()

    def greet(there):
        pl.semaphore_signal(barrier, inc=1, device_id=there, device_id_type=MESH)

    def greet_line(r, carry):
        greet((2 * lax.rem(z + r, NZ) + c, u))
        return carry

    def greet_plane(n, carry):
        greet((blk, lax.rem(u + n, NU)))
        return carry

    for l in range(3):
        at_line = (2 * lax.rem(lift(u) + 3 * l, NZ) + l % 2, u)
        pl.when(at_line[0] != blk)(functools.partial(greet, at_line))
        up = lax.rem(z - 3 * l + 2 * NZ, NZ)
        for half in range(2):
            x = lax.div(lax.rem(up - lax.rem(up, 2) - 4 * half + NZ, NZ), 2)
            line = 4 * (2 * lax.rem(up, 2) + half) + x
            away = jnp.logical_or(line != u, c != l % 2)
            pl.when(away)(functools.partial(greet, (2 * z + l % 2, line)))
    lax.fori_loop(1, NZ, greet_line, 0)
    lax.fori_loop(1, NU, greet_plane, 0)

    @pl.when(is_host)
    def _():
        def stage(j, carry):
            dk = acc[j, 0] * FACTOR
            dv = acc[j, 1]
            for n in range(NU):
                piece = jnp.concatenate([dk[8 * n:8 * n + 8], dv[8 * n:8 * n + 8]], axis=0)
                kv_out[NU * lax.div(j, NZ) + n, lax.rem(j, NZ)] = piece.astype(BF16)
            return carry

        lax.fori_loop(0, 16, stage, 0)

    pl.semaphore_wait(barrier, 7 + 15 + (15 + 31) * is_host.astype(jnp.int32))

    @pl.when(is_host)
    def _():
        for side in range(2):

            def send_k(i, carry, side=side):
                to = lax.rem(u + i, NU)
                remote(
                    kv_out.at[NU * side + to], r_kv.at[seat], p1k_send, rkv_sem, (2 * z + side, to)
                ).start()
                return carry

            lax.fori_loop(1, NU, send_k, 0)

            @pl.when(c != side)
            def _():
                send_k(0, 0)

            @pl.when(c == side)
            def _():
                pltpu.make_async_copy(kv_out.at[NU * side + u], r_kv.at[seat], rkv_sem).start()

        def send_q(n, carry):
            there = lax.rem(blk + n, 2 * NZ)
            r = lax.rem(lax.div(there, 2) - z + NZ, NZ)
            tile = NZ * lax.rem(there, 2) + r
            remote(dq_in.at[tile], r_q.at[mine], p1q_send, rq_sem, (there, u)).start()
            return carry

        lax.fori_loop(1, 2 * NZ, send_q, 0)
        pltpu.make_async_copy(dq_in.at[NZ * c], r_q.at[mine], rq_sem).start()

    arrived(r_q, rq_sem)
    heads = [r_q[l].astype(F32) for l in range(3)]
    for i in range(NU):
        rows = slice(8 * i, 8 * i + 8)
        t_q[i, :16] = jnp.concatenate([heads[0][rows], heads[1][rows]], axis=0).astype(BF16)
        t_q[i, 16:] = jnp.concatenate([heads[2][rows], heads[2][rows]], axis=0).astype(BF16)

    def pass_q(i, carry):
        to = lax.rem(u + i, NU)
        remote(t_q.at[to], f_q.at[u], p2q_send, fq_sem, (blk, to)).start()
        return carry

    lax.fori_loop(1, NU, pass_q, 0)
    pltpu.make_async_copy(t_q.at[u], f_q.at[u], fq_sem).start()

    def pass_k(r, carry):
        there = (2 * lax.rem(z + r, NZ) + c, u)
        remote(r_kv.at[:, r], f_kv.at[z], p2k_send, fkv_sem, there).start()
        return carry

    arrived(r_kv, rkv_sem)
    lax.fori_loop(1, NZ, pass_k, 0)
    pltpu.make_async_copy(r_kv.at[:, 0], f_kv.at[z], fkv_sem).start()

    @pl.when(is_host)
    def _():
        arrived(dq_in.at[pl.ds(0, 15)], p1q_send)
        arrived(kv_out.at[pl.ds(0, 31)], p1k_send)

    arrived(r_kv.at[:, pl.ds(0, NZ - 1)], p2k_send)
    arrived(t_q.at[pl.ds(0, NU - 1)], p2q_send)
    arrived(f_q, fq_sem)
    arrived(f_kv, fkv_sem)


def assemble(f_q, f_kv, q_hbm, k_hbm, v_hbm, out_q, out_k, out_v, sems):
    def columns(head):
        return slice(head * DH, head * DH + DH)

    copies = [
        pltpu.make_async_copy(src, dst, sems.at[n])
        for n, (src, dst) in enumerate(((out_q, q_hbm), (out_k, k_hbm), (out_v, v_hbm)))
    ]
    for n in range(NU):
        first = f_q[n, :16].astype(F32)
        out_q[:, columns(3 * n)] = first[:8].astype(BF16)
        out_q[:, columns(3 * n + 1)] = first[8:].astype(BF16)
        out_q[:, columns(3 * n + 2)] = f_q[n, 16:].astype(F32)[:8].astype(BF16)
    copies[0].start()
    for d in range(NZ):
        for l in range(3):
            for half in range(2):
                both = f_kv[d, 2 * l + half].astype(F32)
                up = (d - 3 * l) % NZ
                x = (up - up % 2 - 4 * half) % NZ // 2
                head = 3 * (4 * (2 * (up % 2) + half) + x) + l
                out_k[:, columns(head)] = both[:8].astype(BF16)
                out_v[:, columns(head)] = both[8:].astype(BF16)
    copies[1].start()
    copies[2].start()
    for copy in copies:
        copy.wait()


def local(query, key, value, grad_out, tile_mask, tile_order):
    anywhere = pl.BlockSpec(memory_space=pl.ANY)
    vmem = pl.BlockSpec(memory_space=pltpu.VMEM)
    smem = pl.BlockSpec(memory_space=pltpu.SMEM)
    dma = pltpu.SemaphoreType.DMA
    shape = jax.ShapeDtypeStruct
    most = 16 * 16 // SLOTS + WIDE
    operands = (query, key, value, grad_out, jnp.transpose(tile_mask, (1, 2, 0)), tile_order)
    kv, qg, picked = pl.pallas_call(
        collect,
        out_shape=(
            shape((2, NZ, 2, 128, 128), BF16),
            shape((2, NZ, 2, 128, 128), BF16),
            shape((16, 128), jnp.int32),
        ),
        in_specs=[anywhere] * 5 + [smem],
        out_specs=(vmem, vmem, vmem),
        scratch_shapes=[
            pltpu.VMEM((16, 16, H), jnp.int32),
            pltpu.VMEM((3, 3, 128, 128), BF16),
            dma, dma, dma, dma, dma((3, 3)), dma((3, 3)),
        ],
        compiler_params=pltpu.CompilerParams(
            collective_id=0, has_side_effects=True, vmem_limit_bytes=16 * 1024 * 1024
        ),
    )(*[pltpu.with_memory_space_constraint(a, pltpu.HBM) for a in operands])
    dq, acc = pl.pallas_call(
        gradients,
        out_shape=(
            shape((16, 128, 128), BF16),
            shape((16, 2, 128, 128), F32),
        ),
        in_specs=[vmem, vmem, anywhere],
        out_specs=(vmem, vmem),
        scratch_shapes=[
            pltpu.SMEM((16, 128), jnp.int32),
            pltpu.SMEM((most,), jnp.int32),
            pltpu.SMEM((most,), jnp.int32),
            pltpu.VMEM((most, 128 * SLOTS, 128), F32),
            pltpu.VMEM((most, 128 * SLOTS, 128), F32),
            pltpu.VMEM((most, 1, 128), F32),
            pltpu.VMEM((16, 1, 128), F32),
            pltpu.VMEM((16, 1, 128), F32),
            pltpu.VMEM((16, 1, 128), F32),
            pltpu.VMEM((16, 128, 128), F32),
            dma,
        ],
        compiler_params=pltpu.CompilerParams(vmem_limit_bytes=48 * 1024 * 1024),
    )(kv.reshape(16, 2, 128, 128), qg.reshape(16, 2, 128, 128), picked)
    f_q, f_kv = pl.pallas_call(
        give_back,
        out_shape=(shape((NU, 32, 128), BF16), shape((NZ, 6, 16, 128), BF16)),
        in_specs=[vmem] * 2,
        out_specs=(vmem, vmem),
        scratch_shapes=[
            pltpu.VMEM((2 * NU, NZ, 16, 128), BF16),
            pltpu.VMEM((3, 128, 128), BF16),
            pltpu.VMEM((6, NZ, 16, 128), BF16),
            pltpu.VMEM((NU, 32, 128), BF16),
            dma, dma, dma, dma, dma, dma, dma, dma,
        ],
        compiler_params=pltpu.CompilerParams(
            collective_id=1, has_side_effects=True, vmem_limit_bytes=16 * 1024 * 1024
        ),
    )(dq, acc)
    out = shape((8, H * DH), BF16)
    return pl.pallas_call(
        assemble,
        out_shape=(out, out, out),
        in_specs=[vmem] * 2,
        out_specs=(anywhere, anywhere, anywhere),
        scratch_shapes=[pltpu.VMEM((8, H * DH), BF16)] * 3 + [dma((3,))],
        compiler_params=pltpu.CompilerParams(vmem_limit_bytes=8 * 1024 * 1024),
    )(*[pltpu.with_memory_space_constraint(a, pltpu.VMEM) for a in (f_q, f_kv)])


def solution(mesh):
    placed = (P("blk", "uly"), P("blk", "uly"), P("blk", "uly"), P("blk", "uly"), P(), P())
    return jax.shard_map(
        local,
        mesh=mesh,
        in_specs=placed,
        out_specs=(P(("blk", "uly"), None), P(("blk", "uly"), None), P(("blk", "uly"), None)),
        check_vma=False,
    )
```

```python
import functools

import jax
import jax.numpy as jnp
from jax import lax
from jax.experimental import pallas as pl
from jax.experimental.pallas import tpu as pltpu
from jax.sharding import PartitionSpec as P

H = 48
DH = 128
TILE = 128
NZ = 8
NU = 16
SLOTS = 2
WIDE = 6
SECOND = 16
COUNT = 32
EMPTY = 40
MESH = pl.DeviceIdType.MESH
FACTOR = DH ** -0.5
LOG2E = 1.4426950408889634
F32 = jnp.float32
BF16 = jnp.bfloat16


def nt(a, b):
    return lax.dot_general(a, b, (((1,), (1,)), ((), ())), preferred_element_type=F32)


def nn(a, b):
    return lax.dot_general(a, b, (((1,), (0,)), ((), ())), preferred_element_type=F32)


def lift(u):
    x, y = lax.rem(u, 4), lax.div(u, 4)
    return lax.rem(2 * x + 4 * lax.rem(y, 2) + lax.div(y, 2), NZ)


def beside(u):
    x, y = lax.rem(u, 4), lax.div(u, 4)
    other = y + 1 - 2 * lax.rem(y, 2)
    return 4 * y + lax.rem(x + 1, 4), 4 * other + x, 4 * y + lax.rem(x + 3, 4)


def hosted(z, u):
    rel = lax.rem(z - lift(u) + NZ, NZ)
    yes = jnp.logical_or(rel == 0, jnp.logical_or(rel == 3, rel == 6))
    return yes, lax.div(rel, 3)


def remote(src, dst, send, recv, there):
    return pltpu.make_async_remote_copy(
        src_ref=src, dst_ref=dst, send_sem=send, recv_sem=recv,
        device_id=there, device_id_type=MESH,
    )


def arrived(ref, sem):
    pltpu.make_async_copy(ref, ref, sem).wait()


def place():
    blk = lax.axis_index("blk")
    u = lax.axis_index("uly")
    z = lax.div(blk, 2)
    c = lax.rem(blk, 2)
    is_host, mine = hosted(z, u)
    return blk, u, z, c, is_host, mine


def collect(
    q_in, k_in, v_in, g_in, mask_in, order_ref, kv, qg, picked,
    mask, passing, in_send, kv_sem, qg_sem, kv_send, kv_recv, qg_send, qg_recv,
    mask_sem, pass_sem, pass_send,
):
    blk, u, z, c, is_host, mine = place()
    sibling = (2 * z + 1 - c, u)
    via = beside(u)
    served = (via[2], via[1], via[0])
    barrier = pltpu.get_barrier_semaphore()
    get_mask = pltpu.make_async_copy(mask_in, mask, mask_sem)

    def greet(there):
        pl.semaphore_signal(barrier, inc=1, device_id=there, device_id_type=MESH)

    @pl.when(is_host)
    def _():
        get_mask.start()

        def greet_line(r, carry):
            greet((2 * lax.rem(z + r, NZ) + c, u))
            return carry

        lax.fori_loop(1, NZ, greet_line, 0)
        greet(sibling)

    for line in served:
        greet((blk, line))

    pl.semaphore_wait(barrier, 6)

    def inputs(l):
        host = lax.rem(lift(u) + 3 * l, NZ)
        r = lax.rem(z - host + NZ, NZ)
        cols = pl.ds(pl.multiple_of(l * DH, DH), DH)
        home = [
            (src.at[:, cols], dst, sem)
            for src, dst, sem in (
                (k_in, kv.at[1, r, 0], kv_sem.at[r]),
                (v_in, kv.at[1, r, 1], kv_sem.at[r]),
                (q_in, qg.at[1, r, 0], qg_sem.at[r]),
                (g_in, qg.at[1, r, 1], qg_sem.at[r]),
            )
        ]
        away = [(*home[0][:2], in_send, home[0][2], (2 * host + c, u))] + [
            (home[n + 1][0], passing.at[n, l], in_send, pass_sem.at[n, l], (blk, via[n]))
            for n in range(3)
        ]
        return host, home, away

    def nth(n, line):
        return lax.rem(z + line + n, 3)

    for part in (slice(0, 2), slice(2, 4)):
        for n in range(3):
            host, home, away = inputs(nth(n, u))

            @pl.when(host != z)
            def _():
                for move in away[part]:
                    remote(*move).start()

            @pl.when(host == z)
            def _():
                for move in home[part]:
                    pltpu.make_async_copy(*move).start()

    @pl.when(is_host)
    def _():
        row = lax.broadcasted_iota(jnp.int32, (16, 16), 0)
        lane = lax.broadcasted_iota(jnp.int32, (16, 16), 1)
        ident = jnp.zeros((16, 16), jnp.int32)
        for j in range(16):
            side = c if j // NZ else 1 - c
            ident = jnp.where(row == j, order_ref[2 * lax.rem(z + j % NZ, NZ) + side], ident)
        hot = jnp.where(lane == ident, 1.0, 0.0).astype(BF16)
        wide = lax.broadcasted_iota(jnp.int32, (16, 128), 1)
        hot_wide = jnp.where(wide == ident[:, :1], 1.0, 0.0).astype(BF16)
        get_mask.wait()
        flat = jnp.where(mask[...] > 0, 1.0, 0.0).reshape(256, H).astype(BF16)
        head = lax.broadcasted_iota(jnp.int32, (H, 128), 0) == 3 * u + mine
        picked_out = nn(flat, jnp.where(head, 1.0, 0.0).astype(BF16))
        tall = lax.broadcasted_iota(jnp.int32, (16, 16, 128), 1)
        across = lax.broadcasted_iota(jnp.int32, (16, 16, 128), 2)
        table = jnp.where(tall == across, picked_out.reshape(16, 16, 128), 0.0)
        table = jnp.sum(table, axis=1).astype(BF16)
        by_query = nn(hot, table).astype(BF16)
        allowed = nt(by_query, hot_wide)
        one_side = lax.div(row, NZ) == lax.div(lane, NZ)
        before = jnp.where(jnp.logical_and(row < lane, one_side), 1.0, 0.0).astype(BF16)
        rank = nn(allowed.astype(BF16), before)
        near = jnp.where(lane >= NZ, allowed, 0.0)
        far = jnp.where(lane >= NZ, 0.0, allowed)
        listed = jnp.where(wide == COUNT, jnp.sum(near, axis=1, keepdims=True), 0.0)
        ends = SECOND + jnp.sum(far, axis=1, keepdims=True)
        listed = jnp.where(wide == COUNT + 1, ends, listed)
        for first, some in ((0, near), (SECOND, far)):
            for n in range(NZ):
                here = jnp.logical_and(some > 0.5, jnp.abs(rank - n) < 0.5)
                one = jnp.sum(jnp.where(here, lane.astype(F32), 0.0), axis=1, keepdims=True)
                listed = jnp.where(wide == first + n, one, listed)
        picked[...] = listed.astype(jnp.int32)

    def passed(n, l):
        host = lax.rem(lift(served[n]) + 3 * l, NZ)
        r = lax.rem(z - host + NZ, NZ)
        dst, sem = (
            (kv.at[1, r, 1], kv_sem.at[r]),
            (qg.at[1, r, 0], qg_sem.at[r]),
            (qg.at[1, r, 1], qg_sem.at[r]),
        )[n]
        there = (2 * host + c, served[n])
        return host != z, remote(passing.at[n, l], dst, pass_send.at[n, l], sem, there)

    for part in ((0,), (1, 2)):
        for i in range(3):
            for n in part:
                l = nth(i, served[n])
                on, move = passed(n, l)

                @pl.when(on)
                def _():
                    arrived(passing.at[n, l], pass_sem.at[n, l])
                    move.start()

    @pl.when(is_host)
    def _():
        for ref, sems, send, recv in (
            (kv, kv_sem, kv_send, kv_recv), (qg, qg_sem, qg_send, qg_recv)
        ):

            def share(n, carry, ref=ref, sems=sems, send=send, recv=recv):
                odd = lax.rem(n, 2)
                r = lax.rem(odd * lax.div(n + 1, 2) + (1 - odd) * (NZ - lax.div(n, 2)), NZ)
                arrived(ref.at[1, r], sems.at[r])
                remote(ref.at[1, r], ref.at[0, r], send, recv, sibling).start()
                return carry

            lax.fori_loop(0, NZ, share, 0)
        for ref, send, recv in ((kv, kv_send, kv_recv), (qg, qg_send, qg_recv)):
            arrived(ref.at[0], recv)
            arrived(ref.at[1], send)
        arrived(kv.at[0, pl.ds(0, 4)], in_send)

    @pl.when(jnp.logical_not(is_host))
    def _():
        arrived(kv.at[0, pl.ds(0, 6)], in_send)

    for l in range(3):
        for n in range(3):
            on, move = passed(n, l)
            pl.when(on)(move.wait_send)


def gradients(
    kv, qg, picked_in, dq_out, acc,
    picked, item_row, item_base, item_end, e_buf, d_buf, top_buf, row_top, row_sum, row_mix, dq_acc, sem,
):
    blk, u, z, c, is_host, mine = place()

    @pl.when(is_host)
    def _():
        get = pltpu.make_async_copy(picked_in, picked, sem)
        get.start()
        acc[NZ:] = jnp.zeros((NZ, 2, 128, 128), F32)
        dq_acc[NZ:] = jnp.zeros((NZ, 128, 128), F32)
        row_top[...] = jnp.full_like(row_top, -1e30)
        row_sum[...] = jnp.zeros_like(row_sum)
        row_mix[...] = jnp.zeros_like(row_mix)
        get.wait()

        def listing(rows, first, end, items):
            for r in rows:
                stop = picked[r, end]

                def add(b, n, r=r, stop=stop):
                    item_row[n] = r
                    item_base[n] = first + b * SLOTS
                    item_end[n] = stop
                    return n + 1

                items = lax.fori_loop(0, lax.div(stop - first + SLOTS - 1, SLOTS), add, items)
            return items

        own, other = range(NZ, 16), range(NZ)
        items = listing(own, 0, COUNT, jnp.int32(0))
        items = listing(other, 0, COUNT, items)
        needed = listing(own, SECOND, COUNT + 1, items)
        items = listing(other, SECOND, COUNT + 1, needed)
        for m in range(WIDE - 1):
            item_row[items + m] = 0
            item_base[items + m] = EMPTY
            item_end[items + m] = 0

        def tiles(ref, r, base, part):
            return jnp.concatenate(
                [ref[picked[r, base + m], part] for m in range(SLOTS)], axis=0
            )

        def weigh(t, carry):
            for w in range(WIDE):
                i = t * WIDE + w
                r = item_row[i]
                base = item_base[i]
                scores = nt(tiles(kv, r, base, 0), qg[r, 0]) * (FACTOR * LOG2E)
                scores = jnp.concatenate(
                    [
                        scores[128 * m:128 * m + 128]
                        + jnp.where(base + m < item_end[i], 0.0, -1e30)
                        for m in range(SLOTS)
                    ],
                    axis=0,
                )
                top = jnp.max(scores, axis=0, keepdims=True)
                e = jnp.exp2(scores - top)
                dprob = nt(tiles(kv, r, base, 1), qg[r, 1])
                e_buf[i] = e
                d_buf[i] = dprob
                top_buf[i] = top
                total = jnp.sum(e, axis=0, keepdims=True)
                mixed = jnp.sum(e * dprob, axis=0, keepdims=True)
                old = row_top[r]
                new = jnp.maximum(old, top)
                keep = jnp.exp2(old - new)
                part = jnp.exp2(top - new)
                row_top[r] = new
                row_sum[r] = row_sum[r] * keep + total * part
                row_mix[r] = row_mix[r] * keep + mixed * part
            return carry

        lax.fori_loop(0, lax.div(items + WIDE - 1, WIDE), weigh, 0)

        def spread(t, carry):
            for w in range(WIDE):
                i = t * WIDE + w
                r = item_row[i]
                base = item_base[i]
                whole = 1.0 / row_sum[r]
                prob = e_buf[i] * (jnp.exp2(top_buf[i] - row_top[r]) * whole)
                dscore = (prob * (d_buf[i] - row_mix[r] * whole)).astype(BF16)
                dk = nn(dscore, qg[r, 0])
                dv = nn(prob.astype(BF16), qg[r, 1])
                dq_acc[r] += lax.dot_general(
                    dscore, tiles(kv, r, base, 0), (((0,), (0,)), ((), ())),
                    preferred_element_type=F32,
                )
                for m in range(SLOTS):
                    j = picked[r, base + m]
                    acc[j, 0] += dk[128 * m:128 * m + 128]
                    acc[j, 1] += dv[128 * m:128 * m + 128]
            return carry

        lax.fori_loop(0, lax.div(needed + WIDE - 1, WIDE), spread, 0)
        dq_out[...] = (dq_acc[NZ:] * FACTOR).astype(BF16)


def give_back(
    dq_in, acc, f_q, f_kv, kv_out, r_q, r_kv, t_q,
    p1q_send, p1k_send, rq_sem, rkv_sem, p2q_send, p2k_send, fq_sem, fkv_sem, others,
):
    blk, u, z, c, is_host, mine = place()
    seat = mine * 2 + lax.rem(lax.div(u, 4), 2)
    rest = jnp.logical_not(is_host)
    barrier = pltpu.get_barrier_semaphore()

    def greet(there, other):
        @pl.when(jnp.logical_or(rest, jnp.logical_not(other)))
        def _():
            pl.semaphore_signal(barrier, inc=1, device_id=there, device_id_type=MESH)

    def greet_line(r, carry):
        h = lax.rem(z + r, NZ)
        greet((2 * h + c, u), hosted(h, u)[0])
        return carry

    def greet_plane(n, carry):
        to = lax.rem(u + n, NU)
        greet((blk, to), hosted(z, to)[0])
        return carry

    lax.fori_loop(1, NZ, greet_line, 0)
    lax.fori_loop(1, NU, greet_plane, 0)

    @pl.when(is_host)
    def _():
        def stage(r, carry):
            dk = acc[NZ + r, 0] * FACTOR
            dv = acc[NZ + r, 1]
            for n in range(NU):
                piece = jnp.concatenate([dk[8 * n:8 * n + 8], dv[8 * n:8 * n + 8]], axis=0)
                kv_out[n, lax.rem(z + r, NZ)] = piece.astype(BF16)
            return carry

        lax.fori_loop(0, NZ, stage, 0)

    pl.semaphore_wait(barrier, 22 - 7 * is_host.astype(jnp.int32))

    def tell(there):
        pl.semaphore_signal(others, inc=1, device_id=there, device_id_type=MESH)

    @pl.when(rest)
    def _():
        below = lax.rem(z + NZ - 1, NZ)
        right, _, left = beside(u)
        left_hosts, left_head = hosted(z, left)
        right_hosts, right_head = hosted(z, right)
        pl.when(hosted(below, u)[0])(functools.partial(tell, (2 * below + c, u)))
        on = jnp.logical_and(left_hosts, left_head > 0)
        pl.when(on)(functools.partial(tell, (blk, left)))
        on = jnp.logical_and(right_hosts, right_head == 0)
        pl.when(on)(functools.partial(tell, (blk, right)))

    @pl.when(is_host)
    def _():
        def send_k(part, to_hosts):
            heights = pl.ds(4 * part, 4)

            def one(n, carry):
                to = lax.rem(u + n, NU)

                @pl.when(hosted(z, to)[0] == to_hosts)
                def _():
                    remote(
                        kv_out.at[to, heights], r_kv.at[seat, heights],
                        p1k_send, rkv_sem.at[part], (blk, to),
                    ).start()

                return carry

            lax.fori_loop(1, NU, one, 0)

        def send_q(to_hosts):
            def one(h, carry):
                on = jnp.logical_and(h != z, hosted(h, u)[0] == to_hosts)

                @pl.when(on)
                def _():
                    tile = dq_in.at[lax.rem(h - z + NZ, NZ)]
                    remote(tile, r_q.at[mine], p1q_send, rq_sem, (2 * h + c, u)).start()

                return carry

            lax.fori_loop(0, NZ, one, 0)

        send_k(0, False)
        send_q(False)
        send_k(1, False)
        pltpu.make_async_copy(dq_in.at[0], r_q.at[mine], rq_sem).start()
        for part in range(2):
            heights = pl.ds(4 * part, 4)
            pltpu.make_async_copy(
                kv_out.at[u, heights], r_kv.at[seat, heights], rkv_sem.at[part]
            ).start()
        pl.semaphore_wait(others, 2)
        send_k(0, True)
        send_q(True)
        send_k(1, True)

    arrived(r_q, rq_sem)
    heads = [r_q[l].astype(F32) for l in range(3)]
    for i in range(NU):
        rows = slice(8 * i, 8 * i + 8)
        t_q[i, :16] = jnp.concatenate([heads[0][rows], heads[1][rows]], axis=0).astype(BF16)
        t_q[i, 16:] = jnp.concatenate([heads[2][rows], heads[2][rows]], axis=0).astype(BF16)

    def pass_q(i, carry):
        to = lax.rem(u + i, NU)
        remote(t_q.at[to], f_q.at[u], p2q_send, fq_sem, (blk, to)).start()
        return carry

    lax.fori_loop(1, NU, pass_q, 0)
    pltpu.make_async_copy(t_q.at[u], f_q.at[u], fq_sem).start()

    def pass_k(h, carry):
        @pl.when(h != z)
        def _():
            remote(r_kv.at[:, h], f_kv.at[z], p2k_send, fkv_sem, (2 * h + c, u)).start()

        @pl.when(h == z)
        def _():
            pltpu.make_async_copy(r_kv.at[:, h], f_kv.at[z], fkv_sem).start()

        return carry

    for part in range(2):
        arrived(r_kv.at[:, pl.ds(4 * part, 4)], rkv_sem.at[part])
        lax.fori_loop(4 * part, 4 * part + 4, pass_k, 0)

    @pl.when(is_host)
    def _():
        arrived(dq_in.at[pl.ds(0, NZ - 1)], p1q_send)
        arrived(kv_out.at[pl.ds(0, NU - 1)], p1k_send)

    arrived(r_kv.at[:, pl.ds(0, NZ - 1)], p2k_send)
    arrived(t_q.at[pl.ds(0, NU - 1)], p2q_send)
    arrived(f_q, fq_sem)
    arrived(f_kv, fkv_sem)


def assemble(f_q, f_kv, q_hbm, k_hbm, v_hbm, out_q, out_k, out_v, sems):
    def columns(head):
        return slice(head * DH, head * DH + DH)

    copies = [
        pltpu.make_async_copy(src, dst, sems.at[n])
        for n, (src, dst) in enumerate(((out_q, q_hbm), (out_k, k_hbm), (out_v, v_hbm)))
    ]
    for n in range(NU):
        first = f_q[n, :16].astype(F32)
        out_q[:, columns(3 * n)] = first[:8].astype(BF16)
        out_q[:, columns(3 * n + 1)] = first[8:].astype(BF16)
        out_q[:, columns(3 * n + 2)] = f_q[n, 16:].astype(F32)[:8].astype(BF16)
    copies[0].start()
    for d in range(NZ):
        for l in range(3):
            for half in range(2):
                both = f_kv[d, 2 * l + half].astype(F32)
                up = (d - 3 * l) % NZ
                x = (up - up % 2 - 4 * half) % NZ // 2
                head = 3 * (4 * (2 * (up % 2) + half) + x) + l
                out_k[:, columns(head)] = both[:8].astype(BF16)
                out_v[:, columns(head)] = both[8:].astype(BF16)
    copies[1].start()
    copies[2].start()
    for copy in copies:
        copy.wait()


def local(query, key, value, grad_out, tile_mask, tile_order):
    anywhere = pl.BlockSpec(memory_space=pl.ANY)
    vmem = pl.BlockSpec(memory_space=pltpu.VMEM)
    smem = pl.BlockSpec(memory_space=pltpu.SMEM)
    dma = pltpu.SemaphoreType.DMA
    shape = jax.ShapeDtypeStruct
    most = 16 * 16 // SLOTS + WIDE
    operands = (query, key, value, grad_out, jnp.transpose(tile_mask, (1, 2, 0)), tile_order)
    kv, qg, picked = pl.pallas_call(
        collect,
        out_shape=(
            shape((2, NZ, 2, 128, 128), BF16),
            shape((2, NZ, 2, 128, 128), BF16),
            shape((16, 128), jnp.int32),
        ),
        in_specs=[anywhere] * 5 + [smem],
        out_specs=(vmem, vmem, vmem),
        scratch_shapes=[
            pltpu.VMEM((16, 16, H), jnp.int32),
            pltpu.VMEM((3, 3, 128, 128), BF16),
            dma, dma((NZ,)), dma((NZ,)), dma, dma, dma, dma, dma, dma((3, 3)), dma((3, 3)),
        ],
        compiler_params=pltpu.CompilerParams(
            collective_id=0, has_side_effects=True, vmem_limit_bytes=16 * 1024 * 1024
        ),
    )(*[pltpu.with_memory_space_constraint(a, pltpu.HBM) for a in operands])
    dq, acc = pl.pallas_call(
        gradients,
        out_shape=(
            shape((NZ, 128, 128), BF16),
            shape((16, 2, 128, 128), F32),
        ),
        in_specs=[vmem, vmem, anywhere],
        out_specs=(vmem, vmem),
        scratch_shapes=[
            pltpu.SMEM((16, 128), jnp.int32),
            pltpu.SMEM((most,), jnp.int32),
            pltpu.SMEM((most,), jnp.int32),
            pltpu.SMEM((most,), jnp.int32),
            pltpu.VMEM((most, 128 * SLOTS, 128), F32),
            pltpu.VMEM((most, 128 * SLOTS, 128), F32),
            pltpu.VMEM((most, 1, 128), F32),
            pltpu.VMEM((16, 1, 128), F32),
            pltpu.VMEM((16, 1, 128), F32),
            pltpu.VMEM((16, 1, 128), F32),
            pltpu.VMEM((16, 128, 128), F32),
            dma,
        ],
        compiler_params=pltpu.CompilerParams(vmem_limit_bytes=48 * 1024 * 1024),
    )(kv.reshape(16, 2, 128, 128), qg.reshape(16, 2, 128, 128), picked)
    f_q, f_kv = pl.pallas_call(
        give_back,
        out_shape=(shape((NU, 32, 128), BF16), shape((NZ, 6, 16, 128), BF16)),
        in_specs=[vmem] * 2,
        out_specs=(vmem, vmem),
        scratch_shapes=[
            pltpu.VMEM((NU, NZ, 16, 128), BF16),
            pltpu.VMEM((3, 128, 128), BF16),
            pltpu.VMEM((6, NZ, 16, 128), BF16),
            pltpu.VMEM((NU, 32, 128), BF16),
            dma, dma, dma, dma((2,)), dma, dma, dma, dma,
            pltpu.SemaphoreType.REGULAR,
        ],
        compiler_params=pltpu.CompilerParams(
            collective_id=1, has_side_effects=True, vmem_limit_bytes=16 * 1024 * 1024
        ),
    )(dq, acc)
    out = shape((8, H * DH), BF16)
    return pl.pallas_call(
        assemble,
        out_shape=(out, out, out),
        in_specs=[vmem] * 2,
        out_specs=(anywhere, anywhere, anywhere),
        scratch_shapes=[pltpu.VMEM((8, H * DH), BF16)] * 3 + [dma((3,))],
        compiler_params=pltpu.CompilerParams(vmem_limit_bytes=8 * 1024 * 1024),
    )(*[pltpu.with_memory_space_constraint(a, pltpu.VMEM) for a in (f_q, f_kv)])


def solution(mesh):
    placed = (P("blk", "uly"), P("blk", "uly"), P("blk", "uly"), P("blk", "uly"), P(), P())
    return jax.shard_map(
        local,
        mesh=mesh,
        in_specs=placed,
        out_specs=(P(("blk", "uly"), None), P(("blk", "uly"), None), P(("blk", "uly"), None)),
        check_vma=False,
    )
```

```python
import functools

import jax
import jax.numpy as jnp
from jax import lax
from jax.experimental import pallas as pl
from jax.experimental.pallas import tpu as pltpu
from jax.sharding import PartitionSpec as P

H = 48
DH = 128
TILE = 128
NZ = 8
NU = 16
SLOTS = 2
WIDE = 6
SECOND = 16
COUNT = 32
EMPTY = 40
MESH = pl.DeviceIdType.MESH
FACTOR = DH ** -0.5
LOG2E = 1.4426950408889634
F32 = jnp.float32
BF16 = jnp.bfloat16


def nt(a, b):
    return lax.dot_general(a, b, (((1,), (1,)), ((), ())), preferred_element_type=F32)


def nn(a, b):
    return lax.dot_general(a, b, (((1,), (0,)), ((), ())), preferred_element_type=F32)


def lift(u):
    x, y = lax.rem(u, 4), lax.div(u, 4)
    return lax.rem(2 * x + 4 * lax.rem(y, 2) + lax.div(y, 2), NZ)


def beside(u):
    x, y = lax.rem(u, 4), lax.div(u, 4)
    other = y + 1 - 2 * lax.rem(y, 2)
    return 4 * y + lax.rem(x + 1, 4), 4 * other + x, 4 * y + lax.rem(x + 3, 4)


def hosted(z, u):
    rel = lax.rem(z - lift(u) + NZ, NZ)
    yes = jnp.logical_or(rel == 0, jnp.logical_or(rel == 3, rel == 6))
    return yes, lax.div(rel, 3)


def remote(src, dst, send, recv, there):
    return pltpu.make_async_remote_copy(
        src_ref=src, dst_ref=dst, send_sem=send, recv_sem=recv,
        device_id=there, device_id_type=MESH,
    )


def arrived(ref, sem):
    pltpu.make_async_copy(ref, ref, sem).wait()


def place():
    blk = lax.axis_index("blk")
    u = lax.axis_index("uly")
    z = lax.div(blk, 2)
    c = lax.rem(blk, 2)
    is_host, mine = hosted(z, u)
    return blk, u, z, c, is_host, mine


def collect(
    q_in, k_in, v_in, g_in, mask_in, order_ref, kv, qg, picked,
    mask, passing, in_send, kv_sem, qg_sem, kv_send, kv_recv, qg_send, qg_recv,
    mask_sem, pass_sem, pass_send,
):
    blk, u, z, c, is_host, mine = place()
    sibling = (2 * z + 1 - c, u)
    via = beside(u)
    served = (via[2], via[1], via[0])
    barrier = pltpu.get_barrier_semaphore()
    get_mask = pltpu.make_async_copy(mask_in, mask, mask_sem)

    def greet(there):
        pl.semaphore_signal(barrier, inc=1, device_id=there, device_id_type=MESH)

    @pl.when(is_host)
    def _():
        get_mask.start()

        def greet_line(r, carry):
            greet((2 * lax.rem(z + r, NZ) + c, u))
            return carry

        lax.fori_loop(1, NZ, greet_line, 0)
        greet(sibling)

    for line in served:
        greet((blk, line))

    pl.semaphore_wait(barrier, 6)

    def inputs(l):
        host = lax.rem(lift(u) + 3 * l, NZ)
        r = lax.rem(z - host + NZ, NZ)
        cols = pl.ds(pl.multiple_of(l * DH, DH), DH)
        home = [
            (src.at[:, cols], dst, sem)
            for src, dst, sem in (
                (k_in, kv.at[1, r, 0], kv_sem.at[r]),
                (v_in, kv.at[1, r, 1], kv_sem.at[r]),
                (q_in, qg.at[1, r, 0], qg_sem.at[r]),
                (g_in, qg.at[1, r, 1], qg_sem.at[r]),
            )
        ]
        away = [(*home[0][:2], in_send, home[0][2], (2 * host + c, u))] + [
            (home[n + 1][0], passing.at[n, l], in_send, pass_sem.at[n, l], (blk, via[n]))
            for n in range(3)
        ]
        return host, home, away

    def nth(n, line):
        return lax.rem(z + line + n, 3)

    for part in (slice(0, 2), slice(2, 4)):
        for n in range(3):
            host, home, away = inputs(nth(n, u))

            @pl.when(host != z)
            def _():
                for move in away[part]:
                    remote(*move).start()

            @pl.when(host == z)
            def _():
                for move in home[part]:
                    pltpu.make_async_copy(*move).start()

    @pl.when(is_host)
    def _():
        row = lax.broadcasted_iota(jnp.int32, (16, 16), 0)
        lane = lax.broadcasted_iota(jnp.int32, (16, 16), 1)
        ident = jnp.zeros((16, 16), jnp.int32)
        for j in range(16):
            side = c if j // NZ else 1 - c
            ident = jnp.where(row == j, order_ref[2 * lax.rem(z + j % NZ, NZ) + side], ident)
        hot = jnp.where(lane == ident, 1.0, 0.0).astype(BF16)
        wide = lax.broadcasted_iota(jnp.int32, (16, 128), 1)
        hot_wide = jnp.where(wide == ident[:, :1], 1.0, 0.0).astype(BF16)
        get_mask.wait()
        flat = jnp.where(mask[...] > 0, 1.0, 0.0).reshape(256, H).astype(BF16)
        head = lax.broadcasted_iota(jnp.int32, (H, 128), 0) == 3 * u + mine
        picked_out = nn(flat, jnp.where(head, 1.0, 0.0).astype(BF16))
        tall = lax.broadcasted_iota(jnp.int32, (16, 16, 128), 1)
        across = lax.broadcasted_iota(jnp.int32, (16, 16, 128), 2)
        table = jnp.where(tall == across, picked_out.reshape(16, 16, 128), 0.0)
        table = jnp.sum(table, axis=1).astype(BF16)
        by_query = nn(hot, table).astype(BF16)
        allowed = nt(by_query, hot_wide)
        one_side = lax.div(row, NZ) == lax.div(lane, NZ)
        before = jnp.where(jnp.logical_and(row < lane, one_side), 1.0, 0.0).astype(BF16)
        rank = nn(allowed.astype(BF16), before)
        near = jnp.where(lane >= NZ, allowed, 0.0)
        far = jnp.where(lane >= NZ, 0.0, allowed)
        listed = jnp.where(wide == COUNT, jnp.sum(near, axis=1, keepdims=True), 0.0)
        ends = SECOND + jnp.sum(far, axis=1, keepdims=True)
        listed = jnp.where(wide == COUNT + 1, ends, listed)
        for first, some in ((0, near), (SECOND, far)):
            for n in range(NZ):
                here = jnp.logical_and(some > 0.5, jnp.abs(rank - n) < 0.5)
                one = jnp.sum(jnp.where(here, lane.astype(F32), 0.0), axis=1, keepdims=True)
                listed = jnp.where(wide == first + n, one, listed)
        picked[...] = listed.astype(jnp.int32)

    def passed(n, l):
        host = lax.rem(lift(served[n]) + 3 * l, NZ)
        r = lax.rem(z - host + NZ, NZ)
        dst, sem = (
            (kv.at[1, r, 1], kv_sem.at[r]),
            (qg.at[1, r, 0], qg_sem.at[r]),
            (qg.at[1, r, 1], qg_sem.at[r]),
        )[n]
        there = (2 * host + c, served[n])
        return host != z, remote(passing.at[n, l], dst, pass_send.at[n, l], sem, there)

    for part in ((0,), (1, 2)):
        for i in range(3):
            for n in part:
                l = nth(i, served[n])
                on, move = passed(n, l)

                @pl.when(on)
                def _():
                    arrived(passing.at[n, l], pass_sem.at[n, l])
                    move.start()

    @pl.when(is_host)
    def _():
        for ref, sems, send, recv in (
            (kv, kv_sem, kv_send, kv_recv), (qg, qg_sem, qg_send, qg_recv)
        ):

            def share(n, carry, ref=ref, sems=sems, send=send, recv=recv):
                odd = lax.rem(n, 2)
                r = lax.rem(odd * lax.div(n + 1, 2) + (1 - odd) * (NZ - lax.div(n, 2)), NZ)
                arrived(ref.at[1, r], sems.at[r])
                remote(ref.at[1, r], ref.at[0, r], send, recv, sibling).start()
                return carry

            lax.fori_loop(0, NZ, share, 0)
        for ref, send, recv in ((kv, kv_send, kv_recv), (qg, qg_send, qg_recv)):
            arrived(ref.at[0], recv)
            arrived(ref.at[1], send)
        arrived(kv.at[0, pl.ds(0, 4)], in_send)

    @pl.when(jnp.logical_not(is_host))
    def _():
        arrived(kv.at[0, pl.ds(0, 6)], in_send)

    for l in range(3):
        for n in range(3):
            on, move = passed(n, l)
            pl.when(on)(move.wait_send)


def gradients(
    kv, qg, picked_in, dq_out, acc,
    picked, item_code, e_buf, d_buf, top_buf, row_top, row_sum, row_mix, dq_acc, sem,
):
    blk, u, z, c, is_host, mine = place()

    @pl.when(is_host)
    def _():
        get = pltpu.make_async_copy(picked_in, picked, sem)
        get.start()
        acc[NZ:] = jnp.zeros((NZ, 2, 128, 128), F32)
        dq_acc[NZ:] = jnp.zeros((NZ, 128, 128), F32)
        row_top[...] = jnp.full_like(row_top, -1e30)
        row_sum[...] = jnp.zeros_like(row_sum)
        row_mix[...] = jnp.zeros_like(row_mix)
        get.wait()

        def listing(rows, first, end, items):
            for r in rows:
                stop = picked[r, end]
                for base in range(first, first + NZ, SLOTS):
                    item_code[items] = r * 4096 + base * 64 + stop
                    items = items + (base < stop).astype(jnp.int32)
            return items

        def item(i):
            code = item_code[i]
            return lax.shift_right_logical(code, 12), lax.bitwise_and(lax.shift_right_logical(code, 6), 63), lax.bitwise_and(code, 63)

        own, other = range(NZ, 16), range(NZ)
        items = listing(own, 0, COUNT, jnp.int32(0))
        items = listing(other, 0, COUNT, items)
        needed = listing(own, SECOND, COUNT + 1, items)
        items = listing(other, SECOND, COUNT + 1, needed)
        for m in range(WIDE - 1):
            item_code[items + m] = EMPTY * 64

        def tiles(ref, r, base, part):
            return jnp.concatenate(
                [ref[picked[r, base + m], part] for m in range(SLOTS)], axis=0
            )

        def weigh(t, carry):
            for w in range(WIDE):
                i = t * WIDE + w
                r, base, end = item(i)
                scores = nt(tiles(kv, r, base, 0), qg[r, 0]) * (FACTOR * LOG2E)
                scores = jnp.concatenate(
                    [
                        scores[128 * m:128 * m + 128]
                        + jnp.where(base + m < end, 0.0, -1e30)
                        for m in range(SLOTS)
                    ],
                    axis=0,
                )
                top = jnp.max(scores, axis=0, keepdims=True)
                e = jnp.exp2(scores - top)
                dprob = nt(tiles(kv, r, base, 1), qg[r, 1])
                e_buf[i] = e
                d_buf[i] = dprob
                top_buf[i] = top
                total = jnp.sum(e, axis=0, keepdims=True)
                mixed = jnp.sum(e * dprob, axis=0, keepdims=True)
                old = row_top[r]
                new = jnp.maximum(old, top)
                keep = jnp.exp2(old - new)
                part = jnp.exp2(top - new)
                row_top[r] = new
                row_sum[r] = row_sum[r] * keep + total * part
                row_mix[r] = row_mix[r] * keep + mixed * part
            return carry

        lax.fori_loop(0, lax.div(items + WIDE - 1, WIDE), weigh, 0)

        def spread(t, carry):
            for w in range(WIDE):
                i = t * WIDE + w
                r, base, _ = item(i)
                whole = 1.0 / row_sum[r]
                prob = e_buf[i] * (jnp.exp2(top_buf[i] - row_top[r]) * whole)
                dscore = (prob * (d_buf[i] - row_mix[r] * whole)).astype(BF16)
                dk = nn(dscore, qg[r, 0])
                dv = nn(prob.astype(BF16), qg[r, 1])
                dq_acc[r] += lax.dot_general(
                    dscore, tiles(kv, r, base, 0), (((0,), (0,)), ((), ())),
                    preferred_element_type=F32,
                )
                for m in range(SLOTS):
                    j = picked[r, base + m]
                    acc[j, 0] += dk[128 * m:128 * m + 128]
                    acc[j, 1] += dv[128 * m:128 * m + 128]
            return carry

        lax.fori_loop(0, lax.div(needed + WIDE - 1, WIDE), spread, 0)
        dq_out[...] = (dq_acc[NZ:] * FACTOR).astype(BF16)


def give_back(
    dq_in, acc, f_q, f_kv, kv_out, r_q, r_kv, t_q,
    p1q_send, p1k_send, rq_sem, rkv_sem, p2q_send, p2k_send, fq_sem, fkv_sem, others,
):
    blk, u, z, c, is_host, mine = place()
    seat = mine * 2 + lax.rem(lax.div(u, 4), 2)
    rest = jnp.logical_not(is_host)
    barrier = pltpu.get_barrier_semaphore()

    def greet(there, other):
        @pl.when(jnp.logical_or(rest, jnp.logical_not(other)))
        def _():
            pl.semaphore_signal(barrier, inc=1, device_id=there, device_id_type=MESH)

    def greet_line(r, carry):
        h = lax.rem(z + r, NZ)
        greet((2 * h + c, u), hosted(h, u)[0])
        return carry

    def greet_plane(n, carry):
        to = lax.rem(u + n, NU)
        greet((blk, to), hosted(z, to)[0])
        return carry

    lax.fori_loop(1, NZ, greet_line, 0)
    lax.fori_loop(1, NU, greet_plane, 0)

    @pl.when(is_host)
    def _():
        def stage(r, carry):
            dk = acc[NZ + r, 0] * FACTOR
            dv = acc[NZ + r, 1]
            for n in range(NU):
                piece = jnp.concatenate([dk[8 * n:8 * n + 8], dv[8 * n:8 * n + 8]], axis=0)
                kv_out[n, lax.rem(z + r, NZ)] = piece.astype(BF16)
            return carry

        lax.fori_loop(0, NZ, stage, 0)

    pl.semaphore_wait(barrier, 22 - 7 * is_host.astype(jnp.int32))

    def tell(there):
        pl.semaphore_signal(others, inc=1, device_id=there, device_id_type=MESH)

    @pl.when(rest)
    def _():
        below = lax.rem(z + NZ - 1, NZ)
        right, _, left = beside(u)
        left_hosts, left_head = hosted(z, left)
        right_hosts, right_head = hosted(z, right)
        pl.when(hosted(below, u)[0])(functools.partial(tell, (2 * below + c, u)))
        on = jnp.logical_and(left_hosts, left_head > 0)
        pl.when(on)(functools.partial(tell, (blk, left)))
        on = jnp.logical_and(right_hosts, right_head == 0)
        pl.when(on)(functools.partial(tell, (blk, right)))

    @pl.when(is_host)
    def _():
        def send_k(part, to_hosts):
            heights = pl.ds(4 * part, 4)

            def one(n, carry):
                to = lax.rem(u + n, NU)

                @pl.when(hosted(z, to)[0] == to_hosts)
                def _():
                    remote(
                        kv_out.at[to, heights], r_kv.at[seat, heights],
                        p1k_send, rkv_sem.at[part, seat], (blk, to),
                    ).start()

                return carry

            lax.fori_loop(1, NU, one, 0)

        def send_q(to_hosts):
            def one(h, carry):
                on = jnp.logical_and(h != z, hosted(h, u)[0] == to_hosts)

                @pl.when(on)
                def _():
                    tile = dq_in.at[lax.rem(h - z + NZ, NZ)]
                    remote(tile, r_q.at[mine], p1q_send, rq_sem, (2 * h + c, u)).start()

                return carry

            lax.fori_loop(0, NZ, one, 0)

        send_k(0, False)
        send_q(False)
        send_k(1, False)
        pltpu.make_async_copy(dq_in.at[0], r_q.at[mine], rq_sem).start()
        for part in range(2):
            heights = pl.ds(4 * part, 4)
            pltpu.make_async_copy(
                kv_out.at[u, heights], r_kv.at[seat, heights], rkv_sem.at[part, seat]
            ).start()
        pl.semaphore_wait(others, 2)
        send_k(0, True)
        send_q(True)
        send_k(1, True)

    def pass_k(part):
        for at in range(6):
            arrived(r_kv.at[at, pl.ds(4 * part, 4)], rkv_sem.at[part, at])

            def one(h, carry, at=at):
                @pl.when(h != z)
                def _():
                    there = (2 * h + c, u)
                    remote(r_kv.at[at, h], f_kv.at[z, at], p2k_send, fkv_sem, there).start()

                @pl.when(h == z)
                def _():
                    pltpu.make_async_copy(r_kv.at[at, h], f_kv.at[z, at], fkv_sem).start()

                return carry

            lax.fori_loop(4 * part, 4 * part + 4, one, 0)

    pass_k(0)

    arrived(r_q, rq_sem)
    heads = [r_q[l].astype(F32) for l in range(3)]
    for i in range(NU):
        rows = slice(8 * i, 8 * i + 8)
        t_q[i, :16] = jnp.concatenate([heads[0][rows], heads[1][rows]], axis=0).astype(BF16)
        t_q[i, 16:] = jnp.concatenate([heads[2][rows], heads[2][rows]], axis=0).astype(BF16)

    def pass_q(i, carry):
        to = lax.rem(u + i, NU)
        remote(t_q.at[to], f_q.at[u], p2q_send, fq_sem, (blk, to)).start()
        return carry

    lax.fori_loop(1, NU, pass_q, 0)
    pltpu.make_async_copy(t_q.at[u], f_q.at[u], fq_sem).start()

    pass_k(1)

    @pl.when(is_host)
    def _():
        arrived(dq_in.at[pl.ds(0, NZ - 1)], p1q_send)
        arrived(kv_out.at[pl.ds(0, NU - 1)], p1k_send)

    arrived(r_kv.at[:, pl.ds(0, NZ - 1)], p2k_send)
    arrived(t_q.at[pl.ds(0, NU - 1)], p2q_send)
    arrived(f_q, fq_sem)
    arrived(f_kv, fkv_sem)


def assemble(f_q, f_kv, q_hbm, k_hbm, v_hbm, out_q, out_k, out_v, sems):
    def columns(head):
        return slice(head * DH, head * DH + DH)

    copies = [
        pltpu.make_async_copy(src, dst, sems.at[n])
        for n, (src, dst) in enumerate(((out_q, q_hbm), (out_k, k_hbm), (out_v, v_hbm)))
    ]
    for n in range(NU):
        first = f_q[n, :16].astype(F32)
        out_q[:, columns(3 * n)] = first[:8].astype(BF16)
        out_q[:, columns(3 * n + 1)] = first[8:].astype(BF16)
        out_q[:, columns(3 * n + 2)] = f_q[n, 16:].astype(F32)[:8].astype(BF16)
    copies[0].start()
    for d in range(NZ):
        for l in range(3):
            for half in range(2):
                both = f_kv[d, 2 * l + half].astype(F32)
                up = (d - 3 * l) % NZ
                x = (up - up % 2 - 4 * half) % NZ // 2
                head = 3 * (4 * (2 * (up % 2) + half) + x) + l
                out_k[:, columns(head)] = both[:8].astype(BF16)
                out_v[:, columns(head)] = both[8:].astype(BF16)
    copies[1].start()
    copies[2].start()
    for copy in copies:
        copy.wait()


def local(query, key, value, grad_out, tile_mask, tile_order):
    anywhere = pl.BlockSpec(memory_space=pl.ANY)
    vmem = pl.BlockSpec(memory_space=pltpu.VMEM)
    smem = pl.BlockSpec(memory_space=pltpu.SMEM)
    dma = pltpu.SemaphoreType.DMA
    shape = jax.ShapeDtypeStruct
    most = 16 * 16 // SLOTS + WIDE
    operands = (query, key, value, grad_out, jnp.transpose(tile_mask, (1, 2, 0)), tile_order)
    kv, qg, picked = pl.pallas_call(
        collect,
        out_shape=(
            shape((2, NZ, 2, 128, 128), BF16),
            shape((2, NZ, 2, 128, 128), BF16),
            shape((16, 128), jnp.int32),
        ),
        in_specs=[anywhere] * 5 + [smem],
        out_specs=(vmem, vmem, vmem),
        scratch_shapes=[
            pltpu.VMEM((16, 16, H), jnp.int32),
            pltpu.VMEM((3, 3, 128, 128), BF16),
            dma, dma((NZ,)), dma((NZ,)), dma, dma, dma, dma, dma, dma((3, 3)), dma((3, 3)),
        ],
        compiler_params=pltpu.CompilerParams(
            collective_id=0, has_side_effects=True, vmem_limit_bytes=16 * 1024 * 1024
        ),
    )(*[pltpu.with_memory_space_constraint(a, pltpu.HBM) for a in operands])
    dq, acc = pl.pallas_call(
        gradients,
        out_shape=(
            shape((NZ, 128, 128), BF16),
            shape((16, 2, 128, 128), F32),
        ),
        in_specs=[vmem, vmem, anywhere],
        out_specs=(vmem, vmem),
        scratch_shapes=[
            pltpu.SMEM((16, 128), jnp.int32),
            pltpu.SMEM((most,), jnp.int32),
            pltpu.VMEM((most, 128 * SLOTS, 128), F32),
            pltpu.VMEM((most, 128 * SLOTS, 128), F32),
            pltpu.VMEM((most, 1, 128), F32),
            pltpu.VMEM((16, 1, 128), F32),
            pltpu.VMEM((16, 1, 128), F32),
            pltpu.VMEM((16, 1, 128), F32),
            pltpu.VMEM((16, 128, 128), F32),
            dma,
        ],
        compiler_params=pltpu.CompilerParams(vmem_limit_bytes=48 * 1024 * 1024),
    )(kv.reshape(16, 2, 128, 128), qg.reshape(16, 2, 128, 128), picked)
    f_q, f_kv = pl.pallas_call(
        give_back,
        out_shape=(shape((NU, 32, 128), BF16), shape((NZ, 6, 16, 128), BF16)),
        in_specs=[vmem] * 2,
        out_specs=(vmem, vmem),
        scratch_shapes=[
            pltpu.VMEM((NU, NZ, 16, 128), BF16),
            pltpu.VMEM((3, 128, 128), BF16),
            pltpu.VMEM((6, NZ, 16, 128), BF16),
            pltpu.VMEM((NU, 32, 128), BF16),
            dma, dma, dma, dma((2, 6)), dma, dma, dma, dma,
            pltpu.SemaphoreType.REGULAR,
        ],
        compiler_params=pltpu.CompilerParams(
            collective_id=1, has_side_effects=True, vmem_limit_bytes=16 * 1024 * 1024
        ),
    )(dq, acc)
    out = shape((8, H * DH), BF16)
    return pl.pallas_call(
        assemble,
        out_shape=(out, out, out),
        in_specs=[vmem] * 2,
        out_specs=(anywhere, anywhere, anywhere),
        scratch_shapes=[pltpu.VMEM((8, H * DH), BF16)] * 3 + [dma((3,))],
        compiler_params=pltpu.CompilerParams(vmem_limit_bytes=8 * 1024 * 1024),
    )(*[pltpu.with_memory_space_constraint(a, pltpu.VMEM) for a in (f_q, f_kv)])


def solution(mesh):
    placed = (P("blk", "uly"), P("blk", "uly"), P("blk", "uly"), P("blk", "uly"), P(), P())
    return jax.shard_map(
        local,
        mesh=mesh,
        in_specs=placed,
        out_specs=(P(("blk", "uly"), None), P(("blk", "uly"), None), P(("blk", "uly"), None)),
        check_vma=False,
    )
```

```python
import functools

import jax
import jax.numpy as jnp
from jax import lax
from jax.experimental import pallas as pl
from jax.experimental.pallas import tpu as pltpu
from jax.sharding import PartitionSpec as P

H = 48
DH = 128
TILE = 128
NZ = 8
NU = 16
SLOTS = 2
WIDE = 6
SECOND = 16
COUNT = 32
EMPTY = 40
MESH = pl.DeviceIdType.MESH
FACTOR = DH ** -0.5
LOG2E = 1.4426950408889634
F32 = jnp.float32
BF16 = jnp.bfloat16


def nt(a, b):
    return lax.dot_general(a, b, (((1,), (1,)), ((), ())), preferred_element_type=F32)


def nn(a, b):
    return lax.dot_general(a, b, (((1,), (0,)), ((), ())), preferred_element_type=F32)


def lift(u):
    x, y = lax.rem(u, 4), lax.div(u, 4)
    return lax.rem(2 * x + 4 * lax.rem(y, 2) + lax.div(y, 2), NZ)


def beside(u):
    x, y = lax.rem(u, 4), lax.div(u, 4)
    other = y + 1 - 2 * lax.rem(y, 2)
    return 4 * y + lax.rem(x + 1, 4), 4 * other + x, 4 * y + lax.rem(x + 3, 4)


def hosted(z, u):
    rel = lax.rem(z - lift(u) + NZ, NZ)
    yes = jnp.logical_or(rel == 0, jnp.logical_or(rel == 3, rel == 6))
    return yes, lax.div(rel, 3)


def remote(src, dst, send, recv, there):
    return pltpu.make_async_remote_copy(
        src_ref=src, dst_ref=dst, send_sem=send, recv_sem=recv,
        device_id=there, device_id_type=MESH,
    )


def arrived(ref, sem):
    pltpu.make_async_copy(ref, ref, sem).wait()


def place():
    blk = lax.axis_index("blk")
    u = lax.axis_index("uly")
    z = lax.div(blk, 2)
    c = lax.rem(blk, 2)
    is_host, mine = hosted(z, u)
    return blk, u, z, c, is_host, mine


def collect(
    q_in, k_in, v_in, g_in, mask_in, order_ref, kv, qg, picked,
    mask, passing, in_send, kv_sem, qg_sem, kv_send, kv_recv, qg_send, qg_recv,
    mask_sem, pass_sem, pass_send,
):
    blk, u, z, c, is_host, mine = place()
    sibling = (2 * z + 1 - c, u)
    via = beside(u)
    served = (via[2], via[1], via[0])
    barrier = pltpu.get_barrier_semaphore()
    get_mask = pltpu.make_async_copy(mask_in, mask, mask_sem)

    def greet(there):
        pl.semaphore_signal(barrier, inc=1, device_id=there, device_id_type=MESH)

    @pl.when(is_host)
    def _():
        get_mask.start()

        def greet_line(r, carry):
            greet((2 * lax.rem(z + r, NZ) + c, u))
            return carry

        lax.fori_loop(1, NZ, greet_line, 0)
        greet(sibling)

    for line in served:
        greet((blk, line))

    pl.semaphore_wait(barrier, 6)

    def inputs(l):
        host = lax.rem(lift(u) + 3 * l, NZ)
        r = lax.rem(z - host + NZ, NZ)
        cols = pl.ds(pl.multiple_of(l * DH, DH), DH)
        home = [
            (src.at[:, cols], dst, sem)
            for src, dst, sem in (
                (k_in, kv.at[1, r, 0], kv_sem.at[r]),
                (v_in, kv.at[1, r, 1], kv_sem.at[r]),
                (q_in, qg.at[1, r, 0], qg_sem.at[r]),
                (g_in, qg.at[1, r, 1], qg_sem.at[r]),
            )
        ]
        away = [(*home[0][:2], in_send, home[0][2], (2 * host + c, u))] + [
            (home[n + 1][0], passing.at[n, l], in_send, pass_sem.at[n, l], (blk, via[n]))
            for n in range(3)
        ]
        return host, home, away

    def nth(n, line):
        return lax.rem(z + line + n, 3)

    for part in (slice(0, 2), slice(2, 4)):
        for n in range(3):
            host, home, away = inputs(nth(n, u))

            @pl.when(host != z)
            def _():
                for move in away[part]:
                    remote(*move).start()

            @pl.when(host == z)
            def _():
                for move in home[part]:
                    pltpu.make_async_copy(*move).start()

    @pl.when(is_host)
    def _():
        row = lax.broadcasted_iota(jnp.int32, (16, 16), 0)
        lane = lax.broadcasted_iota(jnp.int32, (16, 16), 1)
        ident = jnp.zeros((16, 16), jnp.int32)
        for j in range(16):
            side = c if j // NZ else 1 - c
            ident = jnp.where(row == j, order_ref[2 * lax.rem(z + j % NZ, NZ) + side], ident)
        hot = jnp.where(lane == ident, 1.0, 0.0).astype(BF16)
        wide = lax.broadcasted_iota(jnp.int32, (16, 128), 1)
        hot_wide = jnp.where(wide == ident[:, :1], 1.0, 0.0).astype(BF16)
        get_mask.wait()
        flat = jnp.where(mask[...] > 0, 1.0, 0.0).reshape(256, H).astype(BF16)
        head = lax.broadcasted_iota(jnp.int32, (H, 128), 0) == 3 * u + mine
        picked_out = nn(flat, jnp.where(head, 1.0, 0.0).astype(BF16))
        tall = lax.broadcasted_iota(jnp.int32, (16, 16, 128), 1)
        across = lax.broadcasted_iota(jnp.int32, (16, 16, 128), 2)
        table = jnp.where(tall == across, picked_out.reshape(16, 16, 128), 0.0)
        table = jnp.sum(table, axis=1).astype(BF16)
        by_query = nn(hot, table).astype(BF16)
        allowed = nt(by_query, hot_wide)
        one_side = lax.div(row, NZ) == lax.div(lane, NZ)
        before = jnp.where(jnp.logical_and(row < lane, one_side), 1.0, 0.0).astype(BF16)
        rank = nn(allowed.astype(BF16), before)
        near = jnp.where(lane >= NZ, allowed, 0.0)
        far = jnp.where(lane >= NZ, 0.0, allowed)
        listed = jnp.where(wide == COUNT, jnp.sum(near, axis=1, keepdims=True), 0.0)
        ends = SECOND + jnp.sum(far, axis=1, keepdims=True)
        listed = jnp.where(wide == COUNT + 1, ends, listed)
        for first, some in ((0, near), (SECOND, far)):
            for n in range(NZ):
                here = jnp.logical_and(some > 0.5, jnp.abs(rank - n) < 0.5)
                one = jnp.sum(jnp.where(here, lane.astype(F32), 0.0), axis=1, keepdims=True)
                listed = jnp.where(wide == first + n, one, listed)
        picked[...] = listed.astype(jnp.int32)

    def passed(n, l):
        host = lax.rem(lift(served[n]) + 3 * l, NZ)
        r = lax.rem(z - host + NZ, NZ)
        dst, sem = (
            (kv.at[1, r, 1], kv_sem.at[r]),
            (qg.at[1, r, 0], qg_sem.at[r]),
            (qg.at[1, r, 1], qg_sem.at[r]),
        )[n]
        there = (2 * host + c, served[n])
        return host != z, remote(passing.at[n, l], dst, pass_send.at[n, l], sem, there)

    for part in ((0,), (1, 2)):
        for i in range(3):
            for n in part:
                l = nth(i, served[n])
                on, move = passed(n, l)

                @pl.when(on)
                def _():
                    arrived(passing.at[n, l], pass_sem.at[n, l])
                    move.start()

    @pl.when(is_host)
    def _():
        for ref, sems, send, recv in (
            (kv, kv_sem, kv_send, kv_recv), (qg, qg_sem, qg_send, qg_recv)
        ):

            def share(n, carry, ref=ref, sems=sems, send=send, recv=recv):
                odd = lax.rem(n, 2)
                r = lax.rem(odd * lax.div(n + 1, 2) + (1 - odd) * (NZ - lax.div(n, 2)), NZ)
                arrived(ref.at[1, r], sems.at[r])
                remote(ref.at[1, r], ref.at[0, r], send, recv, sibling).start()
                return carry

            lax.fori_loop(0, NZ, share, 0)
        for ref, send, recv in ((kv, kv_send, kv_recv), (qg, qg_send, qg_recv)):
            arrived(ref.at[0], recv)
            arrived(ref.at[1], send)
        arrived(kv.at[0, pl.ds(0, 4)], in_send)

    @pl.when(jnp.logical_not(is_host))
    def _():
        arrived(kv.at[0, pl.ds(0, 6)], in_send)

    for l in range(3):
        for n in range(3):
            on, move = passed(n, l)
            pl.when(on)(move.wait_send)


def gradients(
    kv, qg, picked_in, dq_out, acc,
    picked, item_code, e_buf, d_buf, top_buf, row_top, row_sum, row_mix, dq_acc, sem,
):
    blk, u, z, c, is_host, mine = place()

    @pl.when(is_host)
    def _():
        get = pltpu.make_async_copy(picked_in, picked, sem)
        get.start()
        acc[NZ:] = jnp.zeros((NZ, 2, 128, 128), F32)
        dq_acc[NZ:] = jnp.zeros((NZ, 128, 128), F32)
        row_top[...] = jnp.full_like(row_top, -1e30)
        row_sum[...] = jnp.zeros_like(row_sum)
        row_mix[...] = jnp.zeros_like(row_mix)
        get.wait()

        def listing(rows, first, end, items):
            for r in rows:
                stop = picked[r, end]
                for base in range(first, first + NZ, SLOTS):
                    item_code[items] = r * 4096 + base * 64 + stop
                    items = items + (base < stop).astype(jnp.int32)
            return items

        def item(i):
            code = item_code[i]
            return lax.shift_right_logical(code, 12), lax.bitwise_and(lax.shift_right_logical(code, 6), 63), lax.bitwise_and(code, 63)

        own, other = range(NZ, 16), range(NZ)
        items = listing(own, 0, COUNT, jnp.int32(0))
        items = listing(other, 0, COUNT, items)
        needed = listing(own, SECOND, COUNT + 1, items)
        items = listing(other, SECOND, COUNT + 1, needed)
        for m in range(WIDE - 1):
            item_code[items + m] = EMPTY * 64

        def keys(r, base):
            return jnp.concatenate([kv[picked[r, base + m], 0] for m in range(SLOTS)], axis=0)

        def values(r, base):
            return jnp.concatenate([kv[picked[r, base + m], 1] for m in range(SLOTS)], axis=0)

        def diagonal(r):
            none = jnp.zeros((128, 128), BF16)
            return jnp.concatenate(
                [
                    jnp.concatenate([qg[r, 0], none], axis=1),
                    jnp.concatenate([none, qg[r, 1]], axis=1),
                ],
                axis=0,
            )

        def weigh(t, carry):
            for w in range(WIDE):
                i = t * WIDE + w
                r, base, end = item(i)
                both = nt(
                    jnp.concatenate([keys(r, base), values(r, base)], axis=1), diagonal(r)
                )
                scores = both[:, :128] * (FACTOR * LOG2E)
                scores = jnp.concatenate(
                    [
                        scores[128 * m:128 * m + 128]
                        + jnp.where(base + m < end, 0.0, -1e30)
                        for m in range(SLOTS)
                    ],
                    axis=0,
                )
                top = jnp.max(scores, axis=0, keepdims=True)
                e = jnp.exp2(scores - top)
                dprob = both[:, 128:]
                e_buf[i] = e
                d_buf[i] = dprob
                top_buf[i] = top
                total = jnp.sum(e, axis=0, keepdims=True)
                mixed = jnp.sum(e * dprob, axis=0, keepdims=True)
                old = row_top[r]
                new = jnp.maximum(old, top)
                keep = jnp.exp2(old - new)
                part = jnp.exp2(top - new)
                row_top[r] = new
                row_sum[r] = row_sum[r] * keep + total * part
                row_mix[r] = row_mix[r] * keep + mixed * part
            return carry

        lax.fori_loop(0, lax.div(items + WIDE - 1, WIDE), weigh, 0)

        def spread(t, carry):
            for w in range(WIDE):
                i = t * WIDE + w
                r, base, _ = item(i)
                whole = 1.0 / row_sum[r]
                prob = e_buf[i] * (jnp.exp2(top_buf[i] - row_top[r]) * whole)
                dscore = (prob * (d_buf[i] - row_mix[r] * whole)).astype(BF16)
                both = nn(
                    jnp.concatenate([dscore, prob.astype(BF16)], axis=1), diagonal(r)
                )
                dq_acc[r] += lax.dot_general(
                    dscore, keys(r, base), (((0,), (0,)), ((), ())),
                    preferred_element_type=F32,
                )
                for m in range(SLOTS):
                    j = picked[r, base + m]
                    acc[j, 0] += both[128 * m:128 * m + 128, :128]
                    acc[j, 1] += both[128 * m:128 * m + 128, 128:]
            return carry

        lax.fori_loop(0, lax.div(needed + WIDE - 1, WIDE), spread, 0)
        dq_out[...] = (dq_acc[NZ:] * FACTOR).astype(BF16)


def give_back(
    dq_in, acc, f_q, f_kv, kv_out, r_q, r_kv, t_q,
    p1q_send, p1k_send, rq_sem, rkv_sem, p2q_send, p2k_send, fq_sem, fkv_sem, others,
):
    blk, u, z, c, is_host, mine = place()
    seat = mine * 2 + lax.rem(lax.div(u, 4), 2)
    rest = jnp.logical_not(is_host)
    barrier = pltpu.get_barrier_semaphore()

    def greet(there, other):
        @pl.when(jnp.logical_or(rest, jnp.logical_not(other)))
        def _():
            pl.semaphore_signal(barrier, inc=1, device_id=there, device_id_type=MESH)

    def greet_line(r, carry):
        h = lax.rem(z + r, NZ)
        greet((2 * h + c, u), hosted(h, u)[0])
        return carry

    def greet_plane(n, carry):
        to = lax.rem(u + n, NU)
        greet((blk, to), hosted(z, to)[0])
        return carry

    lax.fori_loop(1, NZ, greet_line, 0)
    lax.fori_loop(1, NU, greet_plane, 0)

    pl.semaphore_wait(barrier, 22 - 7 * is_host.astype(jnp.int32))

    def tell(there):
        pl.semaphore_signal(others, inc=1, device_id=there, device_id_type=MESH)

    @pl.when(rest)
    def _():
        below = lax.rem(z + NZ - 1, NZ)
        right, _, left = beside(u)
        left_hosts, left_head = hosted(z, left)
        right_hosts, right_head = hosted(z, right)
        pl.when(hosted(below, u)[0])(functools.partial(tell, (2 * below + c, u)))
        on = jnp.logical_and(left_hosts, left_head > 0)
        pl.when(on)(functools.partial(tell, (blk, left)))
        on = jnp.logical_and(right_hosts, right_head == 0)
        pl.when(on)(functools.partial(tell, (blk, right)))

    @pl.when(is_host)
    def _():
        def stage(h, carry):
            r = lax.rem(h - z + NZ, NZ)
            dk = acc[NZ + r, 0] * FACTOR
            dv = acc[NZ + r, 1]
            for n in range(NU):
                piece = jnp.concatenate([dk[8 * n:8 * n + 8], dv[8 * n:8 * n + 8]], axis=0)
                kv_out[n, h] = piece.astype(BF16)
            return carry

        def send_k(part, to_hosts):
            heights = pl.ds(4 * part, 4)

            def one(n, carry):
                to = lax.rem(u + n, NU)

                @pl.when(hosted(z, to)[0] == to_hosts)
                def _():
                    remote(
                        kv_out.at[to, heights], r_kv.at[seat, heights],
                        p1k_send, rkv_sem.at[part], (blk, to),
                    ).start()

                return carry

            lax.fori_loop(1, NU, one, 0)

        def send_q(to_hosts):
            def one(h, carry):
                on = jnp.logical_and(h != z, hosted(h, u)[0] == to_hosts)

                @pl.when(on)
                def _():
                    tile = dq_in.at[lax.rem(h - z + NZ, NZ)]
                    remote(tile, r_q.at[mine], p1q_send, rq_sem, (2 * h + c, u)).start()

                return carry

            lax.fori_loop(0, NZ, one, 0)

        send_q(False)
        pltpu.make_async_copy(dq_in.at[0], r_q.at[mine], rq_sem).start()
        for part in range(2):
            lax.fori_loop(4 * part, 4 * part + 4, stage, 0)
            send_k(part, False)
            heights = pl.ds(4 * part, 4)
            pltpu.make_async_copy(
                kv_out.at[u, heights], r_kv.at[seat, heights], rkv_sem.at[part]
            ).start()
        pl.semaphore_wait(others, 2)
        send_q(True)
        send_k(0, True)
        send_k(1, True)

    arrived(r_q, rq_sem)
    heads = [r_q[l].astype(F32) for l in range(3)]
    for i in range(NU):
        rows = slice(8 * i, 8 * i + 8)
        t_q[i, :16] = jnp.concatenate([heads[0][rows], heads[1][rows]], axis=0).astype(BF16)
        t_q[i, 16:] = jnp.concatenate([heads[2][rows], heads[2][rows]], axis=0).astype(BF16)

    def pass_q(i, carry):
        to = lax.rem(u + i, NU)
        remote(t_q.at[to], f_q.at[u], p2q_send, fq_sem, (blk, to)).start()
        return carry

    lax.fori_loop(1, NU, pass_q, 0)
    pltpu.make_async_copy(t_q.at[u], f_q.at[u], fq_sem).start()

    def pass_k(h, carry):
        @pl.when(h != z)
        def _():
            remote(r_kv.at[:, h], f_kv.at[z], p2k_send, fkv_sem, (2 * h + c, u)).start()

        @pl.when(h == z)
        def _():
            pltpu.make_async_copy(r_kv.at[:, h], f_kv.at[z], fkv_sem).start()

        return carry

    for part in range(2):
        arrived(r_kv.at[:, pl.ds(4 * part, 4)], rkv_sem.at[part])
        lax.fori_loop(4 * part, 4 * part + 4, pass_k, 0)

    @pl.when(is_host)
    def _():
        arrived(dq_in.at[pl.ds(0, NZ - 1)], p1q_send)
        arrived(kv_out.at[pl.ds(0, NU - 1)], p1k_send)

    arrived(r_kv.at[:, pl.ds(0, NZ - 1)], p2k_send)
    arrived(t_q.at[pl.ds(0, NU - 1)], p2q_send)
    arrived(f_q, fq_sem)
    arrived(f_kv, fkv_sem)


def assemble(f_q, f_kv, q_hbm, k_hbm, v_hbm, out_q, out_k, out_v, sems):
    def columns(head):
        return slice(head * DH, head * DH + DH)

    copies = [
        pltpu.make_async_copy(src, dst, sems.at[n])
        for n, (src, dst) in enumerate(((out_q, q_hbm), (out_k, k_hbm), (out_v, v_hbm)))
    ]
    for n in range(NU):
        first = f_q[n, :16].astype(F32)
        out_q[:, columns(3 * n)] = first[:8].astype(BF16)
        out_q[:, columns(3 * n + 1)] = first[8:].astype(BF16)
        out_q[:, columns(3 * n + 2)] = f_q[n, 16:].astype(F32)[:8].astype(BF16)
    copies[0].start()
    for d in range(NZ):
        for l in range(3):
            for half in range(2):
                both = f_kv[d, 2 * l + half].astype(F32)
                up = (d - 3 * l) % NZ
                x = (up - up % 2 - 4 * half) % NZ // 2
                head = 3 * (4 * (2 * (up % 2) + half) + x) + l
                out_k[:, columns(head)] = both[:8].astype(BF16)
                out_v[:, columns(head)] = both[8:].astype(BF16)
    copies[1].start()
    copies[2].start()
    for copy in copies:
        copy.wait()


def local(query, key, value, grad_out, tile_mask, tile_order):
    anywhere = pl.BlockSpec(memory_space=pl.ANY)
    vmem = pl.BlockSpec(memory_space=pltpu.VMEM)
    smem = pl.BlockSpec(memory_space=pltpu.SMEM)
    dma = pltpu.SemaphoreType.DMA
    shape = jax.ShapeDtypeStruct
    most = 16 * 16 // SLOTS + WIDE
    operands = (query, key, value, grad_out, jnp.transpose(tile_mask, (1, 2, 0)), tile_order)
    kv, qg, picked = pl.pallas_call(
        collect,
        out_shape=(
            shape((2, NZ, 2, 128, 128), BF16),
            shape((2, NZ, 2, 128, 128), BF16),
            shape((16, 128), jnp.int32),
        ),
        in_specs=[anywhere] * 5 + [smem],
        out_specs=(vmem, vmem, vmem),
        scratch_shapes=[
            pltpu.VMEM((16, 16, H), jnp.int32),
            pltpu.VMEM((3, 3, 128, 128), BF16),
            dma, dma((NZ,)), dma((NZ,)), dma, dma, dma, dma, dma, dma((3, 3)), dma((3, 3)),
        ],
        compiler_params=pltpu.CompilerParams(
            collective_id=0, has_side_effects=True, vmem_limit_bytes=16 * 1024 * 1024
        ),
    )(*[pltpu.with_memory_space_constraint(a, pltpu.HBM) for a in operands])
    dq, acc = pl.pallas_call(
        gradients,
        out_shape=(
            shape((NZ, 128, 128), BF16),
            shape((16, 2, 128, 128), F32),
        ),
        in_specs=[vmem, vmem, anywhere],
        out_specs=(vmem, vmem),
        scratch_shapes=[
            pltpu.SMEM((16, 128), jnp.int32),
            pltpu.SMEM((most,), jnp.int32),
            pltpu.VMEM((most, 128 * SLOTS, 128), F32),
            pltpu.VMEM((most, 128 * SLOTS, 128), F32),
            pltpu.VMEM((most, 1, 128), F32),
            pltpu.VMEM((16, 1, 128), F32),
            pltpu.VMEM((16, 1, 128), F32),
            pltpu.VMEM((16, 1, 128), F32),
            pltpu.VMEM((16, 128, 128), F32),
            dma,
        ],
        compiler_params=pltpu.CompilerParams(vmem_limit_bytes=48 * 1024 * 1024),
    )(kv.reshape(16, 2, 128, 128), qg.reshape(16, 2, 128, 128), picked)
    f_q, f_kv = pl.pallas_call(
        give_back,
        out_shape=(shape((NU, 32, 128), BF16), shape((NZ, 6, 16, 128), BF16)),
        in_specs=[vmem] * 2,
        out_specs=(vmem, vmem),
        scratch_shapes=[
            pltpu.VMEM((NU, NZ, 16, 128), BF16),
            pltpu.VMEM((3, 128, 128), BF16),
            pltpu.VMEM((6, NZ, 16, 128), BF16),
            pltpu.VMEM((NU, 32, 128), BF16),
            dma, dma, dma, dma((2,)), dma, dma, dma, dma,
            pltpu.SemaphoreType.REGULAR,
        ],
        compiler_params=pltpu.CompilerParams(
            collective_id=1, has_side_effects=True, vmem_limit_bytes=16 * 1024 * 1024
        ),
    )(dq, acc)
    out = shape((8, H * DH), BF16)
    return pl.pallas_call(
        assemble,
        out_shape=(out, out, out),
        in_specs=[vmem] * 2,
        out_specs=(anywhere, anywhere, anywhere),
        scratch_shapes=[pltpu.VMEM((8, H * DH), BF16)] * 3 + [dma((3,))],
        compiler_params=pltpu.CompilerParams(vmem_limit_bytes=8 * 1024 * 1024),
    )(*[pltpu.with_memory_space_constraint(a, pltpu.VMEM) for a in (f_q, f_kv)])


def solution(mesh):
    placed = (P("blk", "uly"), P("blk", "uly"), P("blk", "uly"), P("blk", "uly"), P(), P())
    return jax.shard_map(
        local,
        mesh=mesh,
        in_specs=placed,
        out_specs=(P(("blk", "uly"), None), P(("blk", "uly"), None), P(("blk", "uly"), None)),
        check_vma=False,
    )
```

```python
import functools

import jax
import jax.numpy as jnp
from jax import lax
from jax.experimental import pallas as pl
from jax.experimental.pallas import tpu as pltpu
from jax.sharding import PartitionSpec as P

H = 48
DH = 128
TILE = 128
NZ = 8
NU = 16
SLOTS = 1
WIDE = 12
SECOND = 16
COUNT = 32
EMPTY = 40
MESH = pl.DeviceIdType.MESH
FACTOR = DH ** -0.5
LOG2E = 1.4426950408889634
F32 = jnp.float32
BF16 = jnp.bfloat16


def nt(a, b):
    return lax.dot_general(a, b, (((1,), (1,)), ((), ())), preferred_element_type=F32)


def nn(a, b):
    return lax.dot_general(a, b, (((1,), (0,)), ((), ())), preferred_element_type=F32)


def lift(u):
    x, y = lax.rem(u, 4), lax.div(u, 4)
    return lax.rem(2 * x + 4 * lax.rem(y, 2) + lax.div(y, 2), NZ)


def beside(u):
    x, y = lax.rem(u, 4), lax.div(u, 4)
    other = y + 1 - 2 * lax.rem(y, 2)
    return 4 * y + lax.rem(x + 1, 4), 4 * other + x, 4 * y + lax.rem(x + 3, 4)


def hosted(z, u):
    rel = lax.rem(z - lift(u) + NZ, NZ)
    yes = jnp.logical_or(rel == 0, jnp.logical_or(rel == 3, rel == 6))
    return yes, lax.div(rel, 3)


def remote(src, dst, send, recv, there):
    return pltpu.make_async_remote_copy(
        src_ref=src, dst_ref=dst, send_sem=send, recv_sem=recv,
        device_id=there, device_id_type=MESH,
    )


def arrived(ref, sem):
    pltpu.make_async_copy(ref, ref, sem).wait()


def place():
    blk = lax.axis_index("blk")
    u = lax.axis_index("uly")
    z = lax.div(blk, 2)
    c = lax.rem(blk, 2)
    is_host, mine = hosted(z, u)
    return blk, u, z, c, is_host, mine


def collect(
    q_in, k_in, v_in, g_in, mask_in, order_ref, kv, qg, picked,
    mask, passing, in_send, kv_sem, qg_sem, kv_send, kv_recv, qg_send, qg_recv,
    mask_sem, pass_sem, pass_send,
):
    blk, u, z, c, is_host, mine = place()
    sibling = (2 * z + 1 - c, u)
    via = beside(u)
    served = (via[2], via[1], via[0])
    barrier = pltpu.get_barrier_semaphore()
    get_mask = pltpu.make_async_copy(mask_in, mask, mask_sem)

    def greet(there):
        pl.semaphore_signal(barrier, inc=1, device_id=there, device_id_type=MESH)

    @pl.when(is_host)
    def _():
        get_mask.start()

        def greet_line(r, carry):
            greet((2 * lax.rem(z + r, NZ) + c, u))
            return carry

        lax.fori_loop(1, NZ, greet_line, 0)
        greet(sibling)

    for line in served:
        greet((blk, line))

    pl.semaphore_wait(barrier, 6)

    def inputs(l):
        host = lax.rem(lift(u) + 3 * l, NZ)
        r = lax.rem(z - host + NZ, NZ)
        cols = pl.ds(pl.multiple_of(l * DH, DH), DH)
        home = [
            (src.at[:, cols], dst, sem)
            for src, dst, sem in (
                (k_in, kv.at[1, r, 0], kv_sem.at[r]),
                (v_in, kv.at[1, r, 1], kv_sem.at[r]),
                (q_in, qg.at[1, r, 0], qg_sem.at[r]),
                (g_in, qg.at[1, r, 1], qg_sem.at[r]),
            )
        ]
        away = [(*home[0][:2], in_send, home[0][2], (2 * host + c, u))] + [
            (home[n + 1][0], passing.at[n, l], in_send, pass_sem.at[n, l], (blk, via[n]))
            for n in range(3)
        ]
        return host, home, away

    def nth(n, line):
        return lax.rem(z + line + n, 3)

    for part in (slice(0, 2), slice(2, 4)):
        for n in range(3):
            host, home, away = inputs(nth(n, u))

            @pl.when(host != z)
            def _():
                for move in away[part]:
                    remote(*move).start()

            @pl.when(host == z)
            def _():
                for move in home[part]:
                    pltpu.make_async_copy(*move).start()

    @pl.when(is_host)
    def _():
        row = lax.broadcasted_iota(jnp.int32, (16, 16), 0)
        lane = lax.broadcasted_iota(jnp.int32, (16, 16), 1)
        ident = jnp.zeros((16, 16), jnp.int32)
        for j in range(16):
            side = c if j // NZ else 1 - c
            ident = jnp.where(row == j, order_ref[2 * lax.rem(z + j % NZ, NZ) + side], ident)
        hot = jnp.where(lane == ident, 1.0, 0.0).astype(BF16)
        wide = lax.broadcasted_iota(jnp.int32, (16, 128), 1)
        hot_wide = jnp.where(wide == ident[:, :1], 1.0, 0.0).astype(BF16)
        get_mask.wait()
        flat = jnp.where(mask[...] > 0, 1.0, 0.0).reshape(256, H).astype(BF16)
        head = lax.broadcasted_iota(jnp.int32, (H, 128), 0) == 3 * u + mine
        picked_out = nn(flat, jnp.where(head, 1.0, 0.0).astype(BF16))
        tall = lax.broadcasted_iota(jnp.int32, (16, 16, 128), 1)
        across = lax.broadcasted_iota(jnp.int32, (16, 16, 128), 2)
        table = jnp.where(tall == across, picked_out.reshape(16, 16, 128), 0.0)
        table = jnp.sum(table, axis=1).astype(BF16)
        by_query = nn(hot, table).astype(BF16)
        allowed = nt(by_query, hot_wide)
        one_side = lax.div(row, NZ) == lax.div(lane, NZ)
        before = jnp.where(jnp.logical_and(row < lane, one_side), 1.0, 0.0).astype(BF16)
        rank = nn(allowed.astype(BF16), before)
        near = jnp.where(lane >= NZ, allowed, 0.0)
        far = jnp.where(lane >= NZ, 0.0, allowed)
        listed = jnp.where(wide == COUNT, jnp.sum(near, axis=1, keepdims=True), 0.0)
        ends = SECOND + jnp.sum(far, axis=1, keepdims=True)
        listed = jnp.where(wide == COUNT + 1, ends, listed)
        for first, some in ((0, near), (SECOND, far)):
            for n in range(NZ):
                here = jnp.logical_and(some > 0.5, jnp.abs(rank - n) < 0.5)
                one = jnp.sum(jnp.where(here, lane.astype(F32), 0.0), axis=1, keepdims=True)
                listed = jnp.where(wide == first + n, one, listed)
        picked[...] = listed.astype(jnp.int32)

    def passed(n, l):
        host = lax.rem(lift(served[n]) + 3 * l, NZ)
        r = lax.rem(z - host + NZ, NZ)
        dst, sem = (
            (kv.at[1, r, 1], kv_sem.at[r]),
            (qg.at[1, r, 0], qg_sem.at[r]),
            (qg.at[1, r, 1], qg_sem.at[r]),
        )[n]
        there = (2 * host + c, served[n])
        return host != z, remote(passing.at[n, l], dst, pass_send.at[n, l], sem, there)

    for part in ((0,), (1, 2)):
        for i in range(3):
            for n in part:
                l = nth(i, served[n])
                on, move = passed(n, l)

                @pl.when(on)
                def _():
                    arrived(passing.at[n, l], pass_sem.at[n, l])
                    move.start()

    @pl.when(is_host)
    def _():
        for ref, sems, send, recv in (
            (kv, kv_sem, kv_send, kv_recv), (qg, qg_sem, qg_send, qg_recv)
        ):

            def share(n, carry, ref=ref, sems=sems, send=send, recv=recv):
                odd = lax.rem(n, 2)
                r = lax.rem(odd * lax.div(n + 1, 2) + (1 - odd) * (NZ - lax.div(n, 2)), NZ)
                arrived(ref.at[1, r], sems.at[r])
                remote(ref.at[1, r], ref.at[0, r], send, recv, sibling).start()
                return carry

            lax.fori_loop(0, NZ, share, 0)
        for ref, send, recv in ((kv, kv_send, kv_recv), (qg, qg_send, qg_recv)):
            arrived(ref.at[0], recv)
            arrived(ref.at[1], send)
        arrived(kv.at[0, pl.ds(0, 4)], in_send)

    @pl.when(jnp.logical_not(is_host))
    def _():
        arrived(kv.at[0, pl.ds(0, 6)], in_send)

    for l in range(3):
        for n in range(3):
            on, move = passed(n, l)
            pl.when(on)(move.wait_send)


def gradients(
    kv, qg, picked_in, dq_out, acc,
    picked, item_code, e_buf, d_buf, top_buf, row_top, row_sum, row_mix, dq_acc, sem,
):
    blk, u, z, c, is_host, mine = place()

    @pl.when(is_host)
    def _():
        get = pltpu.make_async_copy(picked_in, picked, sem)
        get.start()
        acc[NZ:] = jnp.zeros((NZ, 2, 128, 128), F32)
        dq_acc[NZ:] = jnp.zeros((NZ, 128, 128), F32)
        row_top[...] = jnp.full_like(row_top, -1e30)
        row_sum[...] = jnp.zeros_like(row_sum)
        row_mix[...] = jnp.zeros_like(row_mix)
        get.wait()

        def listing(rows, first, end, items):
            for r in rows:
                stop = picked[r, end]
                for base in range(first, first + NZ, SLOTS):
                    item_code[items] = r * 4096 + base * 64 + stop
                    items = items + (base < stop).astype(jnp.int32)
            return items

        def item(i):
            code = item_code[i]
            return lax.shift_right_logical(code, 12), lax.bitwise_and(lax.shift_right_logical(code, 6), 63), lax.bitwise_and(code, 63)

        own, other = range(NZ, 16), range(NZ)
        items = listing(own, 0, COUNT, jnp.int32(0))
        items = listing(other, 0, COUNT, items)
        needed = listing(own, SECOND, COUNT + 1, items)
        items = listing(other, SECOND, COUNT + 1, needed)
        for m in range(WIDE - 1):
            item_code[items + m] = EMPTY * 64

        def tiles(ref, r, base, part):
            return jnp.concatenate(
                [ref[picked[r, base + m], part] for m in range(SLOTS)], axis=0
            )

        def weigh(t, carry):
            for w in range(WIDE):
                i = t * WIDE + w
                r, base, end = item(i)
                scores = nt(tiles(kv, r, base, 0), qg[r, 0]) * (FACTOR * LOG2E)
                scores = jnp.concatenate(
                    [
                        scores[128 * m:128 * m + 128]
                        + jnp.where(base + m < end, 0.0, -1e30)
                        for m in range(SLOTS)
                    ],
                    axis=0,
                )
                top = jnp.max(scores, axis=0, keepdims=True)
                e = jnp.exp2(scores - top)
                dprob = nt(tiles(kv, r, base, 1), qg[r, 1])
                e_buf[i] = e
                d_buf[i] = dprob
                top_buf[i] = top
                total = jnp.sum(e, axis=0, keepdims=True)
                mixed = jnp.sum(e * dprob, axis=0, keepdims=True)
                old = row_top[r]
                new = jnp.maximum(old, top)
                keep = jnp.exp2(old - new)
                part = jnp.exp2(top - new)
                row_top[r] = new
                row_sum[r] = row_sum[r] * keep + total * part
                row_mix[r] = row_mix[r] * keep + mixed * part
            return carry

        lax.fori_loop(0, lax.div(items + WIDE - 1, WIDE), weigh, 0)

        def spread(t, carry):
            for w in range(WIDE):
                i = t * WIDE + w
                r, base, _ = item(i)
                whole = 1.0 / row_sum[r]
                prob = e_buf[i] * (jnp.exp2(top_buf[i] - row_top[r]) * whole)
                dscore = (prob * (d_buf[i] - row_mix[r] * whole)).astype(BF16)
                dk = nn(dscore, qg[r, 0])
                dv = nn(prob.astype(BF16), qg[r, 1])
                dq_acc[r] += lax.dot_general(
                    dscore, tiles(kv, r, base, 0), (((0,), (0,)), ((), ())),
                    preferred_element_type=F32,
                )
                for m in range(SLOTS):
                    j = picked[r, base + m]
                    acc[j, 0] += dk[128 * m:128 * m + 128]
                    acc[j, 1] += dv[128 * m:128 * m + 128]
            return carry

        lax.fori_loop(0, lax.div(needed + WIDE - 1, WIDE), spread, 0)
        dq_out[...] = (dq_acc[NZ:] * FACTOR).astype(BF16)


def give_back(
    dq_in, acc, f_q, f_kv, kv_out, r_q, r_kv, t_q,
    p1q_send, p1k_send, rq_sem, rkv_sem, p2q_send, p2k_send, fq_sem, fkv_sem, others,
):
    blk, u, z, c, is_host, mine = place()
    seat = mine * 2 + lax.rem(lax.div(u, 4), 2)
    rest = jnp.logical_not(is_host)
    barrier = pltpu.get_barrier_semaphore()

    def greet(there, other):
        @pl.when(jnp.logical_or(rest, jnp.logical_not(other)))
        def _():
            pl.semaphore_signal(barrier, inc=1, device_id=there, device_id_type=MESH)

    def greet_line(r, carry):
        h = lax.rem(z + r, NZ)
        greet((2 * h + c, u), hosted(h, u)[0])
        return carry

    def greet_plane(n, carry):
        to = lax.rem(u + n, NU)
        greet((blk, to), hosted(z, to)[0])
        return carry

    lax.fori_loop(1, NZ, greet_line, 0)
    lax.fori_loop(1, NU, greet_plane, 0)

    pl.semaphore_wait(barrier, 22 - 7 * is_host.astype(jnp.int32))

    def tell(there):
        pl.semaphore_signal(others, inc=1, device_id=there, device_id_type=MESH)

    @pl.when(rest)
    def _():
        below = lax.rem(z + NZ - 1, NZ)
        right, _, left = beside(u)
        left_hosts, left_head = hosted(z, left)
        right_hosts, right_head = hosted(z, right)
        pl.when(hosted(below, u)[0])(functools.partial(tell, (2 * below + c, u)))
        on = jnp.logical_and(left_hosts, left_head > 0)
        pl.when(on)(functools.partial(tell, (blk, left)))
        on = jnp.logical_and(right_hosts, right_head == 0)
        pl.when(on)(functools.partial(tell, (blk, right)))

    @pl.when(is_host)
    def _():
        def stage(h, carry):
            r = lax.rem(h - z + NZ, NZ)
            dk = acc[NZ + r, 0] * FACTOR
            dv = acc[NZ + r, 1]
            for n in range(NU):
                piece = jnp.concatenate([dk[8 * n:8 * n + 8], dv[8 * n:8 * n + 8]], axis=0)
                kv_out[n, h] = piece.astype(BF16)
            return carry

        def send_k(part, to_hosts):
            heights = pl.ds(4 * part, 4)

            def one(n, carry):
                to = lax.rem(u + n, NU)

                @pl.when(hosted(z, to)[0] == to_hosts)
                def _():
                    remote(
                        kv_out.at[to, heights], r_kv.at[seat, heights],
                        p1k_send, rkv_sem.at[part], (blk, to),
                    ).start()

                return carry

            lax.fori_loop(1, NU, one, 0)

        def send_q(to_hosts):
            def one(h, carry):
                on = jnp.logical_and(h != z, hosted(h, u)[0] == to_hosts)

                @pl.when(on)
                def _():
                    tile = dq_in.at[lax.rem(h - z + NZ, NZ)]
                    remote(tile, r_q.at[mine], p1q_send, rq_sem, (2 * h + c, u)).start()

                return carry

            lax.fori_loop(0, NZ, one, 0)

        send_q(False)
        pltpu.make_async_copy(dq_in.at[0], r_q.at[mine], rq_sem).start()
        for part in range(2):
            lax.fori_loop(4 * part, 4 * part + 4, stage, 0)
            send_k(part, False)
            heights = pl.ds(4 * part, 4)
            pltpu.make_async_copy(
                kv_out.at[u, heights], r_kv.at[seat, heights], rkv_sem.at[part]
            ).start()
        pl.semaphore_wait(others, 2)
        send_q(True)
        send_k(0, True)
        send_k(1, True)

    arrived(r_q, rq_sem)
    heads = [r_q[l].astype(F32) for l in range(3)]
    for i in range(NU):
        rows = slice(8 * i, 8 * i + 8)
        t_q[i, :16] = jnp.concatenate([heads[0][rows], heads[1][rows]], axis=0).astype(BF16)
        t_q[i, 16:] = jnp.concatenate([heads[2][rows], heads[2][rows]], axis=0).astype(BF16)

    def pass_q(i, carry):
        to = lax.rem(u + i, NU)
        remote(t_q.at[to], f_q.at[u], p2q_send, fq_sem, (blk, to)).start()
        return carry

    lax.fori_loop(1, NU, pass_q, 0)
    pltpu.make_async_copy(t_q.at[u], f_q.at[u], fq_sem).start()

    def pass_k(h, carry):
        @pl.when(h != z)
        def _():
            remote(r_kv.at[:, h], f_kv.at[z], p2k_send, fkv_sem, (2 * h + c, u)).start()

        @pl.when(h == z)
        def _():
            pltpu.make_async_copy(r_kv.at[:, h], f_kv.at[z], fkv_sem).start()

        return carry

    for part in range(2):
        arrived(r_kv.at[:, pl.ds(4 * part, 4)], rkv_sem.at[part])
        lax.fori_loop(4 * part, 4 * part + 4, pass_k, 0)

    @pl.when(is_host)
    def _():
        arrived(dq_in.at[pl.ds(0, NZ - 1)], p1q_send)
        arrived(kv_out.at[pl.ds(0, NU - 1)], p1k_send)

    arrived(r_kv.at[:, pl.ds(0, NZ - 1)], p2k_send)
    arrived(t_q.at[pl.ds(0, NU - 1)], p2q_send)
    arrived(f_q, fq_sem)
    arrived(f_kv, fkv_sem)


def assemble(f_q, f_kv, q_hbm, k_hbm, v_hbm, out_q, out_k, out_v, sems):
    def columns(head):
        return slice(head * DH, head * DH + DH)

    copies = [
        pltpu.make_async_copy(src, dst, sems.at[n])
        for n, (src, dst) in enumerate(((out_q, q_hbm), (out_k, k_hbm), (out_v, v_hbm)))
    ]
    for n in range(NU):
        first = f_q[n, :16].astype(F32)
        out_q[:, columns(3 * n)] = first[:8].astype(BF16)
        out_q[:, columns(3 * n + 1)] = first[8:].astype(BF16)
        out_q[:, columns(3 * n + 2)] = f_q[n, 16:].astype(F32)[:8].astype(BF16)
    copies[0].start()
    for d in range(NZ):
        for l in range(3):
            for half in range(2):
                both = f_kv[d, 2 * l + half].astype(F32)
                up = (d - 3 * l) % NZ
                x = (up - up % 2 - 4 * half) % NZ // 2
                head = 3 * (4 * (2 * (up % 2) + half) + x) + l
                out_k[:, columns(head)] = both[:8].astype(BF16)
                out_v[:, columns(head)] = both[8:].astype(BF16)
    copies[1].start()
    copies[2].start()
    for copy in copies:
        copy.wait()


def local(query, key, value, grad_out, tile_mask, tile_order):
    anywhere = pl.BlockSpec(memory_space=pl.ANY)
    vmem = pl.BlockSpec(memory_space=pltpu.VMEM)
    smem = pl.BlockSpec(memory_space=pltpu.SMEM)
    dma = pltpu.SemaphoreType.DMA
    shape = jax.ShapeDtypeStruct
    most = 16 * 16 // SLOTS + WIDE
    operands = (query, key, value, grad_out, jnp.transpose(tile_mask, (1, 2, 0)), tile_order)
    kv, qg, picked = pl.pallas_call(
        collect,
        out_shape=(
            shape((2, NZ, 2, 128, 128), BF16),
            shape((2, NZ, 2, 128, 128), BF16),
            shape((16, 128), jnp.int32),
        ),
        in_specs=[anywhere] * 5 + [smem],
        out_specs=(vmem, vmem, vmem),
        scratch_shapes=[
            pltpu.VMEM((16, 16, H), jnp.int32),
            pltpu.VMEM((3, 3, 128, 128), BF16),
            dma, dma((NZ,)), dma((NZ,)), dma, dma, dma, dma, dma, dma((3, 3)), dma((3, 3)),
        ],
        compiler_params=pltpu.CompilerParams(
            collective_id=0, has_side_effects=True, vmem_limit_bytes=16 * 1024 * 1024
        ),
    )(*[pltpu.with_memory_space_constraint(a, pltpu.HBM) for a in operands])
    dq, acc = pl.pallas_call(
        gradients,
        out_shape=(
            shape((NZ, 128, 128), BF16),
            shape((16, 2, 128, 128), F32),
        ),
        in_specs=[vmem, vmem, anywhere],
        out_specs=(vmem, vmem),
        scratch_shapes=[
            pltpu.SMEM((16, 128), jnp.int32),
            pltpu.SMEM((most,), jnp.int32),
            pltpu.VMEM((most, 128 * SLOTS, 128), F32),
            pltpu.VMEM((most, 128 * SLOTS, 128), F32),
            pltpu.VMEM((most, 1, 128), F32),
            pltpu.VMEM((16, 1, 128), F32),
            pltpu.VMEM((16, 1, 128), F32),
            pltpu.VMEM((16, 1, 128), F32),
            pltpu.VMEM((16, 128, 128), F32),
            dma,
        ],
        compiler_params=pltpu.CompilerParams(vmem_limit_bytes=48 * 1024 * 1024),
    )(kv.reshape(16, 2, 128, 128), qg.reshape(16, 2, 128, 128), picked)
    f_q, f_kv = pl.pallas_call(
        give_back,
        out_shape=(shape((NU, 32, 128), BF16), shape((NZ, 6, 16, 128), BF16)),
        in_specs=[vmem] * 2,
        out_specs=(vmem, vmem),
        scratch_shapes=[
            pltpu.VMEM((NU, NZ, 16, 128), BF16),
            pltpu.VMEM((3, 128, 128), BF16),
            pltpu.VMEM((6, NZ, 16, 128), BF16),
            pltpu.VMEM((NU, 32, 128), BF16),
            dma, dma, dma, dma((2,)), dma, dma, dma, dma,
            pltpu.SemaphoreType.REGULAR,
        ],
        compiler_params=pltpu.CompilerParams(
            collective_id=1, has_side_effects=True, vmem_limit_bytes=16 * 1024 * 1024
        ),
    )(dq, acc)
    out = shape((8, H * DH), BF16)
    return pl.pallas_call(
        assemble,
        out_shape=(out, out, out),
        in_specs=[vmem] * 2,
        out_specs=(anywhere, anywhere, anywhere),
        scratch_shapes=[pltpu.VMEM((8, H * DH), BF16)] * 3 + [dma((3,))],
        compiler_params=pltpu.CompilerParams(vmem_limit_bytes=8 * 1024 * 1024),
    )(*[pltpu.with_memory_space_constraint(a, pltpu.VMEM) for a in (f_q, f_kv)])


def solution(mesh):
    placed = (P("blk", "uly"), P("blk", "uly"), P("blk", "uly"), P("blk", "uly"), P(), P())
    return jax.shard_map(
        local,
        mesh=mesh,
        in_specs=placed,
        out_specs=(P(("blk", "uly"), None), P(("blk", "uly"), None), P(("blk", "uly"), None)),
        check_vma=False,
    )
```

```python
import functools

import jax
import jax.numpy as jnp
from jax import lax
from jax.experimental import pallas as pl
from jax.experimental.pallas import tpu as pltpu
from jax.sharding import PartitionSpec as P

H = 48
DH = 128
TILE = 128
NZ = 8
NU = 16
SLOTS = 1
WIDE = 8
COUNT = 32
EMPTY = 40
MESH = pl.DeviceIdType.MESH
FACTOR = DH ** -0.5
LOG2E = 1.4426950408889634
F32 = jnp.float32
BF16 = jnp.bfloat16


def nt(a, b):
    return lax.dot_general(a, b, (((1,), (1,)), ((), ())), preferred_element_type=F32)


def nn(a, b):
    return lax.dot_general(a, b, (((1,), (0,)), ((), ())), preferred_element_type=F32)


def lift(u):
    x, y = lax.rem(u, 4), lax.div(u, 4)
    return lax.rem(2 * x + 4 * lax.rem(y, 2) + lax.div(y, 2), NZ)


def beside(u):
    x, y = lax.rem(u, 4), lax.div(u, 4)
    other = y + 1 - 2 * lax.rem(y, 2)
    return 4 * y + lax.rem(x + 1, 4), 4 * other + x, 4 * y + lax.rem(x + 3, 4)


def hosted(z, u):
    rel = lax.rem(z - lift(u) + NZ, NZ)
    yes = jnp.logical_or(rel == 0, jnp.logical_or(rel == 3, rel == 6))
    return yes, lax.div(rel, 3)


def remote(src, dst, send, recv, there):
    return pltpu.make_async_remote_copy(
        src_ref=src, dst_ref=dst, send_sem=send, recv_sem=recv,
        device_id=there, device_id_type=MESH,
    )


def arrived(ref, sem):
    pltpu.make_async_copy(ref, ref, sem).wait()


def place():
    blk = lax.axis_index("blk")
    u = lax.axis_index("uly")
    z = lax.div(blk, 2)
    c = lax.rem(blk, 2)
    yes, mine = hosted(z, u)
    return blk, u, z, c, jnp.logical_and(yes, c == lax.rem(mine, 2)), mine


def collect(
    q_in, k_in, v_in, g_in, mask_in, order_ref, kv, qg, picked,
    mask, passing, in_send, kv_sem, qg_sem, mask_sem, pass_sem, pass_send,
):
    blk, u, z, c, is_host, mine = place()
    via = beside(u)
    served = (via[2], via[1], via[0])
    barrier = pltpu.get_barrier_semaphore()

    def greet(there):
        pl.semaphore_signal(barrier, inc=1, device_id=there, device_id_type=MESH)

    get_mask = pltpu.make_async_copy(mask_in, mask, mask_sem)

    @pl.when(is_host)
    def _():
        get_mask.start()

        def greet_line(n, carry):
            greet((lax.rem(blk + n, 2 * NZ), u))
            return carry

        lax.fori_loop(1, 2 * NZ, greet_line, 0)

    for line in served:
        greet((blk, line))

    pl.semaphore_wait(barrier, 3 + 3 - is_host.astype(jnp.int32))

    def inputs(l):
        host = lax.rem(lift(u) + 3 * l, NZ)
        r = lax.rem(z - host + NZ, NZ)
        cols = pl.ds(pl.multiple_of(l * DH, DH), DH)
        there = (2 * host + lax.rem(l, 2), u)
        home = (
            (k_in, kv.at[c, r, 0], kv_sem),
            (v_in, kv.at[c, r, 1], kv_sem),
            (q_in, qg.at[c, r, 0], qg_sem),
            (g_in, qg.at[c, r, 1], qg_sem),
        )
        home = [(src.at[:, cols], dst, sem) for src, dst, sem in home]
        straight = [(src, dst, in_send, sem, there) for src, dst, sem in home]
        around = [
            (home[n + 1][0], passing.at[n, l], in_send, pass_sem.at[n, l], (blk, via[n]))
            for n in range(3)
        ] + straight[:1]
        return host, home, straight, around

    def nth(n, line):
        return lax.rem(z + line + n, 3)

    for n in range(3):
        l = nth(n, u)
        host, home, straight, around = inputs(l)

        @pl.when(host != z)
        def _():
            for move in around:
                remote(*move).start()

        @pl.when(jnp.logical_and(host == z, c != lax.rem(l, 2)))
        def _():
            for move in straight:
                remote(*move).start()

        @pl.when(jnp.logical_and(host == z, c == lax.rem(l, 2)))
        def _():
            for move in home:
                pltpu.make_async_copy(*move).start()

    @pl.when(is_host)
    def _():
        row = lax.broadcasted_iota(jnp.int32, (16, 16), 0)
        lane = lax.broadcasted_iota(jnp.int32, (16, 16), 1)
        ident = jnp.zeros((16, 16), jnp.int32)
        for j in range(16):
            ident = jnp.where(row == j, order_ref[2 * lax.rem(z + j % NZ, NZ) + j // NZ], ident)
        hot = jnp.where(lane == ident, 1.0, 0.0).astype(BF16)
        wide = lax.broadcasted_iota(jnp.int32, (16, 128), 1)
        hot_wide = jnp.where(wide == ident[:, :1], 1.0, 0.0).astype(BF16)
        get_mask.wait()
        flat = jnp.where(mask[...] > 0, 1.0, 0.0).reshape(256, H).astype(BF16)
        head = lax.broadcasted_iota(jnp.int32, (H, 128), 0) == 3 * u + mine
        picked_out = nn(flat, jnp.where(head, 1.0, 0.0).astype(BF16))
        tall = lax.broadcasted_iota(jnp.int32, (16, 16, 128), 1)
        across = lax.broadcasted_iota(jnp.int32, (16, 16, 128), 2)
        table = jnp.where(tall == across, picked_out.reshape(16, 16, 128), 0.0)
        table = jnp.sum(table, axis=1).astype(BF16)
        by_query = nn(hot, table).astype(BF16)
        allowed = nt(by_query, hot_wide)
        before = jnp.where(row < lane, 1.0, 0.0).astype(BF16)
        rank = nn(allowed.astype(BF16), before)
        listed = jnp.where(wide == COUNT, jnp.sum(allowed, axis=1, keepdims=True), 0.0)
        for n in range(16):
            here = jnp.logical_and(allowed > 0.5, jnp.abs(rank - n) < 0.5)
            one = jnp.sum(jnp.where(here, lane.astype(F32), 0.0), axis=1, keepdims=True)
            listed = jnp.where(wide == n, one, listed)
        picked[...] = listed.astype(jnp.int32)

    def passed(n, l):
        host = lax.rem(lift(served[n]) + 3 * l, NZ)
        r = lax.rem(z - host + NZ, NZ)
        dst, sem = (
            (kv.at[c, r, 1], kv_sem),
            (qg.at[c, r, 0], qg_sem),
            (qg.at[c, r, 1], qg_sem),
        )[n]
        there = (2 * host + lax.rem(l, 2), served[n])
        return host != z, remote(passing.at[n, l], dst, pass_send.at[n, l], sem, there)

    for i in range(3):
        for n in range(3):
            l = nth(i, served[n])
            on, move = passed(n, l)

            @pl.when(on)
            def _():
                arrived(passing.at[n, l], pass_sem.at[n, l])
                move.start()

    @pl.when(is_host)
    def _():
        arrived(kv, kv_sem)
        arrived(qg, qg_sem)
        arrived(kv.at[0, pl.ds(0, 4)], in_send)

    @pl.when(jnp.logical_not(is_host))
    def _():
        arrived(kv.at[0, pl.ds(0, 6)], in_send)

    for l in range(3):
        for n in range(3):
            on, move = passed(n, l)
            pl.when(on)(move.wait_send)


def gradients(
    kv, qg, picked_in, dq_out, acc,
    picked, item_code, e_buf, d_buf, top_buf, row_top, row_sum, row_mix, dq_acc, sem,
):
    blk, u, z, c, is_host, mine = place()

    @pl.when(is_host)
    def _():
        get = pltpu.make_async_copy(picked_in, picked, sem)
        get.start()
        acc[...] = jnp.zeros_like(acc)
        dq_acc[...] = jnp.zeros_like(dq_acc)
        row_top[...] = jnp.full_like(row_top, -1e30)
        row_sum[...] = jnp.zeros_like(row_sum)
        row_mix[...] = jnp.zeros_like(row_mix)
        get.wait()

        items = jnp.int32(0)
        for r in range(16):
            end = picked[r, COUNT]
            for base in range(0, 16, SLOTS):
                item_code[items] = r * 4096 + base * 64 + end
                items = items + (base < end).astype(jnp.int32)
        for m in range(WIDE - 1):
            item_code[items + m] = EMPTY * 64
        rounds = lax.div(items + WIDE - 1, WIDE)

        def item(i):
            code = item_code[i]
            base = lax.bitwise_and(lax.shift_right_logical(code, 6), 63)
            return lax.shift_right_logical(code, 12), base, lax.bitwise_and(code, 63)

        def tiles(ref, r, base, part):
            return jnp.concatenate(
                [ref[picked[r, base + m], part] for m in range(SLOTS)], axis=0
            )

        def weigh(t, carry):
            for w in range(WIDE):
                i = t * WIDE + w
                r, base, end = item(i)
                scores = nt(tiles(kv, r, base, 0), qg[r, 0]) * (FACTOR * LOG2E)
                scores = jnp.concatenate(
                    [
                        scores[128 * m:128 * m + 128]
                        + jnp.where(base + m < end, 0.0, -1e30)
                        for m in range(SLOTS)
                    ],
                    axis=0,
                )
                top = jnp.max(scores, axis=0, keepdims=True)
                e = jnp.exp2(scores - top)
                dprob = nt(tiles(kv, r, base, 1), qg[r, 1])
                e_buf[i] = e
                d_buf[i] = dprob
                top_buf[i] = top
                total = jnp.sum(e, axis=0, keepdims=True)
                mixed = jnp.sum(e * dprob, axis=0, keepdims=True)
                old = row_top[r]
                new = jnp.maximum(old, top)
                keep = jnp.exp2(old - new)
                part = jnp.exp2(top - new)
                row_top[r] = new
                row_sum[r] = row_sum[r] * keep + total * part
                row_mix[r] = row_mix[r] * keep + mixed * part
            return carry

        lax.fori_loop(0, rounds, weigh, 0)

        def spread(t, carry):
            for w in range(WIDE):
                i = t * WIDE + w
                r, base, _ = item(i)
                whole = 1.0 / row_sum[r]
                prob = e_buf[i] * (jnp.exp2(top_buf[i] - row_top[r]) * whole)
                dscore = (prob * (d_buf[i] - row_mix[r] * whole)).astype(BF16)
                dk = nn(dscore, qg[r, 0])
                dv = nn(prob.astype(BF16), qg[r, 1])
                dq_acc[r] += lax.dot_general(
                    dscore, tiles(kv, r, base, 0), (((0,), (0,)), ((), ())),
                    preferred_element_type=F32,
                )
                for m in range(SLOTS):
                    j = picked[r, base + m]
                    acc[j, 0] += dk[128 * m:128 * m + 128]
                    acc[j, 1] += dv[128 * m:128 * m + 128]
            return carry

        lax.fori_loop(0, rounds, spread, 0)
        dq_out[...] = (dq_acc[...] * FACTOR).astype(BF16)


def give_back(
    dq_in, acc, f_q, f_kv, kv_out, r_q, r_kv, t_q,
    p1q_send, p1k_send, rq_sem, rkv_sem, p2q_send, p2k_send, fq_sem, fkv_sem,
):
    blk, u, z, c, is_host, mine = place()
    seat = mine * 2 + lax.rem(lax.div(u, 4), 2)
    chip_hosts = hosted(z, u)[0]
    passes = [
        jnp.logical_and(jnp.logical_not(is_host), jnp.logical_or(chip_hosts, c == side))
        for side in range(2)
    ]
    barrier = pltpu.get_barrier_semaphore()

    def passer(h, line, side):
        yes, l = hosted(h, line)
        return 2 * h + jnp.where(yes, 1 - lax.rem(l, 2), side), line

    def greet(there):
        @pl.when(jnp.logical_or(there[0] != blk, there[1] != u))
        def _():
            pl.semaphore_signal(barrier, inc=1, device_id=there, device_id_type=MESH)

    def greet_line(h, carry):
        greet(passer(h, u, c))
        return carry

    def greet_plane(n, carry):
        greet(passer(z, lax.rem(u + n, NU), c))
        return carry

    lax.fori_loop(0, NZ, greet_line, 0)
    lax.fori_loop(0, NU, greet_plane, 0)

    @pl.when(jnp.logical_not(is_host))
    def _():
        for l in range(3):
            greet((2 * lax.rem(lift(u) + 3 * l, NZ) + l % 2, u))
            up = lax.rem(z - 3 * l + 2 * NZ, NZ)
            for half in range(2):
                x = lax.div(lax.rem(up - lax.rem(up, 2) - 4 * half + NZ, NZ), 2)
                greet((2 * z + l % 2, 4 * (2 * lax.rem(up, 2) + half) + x))

    alone = jnp.logical_not(chip_hosts).astype(jnp.int32)
    pl.semaphore_wait(barrier, jnp.where(is_host, 39, 22 + 24 * (1 - alone)))

    @pl.when(is_host)
    def _():
        def stage(h, carry):
            for side in range(2):
                j = NZ * side + lax.rem(h - z + NZ, NZ)
                dk = acc[j, 0] * FACTOR
                dv = acc[j, 1]
                for n in range(NU):
                    piece = jnp.concatenate([dk[8 * n:8 * n + 8], dv[8 * n:8 * n + 8]], axis=0)
                    kv_out[NU * side + n, h] = piece.astype(BF16)
            return carry

        def send_q(h, carry):
            for side in range(2):
                tile = dq_in.at[NZ * side + lax.rem(h - z + NZ, NZ)]
                there = passer(h, u, side)
                remote(tile, r_q.at[side, mine], p1q_send, rq_sem.at[side], there).start()
            return carry

        lax.fori_loop(0, NZ, send_q, 0)
        for part in range(2):
            heights = pl.ds(4 * part, 4)

            def send_k(n, carry):
                to = lax.rem(u + n, NU)
                for side in range(2):
                    remote(
                        kv_out.at[NU * side + to, heights], r_kv.at[side, seat, heights],
                        p1k_send, rkv_sem.at[part, side], passer(z, to, side),
                    ).start()
                return carry

            lax.fori_loop(4 * part, 4 * part + 4, stage, 0)
            lax.fori_loop(0, NU, send_k, 0)

    def pass_q(side):
        arrived(r_q.at[side], rq_sem.at[side])
        heads = [r_q[side, l].astype(F32) for l in range(3)]
        for n in range(NU):
            rows = slice(8 * n, 8 * n + 8)
            both = jnp.concatenate([heads[0][rows], heads[1][rows]], axis=0)
            t_q[side, n, :16] = both.astype(BF16)
            both = jnp.concatenate([heads[2][rows], heads[2][rows]], axis=0)
            t_q[side, n, 16:] = both.astype(BF16)

        def one(n, carry):
            to = lax.rem(u + n, NU)
            there = (2 * z + side, to)
            remote(t_q.at[side, to], f_q.at[u], p2q_send.at[side], fq_sem, there).start()
            return carry

        lax.fori_loop(1, NU, one, 0)

        @pl.when(c != side)
        def _():
            one(0, 0)

        @pl.when(c == side)
        def _():
            pltpu.make_async_copy(t_q.at[side, u], f_q.at[u], fq_sem).start()

    def pass_k(part, side):
        arrived(r_kv.at[side, :, pl.ds(4 * part, 4)], rkv_sem.at[part, side])

        def one(h, carry):
            src = r_kv.at[side, :, h]

            @pl.when(jnp.logical_or(h != z, c != side))
            def _():
                there = (2 * h + side, u)
                remote(src, f_kv.at[z], p2k_send.at[side], fkv_sem, there).start()

            @pl.when(jnp.logical_and(h == z, c == side))
            def _():
                pltpu.make_async_copy(src, f_kv.at[z], fkv_sem).start()

            return carry

        lax.fori_loop(4 * part, 4 * part + 4, one, 0)

    for side in range(2):
        pl.when(passes[side])(functools.partial(pass_q, side))
    for part in range(2):
        for side in range(2):
            pl.when(passes[side])(functools.partial(pass_k, part, side))

    @pl.when(is_host)
    def _():
        arrived(dq_in, p1q_send)
        arrived(kv_out, p1k_send)

    for side in range(2):

        @pl.when(jnp.logical_and(passes[side], c == side))
        def _():
            arrived(t_q.at[side, pl.ds(0, NU - 1)], p2q_send.at[side])
            arrived(r_kv.at[side, :, pl.ds(0, NZ - 1)], p2k_send.at[side])

        @pl.when(jnp.logical_and(passes[side], c != side))
        def _():
            arrived(t_q.at[side], p2q_send.at[side])
            arrived(r_kv.at[side], p2k_send.at[side])

    arrived(f_q, fq_sem)
    arrived(f_kv, fkv_sem)


def assemble(f_q, f_kv, q_hbm, k_hbm, v_hbm, out_q, out_k, out_v, sems):
    def columns(head):
        return slice(head * DH, head * DH + DH)

    copies = [
        pltpu.make_async_copy(src, dst, sems.at[n])
        for n, (src, dst) in enumerate(((out_q, q_hbm), (out_k, k_hbm), (out_v, v_hbm)))
    ]
    for n in range(NU):
        first = f_q[n, :16].astype(F32)
        out_q[:, columns(3 * n)] = first[:8].astype(BF16)
        out_q[:, columns(3 * n + 1)] = first[8:].astype(BF16)
        out_q[:, columns(3 * n + 2)] = f_q[n, 16:].astype(F32)[:8].astype(BF16)
    copies[0].start()
    for d in range(NZ):
        for l in range(3):
            for half in range(2):
                both = f_kv[d, 2 * l + half].astype(F32)
                up = (d - 3 * l) % NZ
                x = (up - up % 2 - 4 * half) % NZ // 2
                head = 3 * (4 * (2 * (up % 2) + half) + x) + l
                out_k[:, columns(head)] = both[:8].astype(BF16)
                out_v[:, columns(head)] = both[8:].astype(BF16)
    copies[1].start()
    copies[2].start()
    for copy in copies:
        copy.wait()


def local(query, key, value, grad_out, tile_mask, tile_order):
    anywhere = pl.BlockSpec(memory_space=pl.ANY)
    vmem = pl.BlockSpec(memory_space=pltpu.VMEM)
    smem = pl.BlockSpec(memory_space=pltpu.SMEM)
    dma = pltpu.SemaphoreType.DMA
    shape = jax.ShapeDtypeStruct
    most = 16 * 16 // SLOTS + WIDE
    operands = (query, key, value, grad_out, jnp.transpose(tile_mask, (1, 2, 0)), tile_order)
    kv, qg, picked = pl.pallas_call(
        collect,
        out_shape=(
            shape((2, NZ, 2, 128, 128), BF16),
            shape((2, NZ, 2, 128, 128), BF16),
            shape((16, 128), jnp.int32),
        ),
        in_specs=[anywhere] * 5 + [smem],
        out_specs=(vmem, vmem, vmem),
        scratch_shapes=[
            pltpu.VMEM((16, 16, H), jnp.int32),
            pltpu.VMEM((3, 3, 128, 128), BF16),
            dma, dma, dma, dma, dma((3, 3)), dma((3, 3)),
        ],
        compiler_params=pltpu.CompilerParams(
            collective_id=0, has_side_effects=True, vmem_limit_bytes=16 * 1024 * 1024
        ),
    )(*[pltpu.with_memory_space_constraint(a, pltpu.HBM) for a in operands])
    dq, acc = pl.pallas_call(
        gradients,
        out_shape=(
            shape((16, 128, 128), BF16),
            shape((16, 2, 128, 128), F32),
        ),
        in_specs=[vmem, vmem, anywhere],
        out_specs=(vmem, vmem),
        scratch_shapes=[
            pltpu.SMEM((16, 128), jnp.int32),
            pltpu.SMEM((most,), jnp.int32),
            pltpu.VMEM((most, 128 * SLOTS, 128), F32),
            pltpu.VMEM((most, 128 * SLOTS, 128), F32),
            pltpu.VMEM((most, 1, 128), F32),
            pltpu.VMEM((16, 1, 128), F32),
            pltpu.VMEM((16, 1, 128), F32),
            pltpu.VMEM((16, 1, 128), F32),
            pltpu.VMEM((16, 128, 128), F32),
            dma,
        ],
        compiler_params=pltpu.CompilerParams(vmem_limit_bytes=48 * 1024 * 1024),
    )(kv.reshape(16, 2, 128, 128), qg.reshape(16, 2, 128, 128), picked)
    f_q, f_kv = pl.pallas_call(
        give_back,
        out_shape=(shape((NU, 32, 128), BF16), shape((NZ, 6, 16, 128), BF16)),
        in_specs=[vmem] * 2,
        out_specs=(vmem, vmem),
        scratch_shapes=[
            pltpu.VMEM((2 * NU, NZ, 16, 128), BF16),
            pltpu.VMEM((2, 3, 128, 128), BF16),
            pltpu.VMEM((2, 6, NZ, 16, 128), BF16),
            pltpu.VMEM((2, NU, 32, 128), BF16),
            dma, dma, dma((2,)), dma((2, 2)), dma((2,)), dma((2,)), dma, dma,
        ],
        compiler_params=pltpu.CompilerParams(
            collective_id=1, has_side_effects=True, vmem_limit_bytes=16 * 1024 * 1024
        ),
    )(dq, acc)
    out = shape((8, H * DH), BF16)
    return pl.pallas_call(
        assemble,
        out_shape=(out, out, out),
        in_specs=[vmem] * 2,
        out_specs=(anywhere, anywhere, anywhere),
        scratch_shapes=[pltpu.VMEM((8, H * DH), BF16)] * 3 + [dma((3,))],
        compiler_params=pltpu.CompilerParams(vmem_limit_bytes=8 * 1024 * 1024),
    )(*[pltpu.with_memory_space_constraint(a, pltpu.VMEM) for a in (f_q, f_kv)])


def solution(mesh):
    placed = (P("blk", "uly"), P("blk", "uly"), P("blk", "uly"), P("blk", "uly"), P(), P())
    return jax.shard_map(
        local,
        mesh=mesh,
        in_specs=placed,
        out_specs=(P(("blk", "uly"), None), P(("blk", "uly"), None), P(("blk", "uly"), None)),
        check_vma=False,
    )
```

```python
import functools

import jax
import jax.numpy as jnp
from jax import lax
from jax.experimental import pallas as pl
from jax.experimental.pallas import tpu as pltpu
from jax.sharding import PartitionSpec as P

H = 48
DH = 128
TILE = 128
NZ = 8
NU = 16
SLOTS = 2
WIDE = 6
COUNT = 32
EMPTY = 40
MESH = pl.DeviceIdType.MESH
FACTOR = DH ** -0.5
LOG2E = 1.4426950408889634
F32 = jnp.float32
BF16 = jnp.bfloat16


def nt(a, b):
    return lax.dot_general(a, b, (((1,), (1,)), ((), ())), preferred_element_type=F32)


def nn(a, b):
    return lax.dot_general(a, b, (((1,), (0,)), ((), ())), preferred_element_type=F32)


def lift(u):
    x, y = lax.rem(u, 4), lax.div(u, 4)
    return lax.rem(2 * x + 4 * lax.rem(y, 2) + lax.div(y, 2), NZ)


def beside(u):
    x, y = lax.rem(u, 4), lax.div(u, 4)
    other = y + 1 - 2 * lax.rem(y, 2)
    return 4 * y + lax.rem(x + 1, 4), 4 * other + x, 4 * y + lax.rem(x + 3, 4)


def hosted(z, u):
    rel = lax.rem(z - lift(u) + NZ, NZ)
    yes = jnp.logical_or(rel == 0, jnp.logical_or(rel == 3, rel == 6))
    return yes, lax.div(rel, 3)


def remote(src, dst, send, recv, there):
    return pltpu.make_async_remote_copy(
        src_ref=src, dst_ref=dst, send_sem=send, recv_sem=recv,
        device_id=there, device_id_type=MESH,
    )


def arrived(ref, sem):
    pltpu.make_async_copy(ref, ref, sem).wait()


def place():
    blk = lax.axis_index("blk")
    u = lax.axis_index("uly")
    z = lax.div(blk, 2)
    c = lax.rem(blk, 2)
    yes, mine = hosted(z, u)
    return blk, u, z, c, jnp.logical_and(yes, c == lax.rem(mine, 2)), mine


def collect(
    q_in, k_in, v_in, g_in, mask_in, order_ref, kv, qg, picked,
    mask, passing, in_send, kv_sem, qg_sem, mask_sem, pass_sem, pass_send,
):
    blk, u, z, c, is_host, mine = place()
    via = beside(u)
    served = (via[2], via[1], via[0])
    barrier = pltpu.get_barrier_semaphore()

    def greet(there):
        pl.semaphore_signal(barrier, inc=1, device_id=there, device_id_type=MESH)

    get_mask = pltpu.make_async_copy(mask_in, mask, mask_sem)

    @pl.when(is_host)
    def _():
        get_mask.start()

        def greet_line(n, carry):
            greet((lax.rem(blk + n, 2 * NZ), u))
            return carry

        lax.fori_loop(1, 2 * NZ, greet_line, 0)

    for line in served:
        greet((blk, line))

    pl.semaphore_wait(barrier, 3 + 3 - is_host.astype(jnp.int32))

    def inputs(l):
        host = lax.rem(lift(u) + 3 * l, NZ)
        r = lax.rem(z - host + NZ, NZ)
        cols = pl.ds(pl.multiple_of(l * DH, DH), DH)
        there = (2 * host + lax.rem(l, 2), u)
        home = (
            (k_in, kv.at[c, r, 0], kv_sem),
            (v_in, kv.at[c, r, 1], kv_sem),
            (q_in, qg.at[c, r, 0], qg_sem),
            (g_in, qg.at[c, r, 1], qg_sem),
        )
        home = [(src.at[:, cols], dst, sem) for src, dst, sem in home]
        straight = [(src, dst, in_send, sem, there) for src, dst, sem in home]
        around = [
            (home[n + 1][0], passing.at[n, l], in_send, pass_sem.at[n, l], (blk, via[n]))
            for n in range(3)
        ] + straight[:1]
        return host, home, straight, around

    def nth(n, line):
        return lax.rem(z + line + n, 3)

    for n in range(3):
        l = nth(n, u)
        host, home, straight, around = inputs(l)

        @pl.when(host != z)
        def _():
            for move in around:
                remote(*move).start()

        @pl.when(jnp.logical_and(host == z, c != lax.rem(l, 2)))
        def _():
            for move in straight:
                remote(*move).start()

        @pl.when(jnp.logical_and(host == z, c == lax.rem(l, 2)))
        def _():
            for move in home:
                pltpu.make_async_copy(*move).start()

    @pl.when(is_host)
    def _():
        row = lax.broadcasted_iota(jnp.int32, (16, 16), 0)
        lane = lax.broadcasted_iota(jnp.int32, (16, 16), 1)
        ident = jnp.zeros((16, 16), jnp.int32)
        for j in range(16):
            ident = jnp.where(row == j, order_ref[2 * lax.rem(z + j % NZ, NZ) + j // NZ], ident)
        hot = jnp.where(lane == ident, 1.0, 0.0).astype(BF16)
        wide = lax.broadcasted_iota(jnp.int32, (16, 128), 1)
        hot_wide = jnp.where(wide == ident[:, :1], 1.0, 0.0).astype(BF16)
        get_mask.wait()
        flat = jnp.where(mask[...] > 0, 1.0, 0.0).reshape(256, H).astype(BF16)
        head = lax.broadcasted_iota(jnp.int32, (H, 128), 0) == 3 * u + mine
        picked_out = nn(flat, jnp.where(head, 1.0, 0.0).astype(BF16))
        tall = lax.broadcasted_iota(jnp.int32, (16, 16, 128), 1)
        across = lax.broadcasted_iota(jnp.int32, (16, 16, 128), 2)
        table = jnp.where(tall == across, picked_out.reshape(16, 16, 128), 0.0)
        table = jnp.sum(table, axis=1).astype(BF16)
        by_query = nn(hot, table).astype(BF16)
        allowed = nt(by_query, hot_wide)
        before = jnp.where(row < lane, 1.0, 0.0).astype(BF16)
        rank = nn(allowed.astype(BF16), before)
        listed = jnp.where(wide == COUNT, jnp.sum(allowed, axis=1, keepdims=True), 0.0)
        for n in range(16):
            here = jnp.logical_and(allowed > 0.5, jnp.abs(rank - n) < 0.5)
            one = jnp.sum(jnp.where(here, lane.astype(F32), 0.0), axis=1, keepdims=True)
            listed = jnp.where(wide == n, one, listed)
        picked[...] = listed.astype(jnp.int32)

    def passed(n, l):
        host = lax.rem(lift(served[n]) + 3 * l, NZ)
        r = lax.rem(z - host + NZ, NZ)
        dst, sem = (
            (kv.at[c, r, 1], kv_sem),
            (qg.at[c, r, 0], qg_sem),
            (qg.at[c, r, 1], qg_sem),
        )[n]
        there = (2 * host + lax.rem(l, 2), served[n])
        return host != z, remote(passing.at[n, l], dst, pass_send.at[n, l], sem, there)

    for i in range(3):
        for n in range(3):
            l = nth(i, served[n])
            on, move = passed(n, l)

            @pl.when(on)
            def _():
                arrived(passing.at[n, l], pass_sem.at[n, l])
                move.start()

    @pl.when(is_host)
    def _():
        arrived(kv, kv_sem)
        arrived(qg, qg_sem)
        arrived(kv.at[0, pl.ds(0, 4)], in_send)

    @pl.when(jnp.logical_not(is_host))
    def _():
        arrived(kv.at[0, pl.ds(0, 6)], in_send)

    for l in range(3):
        for n in range(3):
            on, move = passed(n, l)
            pl.when(on)(move.wait_send)


def gradients(
    kv, qg, picked_in, dq_out, acc,
    picked, item_code, e_buf, d_buf, top_buf, row_top, row_sum, row_mix, dq_acc, sem,
):
    blk, u, z, c, is_host, mine = place()

    @pl.when(is_host)
    def _():
        get = pltpu.make_async_copy(picked_in, picked, sem)
        get.start()
        acc[...] = jnp.zeros_like(acc)
        dq_acc[...] = jnp.zeros_like(dq_acc)
        row_top[...] = jnp.full_like(row_top, -1e30)
        row_sum[...] = jnp.zeros_like(row_sum)
        row_mix[...] = jnp.zeros_like(row_mix)
        get.wait()

        items = jnp.int32(0)
        for r in range(16):
            end = picked[r, COUNT]
            for base in range(0, 16, SLOTS):
                item_code[items] = r * 4096 + base * 64 + end
                items = items + (base < end).astype(jnp.int32)
        for m in range(WIDE - 1):
            item_code[items + m] = EMPTY * 64
        rounds = lax.div(items + WIDE - 1, WIDE)

        def item(i):
            code = item_code[i]
            base = lax.bitwise_and(lax.shift_right_logical(code, 6), 63)
            return lax.shift_right_logical(code, 12), base, lax.bitwise_and(code, 63)

        def tiles(ref, r, base, part):
            return jnp.concatenate(
                [ref[picked[r, base + m], part] for m in range(SLOTS)], axis=0
            )

        def weigh(t, carry):
            for w in range(WIDE):
                i = t * WIDE + w
                r, base, end = item(i)
                scores = nt(tiles(kv, r, base, 0), qg[r, 0]) * (FACTOR * LOG2E)
                scores = jnp.concatenate(
                    [
                        scores[128 * m:128 * m + 128]
                        + jnp.where(base + m < end, 0.0, -1e30)
                        for m in range(SLOTS)
                    ],
                    axis=0,
                )
                top = jnp.max(scores, axis=0, keepdims=True)
                e = jnp.exp2(scores - top)
                dprob = nt(tiles(kv, r, base, 1), qg[r, 1])
                e_buf[i] = e
                d_buf[i] = dprob
                top_buf[i] = top
                total = jnp.sum(e, axis=0, keepdims=True)
                mixed = jnp.sum(e * dprob, axis=0, keepdims=True)
                old = row_top[r]
                new = jnp.maximum(old, top)
                keep = jnp.exp2(old - new)
                part = jnp.exp2(top - new)
                row_top[r] = new
                row_sum[r] = row_sum[r] * keep + total * part
                row_mix[r] = row_mix[r] * keep + mixed * part
            return carry

        lax.fori_loop(0, rounds, weigh, 0)

        def spread(t, carry):
            for w in range(WIDE):
                i = t * WIDE + w
                r, base, _ = item(i)
                whole = 1.0 / row_sum[r]
                prob = e_buf[i] * (jnp.exp2(top_buf[i] - row_top[r]) * whole)
                dscore = (prob * (d_buf[i] - row_mix[r] * whole)).astype(BF16)
                dk = nn(dscore, qg[r, 0])
                dv = nn(prob.astype(BF16), qg[r, 1])
                dq_acc[r] += lax.dot_general(
                    dscore, tiles(kv, r, base, 0), (((0,), (0,)), ((), ())),
                    preferred_element_type=F32,
                )
                for m in range(SLOTS):
                    j = picked[r, base + m]
                    acc[j, 0] += dk[128 * m:128 * m + 128]
                    acc[j, 1] += dv[128 * m:128 * m + 128]
            return carry

        lax.fori_loop(0, rounds, spread, 0)
        dq_out[...] = (dq_acc[...] * FACTOR).astype(BF16)


def give_back(
    dq_in, acc, f_q, f_kv, kv_out, r_q, r_kv, t_q,
    p1q_send, p1k_send, rq_sem, rkv_sem, p2q_send, p2k_send, fq_sem, fkv_sem,
):
    blk, u, z, c, is_host, mine = place()
    seat = mine * 2 + lax.rem(lax.div(u, 4), 2)
    chip_hosts = hosted(z, u)[0]
    passes = [
        jnp.logical_and(jnp.logical_not(is_host), jnp.logical_or(chip_hosts, c == side))
        for side in range(2)
    ]
    barrier = pltpu.get_barrier_semaphore()

    def passer(h, line, side):
        yes, l = hosted(h, line)
        return 2 * h + jnp.where(yes, 1 - lax.rem(l, 2), side), line

    def greet(there):
        @pl.when(jnp.logical_or(there[0] != blk, there[1] != u))
        def _():
            pl.semaphore_signal(barrier, inc=1, device_id=there, device_id_type=MESH)

    def greet_line(h, carry):
        greet(passer(h, u, c))
        return carry

    def greet_plane(n, carry):
        greet(passer(z, lax.rem(u + n, NU), c))
        return carry

    greet_plane(0, 0)

    @pl.when(jnp.logical_not(is_host))
    def _():
        lax.fori_loop(0, NZ, greet_line, 0)
        lax.fori_loop(1, NU, greet_plane, 0)
        for l in range(3):
            greet((2 * lax.rem(lift(u) + 3 * l, NZ) + l % 2, u))
            up = lax.rem(z - 3 * l + 2 * NZ, NZ)
            for half in range(2):
                x = lax.div(lax.rem(up - lax.rem(up, 2) - 4 * half + NZ, NZ), 2)
                greet((2 * z + l % 2, 4 * (2 * lax.rem(up, 2) + half) + x))

    alone = jnp.logical_not(chip_hosts).astype(jnp.int32)
    pl.semaphore_wait(barrier, jnp.where(is_host, 39, 22 + 24 * (1 - alone)))

    @pl.when(is_host)
    def _():
        def stage(h, carry):
            for side in range(2):
                j = NZ * side + lax.rem(h - z + NZ, NZ)
                dk = acc[j, 0] * FACTOR
                dv = acc[j, 1]
                for n in range(NU):
                    piece = jnp.concatenate([dk[8 * n:8 * n + 8], dv[8 * n:8 * n + 8]], axis=0)
                    kv_out[NU * side + n, h] = piece.astype(BF16)
            return carry

        def send_q(h, carry):
            for side in range(2):
                tile = dq_in.at[NZ * side + lax.rem(h - z + NZ, NZ)]
                there = passer(h, u, side)
                remote(tile, r_q.at[side, mine], p1q_send, rq_sem.at[side], there).start()
            return carry

        lax.fori_loop(0, NZ, send_q, 0)
        lax.fori_loop(0, NZ, greet_line, 0)
        lax.fori_loop(1, NU, greet_plane, 0)
        for part in range(2):
            heights = pl.ds(4 * part, 4)

            def send_k(n, carry):
                to = lax.rem(u + n, NU)
                for side in range(2):
                    remote(
                        kv_out.at[NU * side + to, heights], r_kv.at[side, seat, heights],
                        p1k_send, rkv_sem.at[part, side], passer(z, to, side),
                    ).start()
                return carry

            lax.fori_loop(4 * part, 4 * part + 4, stage, 0)
            lax.fori_loop(0, NU, send_k, 0)

    def pass_q(side):
        arrived(r_q.at[side], rq_sem.at[side])
        heads = [r_q[side, l].astype(F32) for l in range(3)]
        for n in range(NU):
            rows = slice(8 * n, 8 * n + 8)
            both = jnp.concatenate([heads[0][rows], heads[1][rows]], axis=0)
            t_q[side, n, :16] = both.astype(BF16)
            both = jnp.concatenate([heads[2][rows], heads[2][rows]], axis=0)
            t_q[side, n, 16:] = both.astype(BF16)

        def one(n, carry):
            to = lax.rem(u + n, NU)
            there = (2 * z + side, to)
            remote(t_q.at[side, to], f_q.at[u], p2q_send.at[side], fq_sem, there).start()
            return carry

        lax.fori_loop(1, NU, one, 0)

        @pl.when(c != side)
        def _():
            one(0, 0)

        @pl.when(c == side)
        def _():
            pltpu.make_async_copy(t_q.at[side, u], f_q.at[u], fq_sem).start()

    def pass_k(part, side):
        arrived(r_kv.at[side, :, pl.ds(4 * part, 4)], rkv_sem.at[part, side])

        def one(h, carry):
            src = r_kv.at[side, :, h]

            @pl.when(jnp.logical_or(h != z, c != side))
            def _():
                there = (2 * h + side, u)
                remote(src, f_kv.at[z], p2k_send.at[side], fkv_sem, there).start()

            @pl.when(jnp.logical_and(h == z, c == side))
            def _():
                pltpu.make_async_copy(src, f_kv.at[z], fkv_sem).start()

            return carry

        lax.fori_loop(4 * part, 4 * part + 4, one, 0)

    for side in range(2):
        pl.when(passes[side])(functools.partial(pass_q, side))
    for part in range(2):
        for side in range(2):
            pl.when(passes[side])(functools.partial(pass_k, part, side))

    @pl.when(is_host)
    def _():
        arrived(dq_in, p1q_send)
        arrived(kv_out, p1k_send)

    for side in range(2):

        @pl.when(jnp.logical_and(passes[side], c == side))
        def _():
            arrived(t_q.at[side, pl.ds(0, NU - 1)], p2q_send.at[side])
            arrived(r_kv.at[side, :, pl.ds(0, NZ - 1)], p2k_send.at[side])

        @pl.when(jnp.logical_and(passes[side], c != side))
        def _():
            arrived(t_q.at[side], p2q_send.at[side])
            arrived(r_kv.at[side], p2k_send.at[side])

    arrived(f_q, fq_sem)
    arrived(f_kv, fkv_sem)


def assemble(f_q, f_kv, q_hbm, k_hbm, v_hbm, out_q, out_k, out_v, sems):
    def columns(head):
        return slice(head * DH, head * DH + DH)

    copies = [
        pltpu.make_async_copy(src, dst, sems.at[n])
        for n, (src, dst) in enumerate(((out_q, q_hbm), (out_k, k_hbm), (out_v, v_hbm)))
    ]
    for n in range(NU):
        first = f_q[n, :16].astype(F32)
        out_q[:, columns(3 * n)] = first[:8].astype(BF16)
        out_q[:, columns(3 * n + 1)] = first[8:].astype(BF16)
        out_q[:, columns(3 * n + 2)] = f_q[n, 16:].astype(F32)[:8].astype(BF16)
    copies[0].start()
    for d in range(NZ):
        for l in range(3):
            for half in range(2):
                both = f_kv[d, 2 * l + half].astype(F32)
                up = (d - 3 * l) % NZ
                x = (up - up % 2 - 4 * half) % NZ // 2
                head = 3 * (4 * (2 * (up % 2) + half) + x) + l
                out_k[:, columns(head)] = both[:8].astype(BF16)
                out_v[:, columns(head)] = both[8:].astype(BF16)
    copies[1].start()
    copies[2].start()
    for copy in copies:
        copy.wait()


def local(query, key, value, grad_out, tile_mask, tile_order):
    anywhere = pl.BlockSpec(memory_space=pl.ANY)
    vmem = pl.BlockSpec(memory_space=pltpu.VMEM)
    smem = pl.BlockSpec(memory_space=pltpu.SMEM)
    dma = pltpu.SemaphoreType.DMA
    shape = jax.ShapeDtypeStruct
    most = 16 * 16 // SLOTS + WIDE
    operands = (query, key, value, grad_out, jnp.transpose(tile_mask, (1, 2, 0)), tile_order)
    kv, qg, picked = pl.pallas_call(
        collect,
        out_shape=(
            shape((2, NZ, 2, 128, 128), BF16),
            shape((2, NZ, 2, 128, 128), BF16),
            shape((16, 128), jnp.int32),
        ),
        in_specs=[anywhere] * 5 + [smem],
        out_specs=(vmem, vmem, vmem),
        scratch_shapes=[
            pltpu.VMEM((16, 16, H), jnp.int32),
            pltpu.VMEM((3, 3, 128, 128), BF16),
            dma, dma, dma, dma, dma((3, 3)), dma((3, 3)),
        ],
        compiler_params=pltpu.CompilerParams(
            collective_id=0, has_side_effects=True, vmem_limit_bytes=16 * 1024 * 1024
        ),
    )(*[pltpu.with_memory_space_constraint(a, pltpu.HBM) for a in operands])
    dq, acc = pl.pallas_call(
        gradients,
        out_shape=(
            shape((16, 128, 128), BF16),
            shape((16, 2, 128, 128), F32),
        ),
        in_specs=[vmem, vmem, anywhere],
        out_specs=(vmem, vmem),
        scratch_shapes=[
            pltpu.SMEM((16, 128), jnp.int32),
            pltpu.SMEM((most,), jnp.int32),
            pltpu.VMEM((most, 128 * SLOTS, 128), F32),
            pltpu.VMEM((most, 128 * SLOTS, 128), F32),
            pltpu.VMEM((most, 1, 128), F32),
            pltpu.VMEM((16, 1, 128), F32),
            pltpu.VMEM((16, 1, 128), F32),
            pltpu.VMEM((16, 1, 128), F32),
            pltpu.VMEM((16, 128, 128), F32),
            dma,
        ],
        compiler_params=pltpu.CompilerParams(vmem_limit_bytes=48 * 1024 * 1024),
    )(kv.reshape(16, 2, 128, 128), qg.reshape(16, 2, 128, 128), picked)
    f_q, f_kv = pl.pallas_call(
        give_back,
        out_shape=(shape((NU, 32, 128), BF16), shape((NZ, 6, 16, 128), BF16)),
        in_specs=[vmem] * 2,
        out_specs=(vmem, vmem),
        scratch_shapes=[
            pltpu.VMEM((2 * NU, NZ, 16, 128), BF16),
            pltpu.VMEM((2, 3, 128, 128), BF16),
            pltpu.VMEM((2, 6, NZ, 16, 128), BF16),
            pltpu.VMEM((2, NU, 32, 128), BF16),
            dma, dma, dma((2,)), dma((2, 2)), dma((2,)), dma((2,)), dma, dma,
        ],
        compiler_params=pltpu.CompilerParams(
            collective_id=1, has_side_effects=True, vmem_limit_bytes=16 * 1024 * 1024
        ),
    )(dq, acc)
    out = shape((8, H * DH), BF16)
    return pl.pallas_call(
        assemble,
        out_shape=(out, out, out),
        in_specs=[vmem] * 2,
        out_specs=(anywhere, anywhere, anywhere),
        scratch_shapes=[pltpu.VMEM((8, H * DH), BF16)] * 3 + [dma((3,))],
        compiler_params=pltpu.CompilerParams(vmem_limit_bytes=8 * 1024 * 1024),
    )(*[pltpu.with_memory_space_constraint(a, pltpu.VMEM) for a in (f_q, f_kv)])


def solution(mesh):
    placed = (P("blk", "uly"), P("blk", "uly"), P("blk", "uly"), P("blk", "uly"), P(), P())
    return jax.shard_map(
        local,
        mesh=mesh,
        in_specs=placed,
        out_specs=(P(("blk", "uly"), None), P(("blk", "uly"), None), P(("blk", "uly"), None)),
        check_vma=False,
    )
```

```python
import functools

import jax
import jax.numpy as jnp
from jax import lax
from jax.experimental import pallas as pl
from jax.experimental.pallas import tpu as pltpu
from jax.sharding import PartitionSpec as P

H = 48
DH = 128
TILE = 128
NZ = 8
NU = 16
SLOTS = 2
WIDE = 6
COUNT = 32
EMPTY = 40
MESH = pl.DeviceIdType.MESH
FACTOR = DH ** -0.5
LOG2E = 1.4426950408889634
F32 = jnp.float32
BF16 = jnp.bfloat16


def nt(a, b):
    return lax.dot_general(a, b, (((1,), (1,)), ((), ())), preferred_element_type=F32)


def nn(a, b):
    return lax.dot_general(a, b, (((1,), (0,)), ((), ())), preferred_element_type=F32)


def lift(u):
    x, y = lax.rem(u, 4), lax.div(u, 4)
    return lax.rem(2 * x + 4 * lax.rem(y, 2) + lax.div(y, 2), NZ)


def beside(u):
    x, y = lax.rem(u, 4), lax.div(u, 4)
    other = y + 1 - 2 * lax.rem(y, 2)
    return 4 * y + lax.rem(x + 1, 4), 4 * other + x, 4 * y + lax.rem(x + 3, 4)


def hosted(z, u):
    rel = lax.rem(z - lift(u) + NZ, NZ)
    yes = jnp.logical_or(rel == 0, jnp.logical_or(rel == 3, rel == 6))
    return yes, lax.div(rel, 3)


def remote(src, dst, send, recv, there):
    return pltpu.make_async_remote_copy(
        src_ref=src, dst_ref=dst, send_sem=send, recv_sem=recv,
        device_id=there, device_id_type=MESH,
    )


def arrived(ref, sem):
    pltpu.make_async_copy(ref, ref, sem).wait()


def place():
    blk = lax.axis_index("blk")
    u = lax.axis_index("uly")
    z = lax.div(blk, 2)
    c = lax.rem(blk, 2)
    yes, mine = hosted(z, u)
    return blk, u, z, c, jnp.logical_and(yes, c == lax.rem(mine, 2)), mine


def collect(
    q_in, k_in, v_in, g_in, mask_in, order_ref, kv, qg, picked,
    mask, passing, in_send, kv_sem, qg_sem, mask_sem, pass_sem, pass_send,
):
    blk, u, z, c, is_host, mine = place()
    via = beside(u)
    served = (via[2], via[1], via[0])
    barrier = pltpu.get_barrier_semaphore()

    def greet(there):
        pl.semaphore_signal(barrier, inc=1, device_id=there, device_id_type=MESH)

    get_mask = pltpu.make_async_copy(mask_in, mask, mask_sem)

    @pl.when(is_host)
    def _():
        get_mask.start()

        def greet_line(n, carry):
            greet((lax.rem(blk + n, 2 * NZ), u))
            return carry

        lax.fori_loop(1, 2 * NZ, greet_line, 0)

    for line in served:
        greet((blk, line))

    pl.semaphore_wait(barrier, 3 + 3 - is_host.astype(jnp.int32))

    def inputs(l):
        host = lax.rem(lift(u) + 3 * l, NZ)
        r = lax.rem(z - host + NZ, NZ)
        cols = pl.ds(pl.multiple_of(l * DH, DH), DH)
        there = (2 * host + lax.rem(l, 2), u)
        home = (
            (k_in, kv.at[c, r, 0], kv_sem),
            (v_in, kv.at[c, r, 1], kv_sem),
            (q_in, qg.at[c, r, 0], qg_sem),
            (g_in, qg.at[c, r, 1], qg_sem),
        )
        home = [(src.at[:, cols], dst, sem) for src, dst, sem in home]
        straight = [(src, dst, in_send, sem, there) for src, dst, sem in home]
        around = straight[:1] + [
            (home[n + 1][0], passing.at[n, l], in_send, pass_sem.at[n, l], (blk, via[n]))
            for n in range(3)
        ]
        return host, home, straight, around

    def nth(n, line):
        return lax.rem(z + line + n, 3)

    for part in (slice(0, 1), slice(1, 4)):
        for n in range(3):
            l = nth(n, u)
            host, home, straight, around = inputs(l)

            @pl.when(host != z)
            def _():
                for move in around[part]:
                    remote(*move).start()

            @pl.when(jnp.logical_and(host == z, c != lax.rem(l, 2)))
            def _():
                for move in straight[part]:
                    remote(*move).start()

            @pl.when(jnp.logical_and(host == z, c == lax.rem(l, 2)))
            def _():
                for move in home[part]:
                    pltpu.make_async_copy(*move).start()

    @pl.when(is_host)
    def _():
        row = lax.broadcasted_iota(jnp.int32, (16, 16), 0)
        lane = lax.broadcasted_iota(jnp.int32, (16, 16), 1)
        ident = jnp.zeros((16, 16), jnp.int32)
        for j in range(16):
            ident = jnp.where(row == j, order_ref[2 * lax.rem(z + j % NZ, NZ) + j // NZ], ident)
        hot = jnp.where(lane == ident, 1.0, 0.0).astype(BF16)
        wide = lax.broadcasted_iota(jnp.int32, (16, 128), 1)
        hot_wide = jnp.where(wide == ident[:, :1], 1.0, 0.0).astype(BF16)
        get_mask.wait()
        flat = jnp.where(mask[...] > 0, 1.0, 0.0).reshape(256, H).astype(BF16)
        head = lax.broadcasted_iota(jnp.int32, (H, 128), 0) == 3 * u + mine
        picked_out = nn(flat, jnp.where(head, 1.0, 0.0).astype(BF16))
        tall = lax.broadcasted_iota(jnp.int32, (16, 16, 128), 1)
        across = lax.broadcasted_iota(jnp.int32, (16, 16, 128), 2)
        table = jnp.where(tall == across, picked_out.reshape(16, 16, 128), 0.0)
        table = jnp.sum(table, axis=1).astype(BF16)
        by_query = nn(hot, table).astype(BF16)
        allowed = nt(by_query, hot_wide)
        before = jnp.where(row < lane, 1.0, 0.0).astype(BF16)
        rank = nn(allowed.astype(BF16), before)
        listed = jnp.where(wide == COUNT, jnp.sum(allowed, axis=1, keepdims=True), 0.0)
        for n in range(16):
            here = jnp.logical_and(allowed > 0.5, jnp.abs(rank - n) < 0.5)
            one = jnp.sum(jnp.where(here, lane.astype(F32), 0.0), axis=1, keepdims=True)
            listed = jnp.where(wide == n, one, listed)
        picked[...] = listed.astype(jnp.int32)

    def passed(n, l):
        host = lax.rem(lift(served[n]) + 3 * l, NZ)
        r = lax.rem(z - host + NZ, NZ)
        dst, sem = (
            (kv.at[c, r, 1], kv_sem),
            (qg.at[c, r, 0], qg_sem),
            (qg.at[c, r, 1], qg_sem),
        )[n]
        there = (2 * host + lax.rem(l, 2), served[n])
        return host != z, remote(passing.at[n, l], dst, pass_send.at[n, l], sem, there)

    for i in range(3):
        for n in range(3):
            l = nth(i, served[n])
            on, move = passed(n, l)

            @pl.when(on)
            def _():
                arrived(passing.at[n, l], pass_sem.at[n, l])
                move.start()

    @pl.when(is_host)
    def _():
        arrived(kv, kv_sem)
        arrived(qg, qg_sem)
        arrived(kv.at[0, pl.ds(0, 4)], in_send)

    @pl.when(jnp.logical_not(is_host))
    def _():
        arrived(kv.at[0, pl.ds(0, 6)], in_send)

    for l in range(3):
        for n in range(3):
            on, move = passed(n, l)
            pl.when(on)(move.wait_send)


def gradients(
    kv, qg, picked_in, dq_out, acc,
    picked, item_code, e_buf, d_buf, top_buf, row_top, row_sum, row_mix, dq_acc, sem,
):
    blk, u, z, c, is_host, mine = place()

    @pl.when(is_host)
    def _():
        get = pltpu.make_async_copy(picked_in, picked, sem)
        get.start()
        acc[...] = jnp.zeros_like(acc)
        dq_acc[...] = jnp.zeros_like(dq_acc)
        row_top[...] = jnp.full_like(row_top, -1e30)
        row_sum[...] = jnp.zeros_like(row_sum)
        row_mix[...] = jnp.zeros_like(row_mix)
        get.wait()

        items = jnp.int32(0)
        for r in range(16):
            end = picked[r, COUNT]
            for base in range(0, 16, SLOTS):
                item_code[items] = r * 4096 + base * 64 + end
                items = items + (base < end).astype(jnp.int32)
        for m in range(WIDE - 1):
            item_code[items + m] = EMPTY * 64
        rounds = lax.div(items + WIDE - 1, WIDE)

        def item(i):
            code = item_code[i]
            base = lax.bitwise_and(lax.shift_right_logical(code, 6), 63)
            return lax.shift_right_logical(code, 12), base, lax.bitwise_and(code, 63)

        def tiles(ref, r, base, part):
            return jnp.concatenate(
                [ref[picked[r, base + m], part] for m in range(SLOTS)], axis=0
            )

        def weigh(t, carry):
            for w in range(WIDE):
                i = t * WIDE + w
                r, base, end = item(i)
                scores = nt(tiles(kv, r, base, 0), qg[r, 0]) * (FACTOR * LOG2E)
                scores = jnp.concatenate(
                    [
                        scores[128 * m:128 * m + 128]
                        + jnp.where(base + m < end, 0.0, -1e30)
                        for m in range(SLOTS)
                    ],
                    axis=0,
                )
                top = jnp.max(scores, axis=0, keepdims=True)
                e = jnp.exp2(scores - top)
                dprob = nt(tiles(kv, r, base, 1), qg[r, 1])
                e_buf[i] = e
                d_buf[i] = dprob
                top_buf[i] = top
                total = jnp.sum(e, axis=0, keepdims=True)
                mixed = jnp.sum(e * dprob, axis=0, keepdims=True)
                old = row_top[r]
                new = jnp.maximum(old, top)
                keep = jnp.exp2(old - new)
                part = jnp.exp2(top - new)
                row_top[r] = new
                row_sum[r] = row_sum[r] * keep + total * part
                row_mix[r] = row_mix[r] * keep + mixed * part
            return carry

        lax.fori_loop(0, rounds, weigh, 0)

        def spread(t, carry):
            for w in range(WIDE):
                i = t * WIDE + w
                r, base, _ = item(i)
                whole = 1.0 / row_sum[r]
                prob = e_buf[i] * (jnp.exp2(top_buf[i] - row_top[r]) * whole)
                dscore = (prob * (d_buf[i] - row_mix[r] * whole)).astype(BF16)
                dk = nn(dscore, qg[r, 0])
                dv = nn(prob.astype(BF16), qg[r, 1])
                dq_acc[r] += lax.dot_general(
                    dscore, tiles(kv, r, base, 0), (((0,), (0,)), ((), ())),
                    preferred_element_type=F32,
                )
                for m in range(SLOTS):
                    j = picked[r, base + m]
                    acc[j, 0] += dk[128 * m:128 * m + 128]
                    acc[j, 1] += dv[128 * m:128 * m + 128]
            return carry

        lax.fori_loop(0, rounds, spread, 0)
        dq_out[...] = (dq_acc[...] * FACTOR).astype(BF16)


def give_back(
    dq_in, acc, f_q, f_kv, kv_out, r_q, r_kv, t_q,
    p1q_send, p1k_send, rq_sem, rkv_sem, p2q_send, p2k_send, fq_sem, fkv_sem,
):
    blk, u, z, c, is_host, mine = place()
    seat = mine * 2 + lax.rem(lax.div(u, 4), 2)
    chip_hosts = hosted(z, u)[0]
    passes = [
        jnp.logical_and(jnp.logical_not(is_host), jnp.logical_or(chip_hosts, c == side))
        for side in range(2)
    ]
    barrier = pltpu.get_barrier_semaphore()

    def passer(h, line, side):
        yes, l = hosted(h, line)
        return 2 * h + jnp.where(yes, 1 - lax.rem(l, 2), side), line

    def greet(there):
        @pl.when(jnp.logical_or(there[0] != blk, there[1] != u))
        def _():
            pl.semaphore_signal(barrier, inc=1, device_id=there, device_id_type=MESH)

    def greet_line(h, carry):
        greet(passer(h, u, c))
        return carry

    def greet_plane(n, carry):
        greet(passer(z, lax.rem(u + n, NU), c))
        return carry

    greet_plane(0, 0)

    @pl.when(jnp.logical_not(is_host))
    def _():
        lax.fori_loop(0, NZ, greet_line, 0)
        lax.fori_loop(1, NU, greet_plane, 0)
        for l in range(3):
            greet((2 * lax.rem(lift(u) + 3 * l, NZ) + l % 2, u))
            up = lax.rem(z - 3 * l + 2 * NZ, NZ)
            for half in range(2):
                x = lax.div(lax.rem(up - lax.rem(up, 2) - 4 * half + NZ, NZ), 2)
                greet((2 * z + l % 2, 4 * (2 * lax.rem(up, 2) + half) + x))

    alone = jnp.logical_not(chip_hosts).astype(jnp.int32)
    pl.semaphore_wait(barrier, jnp.where(is_host, 39, 22 + 24 * (1 - alone)))

    @pl.when(is_host)
    def _():
        def stage(h, carry):
            for side in range(2):
                j = NZ * side + lax.rem(h - z + NZ, NZ)
                dk = acc[j, 0] * FACTOR
                dv = acc[j, 1]
                for n in range(NU):
                    piece = jnp.concatenate([dk[8 * n:8 * n + 8], dv[8 * n:8 * n + 8]], axis=0)
                    kv_out[NU * side + n, h] = piece.astype(BF16)
            return carry

        def send_q(h, carry):
            for side in range(2):
                tile = dq_in.at[NZ * side + lax.rem(h - z + NZ, NZ)]
                there = passer(h, u, side)
                remote(tile, r_q.at[side, mine], p1q_send, rq_sem.at[side], there).start()
            return carry

        lax.fori_loop(0, NZ, send_q, 0)
        lax.fori_loop(0, NZ, greet_line, 0)
        lax.fori_loop(1, NU, greet_plane, 0)
        for part in range(2):
            heights = pl.ds(4 * part, 4)

            def send_k(to, carry):
                for side in range(2):
                    remote(
                        kv_out.at[NU * side + to, heights], r_kv.at[side, seat, heights],
                        p1k_send, rkv_sem.at[part, side], passer(z, to, side),
                    ).start()
                return carry

            lax.fori_loop(4 * part, 4 * part + 4, stage, 0)
            lax.fori_loop(0, NU, send_k, 0)

    def pass_q(side):
        arrived(r_q.at[side], rq_sem.at[side])
        heads = [r_q[side, l].astype(F32) for l in range(3)]
        for n in range(NU):
            rows = slice(8 * n, 8 * n + 8)
            both = jnp.concatenate([heads[0][rows], heads[1][rows]], axis=0)
            t_q[side, n, :16] = both.astype(BF16)
            both = jnp.concatenate([heads[2][rows], heads[2][rows]], axis=0)
            t_q[side, n, 16:] = both.astype(BF16)

        def one(to, carry):
            @pl.when(jnp.logical_or(to != u, c != side))
            def _():
                there = (2 * z + side, to)
                remote(t_q.at[side, to], f_q.at[u], p2q_send.at[side], fq_sem, there).start()

            @pl.when(jnp.logical_and(to == u, c == side))
            def _():
                pltpu.make_async_copy(t_q.at[side, to], f_q.at[u], fq_sem).start()

            return carry

        lax.fori_loop(0, NU, one, 0)

    def pass_k(part, side):
        arrived(r_kv.at[side, :, pl.ds(4 * part, 4)], rkv_sem.at[part, side])

        def one(h, carry):
            src = r_kv.at[side, :, h]

            @pl.when(jnp.logical_or(h != z, c != side))
            def _():
                there = (2 * h + side, u)
                remote(src, f_kv.at[z], p2k_send.at[side], fkv_sem, there).start()

            @pl.when(jnp.logical_and(h == z, c == side))
            def _():
                pltpu.make_async_copy(src, f_kv.at[z], fkv_sem).start()

            return carry

        lax.fori_loop(4 * part, 4 * part + 4, one, 0)

    for side in range(2):
        pl.when(passes[side])(functools.partial(pass_q, side))
    for part in range(2):
        for side in range(2):
            pl.when(passes[side])(functools.partial(pass_k, part, side))

    @pl.when(is_host)
    def _():
        arrived(dq_in, p1q_send)
        arrived(kv_out, p1k_send)

    for side in range(2):

        @pl.when(jnp.logical_and(passes[side], c == side))
        def _():
            arrived(t_q.at[side, pl.ds(0, NU - 1)], p2q_send.at[side])
            arrived(r_kv.at[side, :, pl.ds(0, NZ - 1)], p2k_send.at[side])

        @pl.when(jnp.logical_and(passes[side], c != side))
        def _():
            arrived(t_q.at[side], p2q_send.at[side])
            arrived(r_kv.at[side], p2k_send.at[side])

    arrived(f_q, fq_sem)
    arrived(f_kv, fkv_sem)


def assemble(f_q, f_kv, q_hbm, k_hbm, v_hbm, out_q, out_k, out_v, sems):
    def columns(head):
        return slice(head * DH, head * DH + DH)

    copies = [
        pltpu.make_async_copy(src, dst, sems.at[n])
        for n, (src, dst) in enumerate(((out_q, q_hbm), (out_k, k_hbm), (out_v, v_hbm)))
    ]
    for n in range(NU):
        first = f_q[n, :16].astype(F32)
        out_q[:, columns(3 * n)] = first[:8].astype(BF16)
        out_q[:, columns(3 * n + 1)] = first[8:].astype(BF16)
        out_q[:, columns(3 * n + 2)] = f_q[n, 16:].astype(F32)[:8].astype(BF16)
    copies[0].start()
    for d in range(NZ):
        for l in range(3):
            for half in range(2):
                both = f_kv[d, 2 * l + half].astype(F32)
                up = (d - 3 * l) % NZ
                x = (up - up % 2 - 4 * half) % NZ // 2
                head = 3 * (4 * (2 * (up % 2) + half) + x) + l
                out_k[:, columns(head)] = both[:8].astype(BF16)
                out_v[:, columns(head)] = both[8:].astype(BF16)
    copies[1].start()
    copies[2].start()
    for copy in copies:
        copy.wait()


def local(query, key, value, grad_out, tile_mask, tile_order):
    anywhere = pl.BlockSpec(memory_space=pl.ANY)
    vmem = pl.BlockSpec(memory_space=pltpu.VMEM)
    smem = pl.BlockSpec(memory_space=pltpu.SMEM)
    dma = pltpu.SemaphoreType.DMA
    shape = jax.ShapeDtypeStruct
    most = 16 * 16 // SLOTS + WIDE
    operands = (query, key, value, grad_out, jnp.transpose(tile_mask, (1, 2, 0)), tile_order)
    kv, qg, picked = pl.pallas_call(
        collect,
        out_shape=(
            shape((2, NZ, 2, 128, 128), BF16),
            shape((2, NZ, 2, 128, 128), BF16),
            shape((16, 128), jnp.int32),
        ),
        in_specs=[anywhere] * 5 + [smem],
        out_specs=(vmem, vmem, vmem),
        scratch_shapes=[
            pltpu.VMEM((16, 16, H), jnp.int32),
            pltpu.VMEM((3, 3, 128, 128), BF16),
            dma, dma, dma, dma, dma((3, 3)), dma((3, 3)),
        ],
        compiler_params=pltpu.CompilerParams(
            collective_id=0, has_side_effects=True, vmem_limit_bytes=16 * 1024 * 1024
        ),
    )(*[pltpu.with_memory_space_constraint(a, pltpu.HBM) for a in operands])
    dq, acc = pl.pallas_call(
        gradients,
        out_shape=(
            shape((16, 128, 128), BF16),
            shape((16, 2, 128, 128), F32),
        ),
        in_specs=[vmem, vmem, anywhere],
        out_specs=(vmem, vmem),
        scratch_shapes=[
            pltpu.SMEM((16, 128), jnp.int32),
            pltpu.SMEM((most,), jnp.int32),
            pltpu.VMEM((most, 128 * SLOTS, 128), F32),
            pltpu.VMEM((most, 128 * SLOTS, 128), F32),
            pltpu.VMEM((most, 1, 128), F32),
            pltpu.VMEM((16, 1, 128), F32),
            pltpu.VMEM((16, 1, 128), F32),
            pltpu.VMEM((16, 1, 128), F32),
            pltpu.VMEM((16, 128, 128), F32),
            dma,
        ],
        compiler_params=pltpu.CompilerParams(vmem_limit_bytes=48 * 1024 * 1024),
    )(kv.reshape(16, 2, 128, 128), qg.reshape(16, 2, 128, 128), picked)
    f_q, f_kv = pl.pallas_call(
        give_back,
        out_shape=(shape((NU, 32, 128), BF16), shape((NZ, 6, 16, 128), BF16)),
        in_specs=[vmem] * 2,
        out_specs=(vmem, vmem),
        scratch_shapes=[
            pltpu.VMEM((2 * NU, NZ, 16, 128), BF16),
            pltpu.VMEM((2, 3, 128, 128), BF16),
            pltpu.VMEM((2, 6, NZ, 16, 128), BF16),
            pltpu.VMEM((2, NU, 32, 128), BF16),
            dma, dma, dma((2,)), dma((2, 2)), dma((2,)), dma((2,)), dma, dma,
        ],
        compiler_params=pltpu.CompilerParams(
            collective_id=1, has_side_effects=True, vmem_limit_bytes=16 * 1024 * 1024
        ),
    )(dq, acc)
    out = shape((8, H * DH), BF16)
    return pl.pallas_call(
        assemble,
        out_shape=(out, out, out),
        in_specs=[vmem] * 2,
        out_specs=(anywhere, anywhere, anywhere),
        scratch_shapes=[pltpu.VMEM((8, H * DH), BF16)] * 3 + [dma((3,))],
        compiler_params=pltpu.CompilerParams(vmem_limit_bytes=8 * 1024 * 1024),
    )(*[pltpu.with_memory_space_constraint(a, pltpu.VMEM) for a in (f_q, f_kv)])


def solution(mesh):
    placed = (P("blk", "uly"), P("blk", "uly"), P("blk", "uly"), P("blk", "uly"), P(), P())
    return jax.shard_map(
        local,
        mesh=mesh,
        in_specs=placed,
        out_specs=(P(("blk", "uly"), None), P(("blk", "uly"), None), P(("blk", "uly"), None)),
        check_vma=False,
    )
```

```python
import functools

import jax
import jax.numpy as jnp
from jax import lax
from jax.experimental import pallas as pl
from jax.experimental.pallas import tpu as pltpu
from jax.sharding import PartitionSpec as P

H = 48
DH = 128
TILE = 128
NZ = 8
NU = 16
SLOTS = 2
WIDE = 6
COUNT = 32
EMPTY = 40
MESH = pl.DeviceIdType.MESH
FACTOR = DH ** -0.5
LOG2E = 1.4426950408889634
F32 = jnp.float32
BF16 = jnp.bfloat16


def nt(a, b):
    return lax.dot_general(a, b, (((1,), (1,)), ((), ())), preferred_element_type=F32)


def nn(a, b):
    return lax.dot_general(a, b, (((1,), (0,)), ((), ())), preferred_element_type=F32)


def lift(u):
    x, y = lax.rem(u, 4), lax.div(u, 4)
    return lax.rem(2 * x + 4 * lax.rem(y, 2) + lax.div(y, 2), NZ)


def beside(u):
    x, y = lax.rem(u, 4), lax.div(u, 4)
    other = y + 1 - 2 * lax.rem(y, 2)
    return 4 * y + lax.rem(x + 1, 4), 4 * other + x, 4 * y + lax.rem(x + 3, 4)


def hosted(z, u):
    rel = lax.rem(z - lift(u) + NZ, NZ)
    yes = jnp.logical_or(rel == 0, jnp.logical_or(rel == 3, rel == 6))
    return yes, lax.div(rel, 3)


def remote(src, dst, send, recv, there):
    return pltpu.make_async_remote_copy(
        src_ref=src, dst_ref=dst, send_sem=send, recv_sem=recv,
        device_id=there, device_id_type=MESH,
    )


def arrived(ref, sem):
    pltpu.make_async_copy(ref, ref, sem).wait()


def place():
    blk = lax.axis_index("blk")
    u = lax.axis_index("uly")
    z = lax.div(blk, 2)
    c = lax.rem(blk, 2)
    yes, mine = hosted(z, u)
    return blk, u, z, c, jnp.logical_and(yes, c == lax.rem(mine, 2)), mine


def collect(
    q_in, k_in, v_in, g_in, mask_in, order_ref, kv, qg, picked,
    mask, passing, in_send, kv_sem, qg_sem, mask_sem, pass_sem, pass_send,
):
    blk, u, z, c, is_host, mine = place()
    via = beside(u)
    served = (via[2], via[1], via[0])
    barrier = pltpu.get_barrier_semaphore()

    def greet(there):
        pl.semaphore_signal(barrier, inc=1, device_id=there, device_id_type=MESH)

    get_mask = pltpu.make_async_copy(mask_in, mask, mask_sem)

    @pl.when(is_host)
    def _():
        get_mask.start()

        def greet_line(n, carry):
            greet((lax.rem(blk + n, 2 * NZ), u))
            return carry

        lax.fori_loop(1, 2 * NZ, greet_line, 0)

    for line in served:
        greet((blk, line))

    pl.semaphore_wait(barrier, 3 + 3 - is_host.astype(jnp.int32))

    def inputs(l):
        host = lax.rem(lift(u) + 3 * l, NZ)
        r = lax.rem(z - host + NZ, NZ)
        cols = pl.ds(pl.multiple_of(l * DH, DH), DH)
        there = (2 * host + lax.rem(l, 2), u)
        home = (
            (k_in, kv.at[c, r, 0], kv_sem),
            (v_in, kv.at[c, r, 1], kv_sem),
            (q_in, qg.at[c, r, 0], qg_sem),
            (g_in, qg.at[c, r, 1], qg_sem),
        )
        home = [(src.at[:, cols], dst, sem) for src, dst, sem in home]
        straight = [(src, dst, in_send, sem, there) for src, dst, sem in home]
        around = straight[:1] + [
            (home[n + 1][0], passing.at[n, l], in_send, pass_sem.at[n, l], (blk, via[n]))
            for n in range(3)
        ]
        return host, home, straight, around

    def nth(n, line):
        return lax.rem(z + line + n, 3)

    for part in (slice(0, 1), slice(1, 4)):
        for n in range(3):
            l = nth(n, u)
            host, home, straight, around = inputs(l)

            @pl.when(host != z)
            def _():
                for move in around[part]:
                    remote(*move).start()

            @pl.when(jnp.logical_and(host == z, c != lax.rem(l, 2)))
            def _():
                for move in straight[part]:
                    remote(*move).start()

            @pl.when(jnp.logical_and(host == z, c == lax.rem(l, 2)))
            def _():
                for move in home[part]:
                    pltpu.make_async_copy(*move).start()

    @pl.when(is_host)
    def _():
        row = lax.broadcasted_iota(jnp.int32, (16, 16), 0)
        lane = lax.broadcasted_iota(jnp.int32, (16, 16), 1)
        ident = jnp.zeros((16, 16), jnp.int32)
        for j in range(16):
            ident = jnp.where(row == j, order_ref[2 * lax.rem(z + j % NZ, NZ) + j // NZ], ident)
        hot = jnp.where(lane == ident, 1.0, 0.0).astype(BF16)
        wide = lax.broadcasted_iota(jnp.int32, (16, 128), 1)
        hot_wide = jnp.where(wide == ident[:, :1], 1.0, 0.0).astype(BF16)
        get_mask.wait()
        flat = jnp.where(mask[...] > 0, 1.0, 0.0).reshape(256, H).astype(BF16)
        head = lax.broadcasted_iota(jnp.int32, (H, 128), 0) == 3 * u + mine
        picked_out = nn(flat, jnp.where(head, 1.0, 0.0).astype(BF16))
        tall = lax.broadcasted_iota(jnp.int32, (16, 16, 128), 1)
        across = lax.broadcasted_iota(jnp.int32, (16, 16, 128), 2)
        table = jnp.where(tall == across, picked_out.reshape(16, 16, 128), 0.0)
        table = jnp.sum(table, axis=1).astype(BF16)
        by_query = nn(hot, table).astype(BF16)
        allowed = nt(by_query, hot_wide)
        before = jnp.where(row < lane, 1.0, 0.0).astype(BF16)
        rank = nn(allowed.astype(BF16), before)
        listed = jnp.where(wide == COUNT, jnp.sum(allowed, axis=1, keepdims=True), 0.0)
        for n in range(16):
            here = jnp.logical_and(allowed > 0.5, jnp.abs(rank - n) < 0.5)
            one = jnp.sum(jnp.where(here, lane.astype(F32), 0.0), axis=1, keepdims=True)
            listed = jnp.where(wide == n, one, listed)
        picked[...] = listed.astype(jnp.int32)

    def passed(n, l):
        host = lax.rem(lift(served[n]) + 3 * l, NZ)
        r = lax.rem(z - host + NZ, NZ)
        dst, sem = (
            (kv.at[c, r, 1], kv_sem),
            (qg.at[c, r, 0], qg_sem),
            (qg.at[c, r, 1], qg_sem),
        )[n]
        there = (2 * host + lax.rem(l, 2), served[n])
        return host != z, remote(passing.at[n, l], dst, pass_send.at[n, l], sem, there)

    for i in range(3):
        for n in range(3):
            l = nth(i, served[n])
            on, move = passed(n, l)

            @pl.when(on)
            def _():
                arrived(passing.at[n, l], pass_sem.at[n, l])
                move.start()

    @pl.when(is_host)
    def _():
        arrived(kv, kv_sem)
        arrived(qg, qg_sem)
        arrived(kv.at[0, pl.ds(0, 4)], in_send)

    @pl.when(jnp.logical_not(is_host))
    def _():
        arrived(kv.at[0, pl.ds(0, 6)], in_send)

    for l in range(3):
        for n in range(3):
            on, move = passed(n, l)
            pl.when(on)(move.wait_send)


def gradients(
    kv, qg, picked_in, dq_out, acc,
    picked, item_code, e_buf, d_buf, top_buf, row_top, row_sum, row_mix, dq_acc, sem,
):
    blk, u, z, c, is_host, mine = place()

    @pl.when(is_host)
    def _():
        get = pltpu.make_async_copy(picked_in, picked, sem)
        get.start()
        acc[...] = jnp.zeros_like(acc)
        dq_acc[...] = jnp.zeros_like(dq_acc)
        row_top[...] = jnp.full_like(row_top, -1e30)
        row_sum[...] = jnp.zeros_like(row_sum)
        row_mix[...] = jnp.zeros_like(row_mix)
        get.wait()

        items = jnp.int32(0)
        for r in range(16):
            end = picked[r, COUNT]
            for base in range(0, 16, SLOTS):
                item_code[items] = r * 4096 + base * 64 + end
                items = items + (base < end).astype(jnp.int32)
        for m in range(WIDE - 1):
            item_code[items + m] = EMPTY * 64
        rounds = lax.div(items + WIDE - 1, WIDE)

        def item(i):
            code = item_code[i]
            base = lax.bitwise_and(lax.shift_right_logical(code, 6), 63)
            return lax.shift_right_logical(code, 12), base, lax.bitwise_and(code, 63)

        def tiles(ref, r, base, part):
            return jnp.concatenate(
                [ref[picked[r, base + m], part] for m in range(SLOTS)], axis=0
            )

        def weigh(t, carry):
            for w in range(WIDE):
                i = t * WIDE + w
                r, base, end = item(i)
                scores = nt(tiles(kv, r, base, 0), qg[r, 0]) * (FACTOR * LOG2E)
                scores = jnp.concatenate(
                    [
                        scores[128 * m:128 * m + 128]
                        + jnp.where(base + m < end, 0.0, -1e30)
                        for m in range(SLOTS)
                    ],
                    axis=0,
                )
                top = jnp.max(scores, axis=0, keepdims=True)
                e = jnp.exp2(scores - top)
                dprob = nt(tiles(kv, r, base, 1), qg[r, 1])
                e_buf[i] = e
                d_buf[i] = dprob
                top_buf[i] = top
                total = jnp.sum(e, axis=0, keepdims=True)
                mixed = jnp.sum(e * dprob, axis=0, keepdims=True)
                old = row_top[r]
                new = jnp.maximum(old, top)
                keep = jnp.exp2(old - new)
                part = jnp.exp2(top - new)
                row_top[r] = new
                row_sum[r] = row_sum[r] * keep + total * part
                row_mix[r] = row_mix[r] * keep + mixed * part
            return carry

        lax.fori_loop(0, rounds, weigh, 0)

        def spread(t, carry):
            for w in range(WIDE):
                i = t * WIDE + w
                r, base, _ = item(i)
                whole = 1.0 / row_sum[r]
                prob = e_buf[i] * (jnp.exp2(top_buf[i] - row_top[r]) * whole)
                dscore = (prob * (d_buf[i] - row_mix[r] * whole)).astype(BF16)
                dk = nn(dscore, qg[r, 0])
                dv = nn(prob.astype(BF16), qg[r, 1])
                dq_acc[r] += lax.dot_general(
                    dscore, tiles(kv, r, base, 0), (((0,), (0,)), ((), ())),
                    preferred_element_type=F32,
                )
                for m in range(SLOTS):
                    j = picked[r, base + m]
                    acc[j, 0] += dk[128 * m:128 * m + 128]
                    acc[j, 1] += dv[128 * m:128 * m + 128]
            return carry

        lax.fori_loop(0, rounds, spread, 0)
        dq_out[...] = (dq_acc[...] * FACTOR).astype(BF16)


def give_back(
    dq_in, acc, f_q, f_kv, kv_out, r_q, r_kv, t_q,
    p1q_send, p1k_send, rq_sem, rkv_sem, p2q_send, p2k_send, fq_sem, fkv_sem,
):
    blk, u, z, c, is_host, mine = place()
    seat = mine * 2 + lax.rem(lax.div(u, 4), 2)
    chip_hosts = hosted(z, u)[0]
    passes = [
        jnp.logical_and(jnp.logical_not(is_host), jnp.logical_or(chip_hosts, c == side))
        for side in range(2)
    ]
    barrier = pltpu.get_barrier_semaphore()

    def passer(h, line, side):
        yes, l = hosted(h, line)
        return 2 * h + jnp.where(yes, 1 - lax.rem(l, 2), side), line

    def greet(there):
        @pl.when(jnp.logical_or(there[0] != blk, there[1] != u))
        def _():
            pl.semaphore_signal(barrier, inc=1, device_id=there, device_id_type=MESH)

    def greet_line(h, carry):
        greet(passer(h, u, c))
        return carry

    def greet_plane(n, carry):
        greet(passer(z, lax.rem(u + n, NU), c))
        return carry

    greet_plane(0, 0)

    @pl.when(jnp.logical_not(is_host))
    def _():
        lax.fori_loop(0, NZ, greet_line, 0)
        lax.fori_loop(1, NU, greet_plane, 0)
        for l in range(3):
            greet((2 * lax.rem(lift(u) + 3 * l, NZ) + l % 2, u))
            up = lax.rem(z - 3 * l + 2 * NZ, NZ)
            for half in range(2):
                x = lax.div(lax.rem(up - lax.rem(up, 2) - 4 * half + NZ, NZ), 2)
                greet((2 * z + l % 2, 4 * (2 * lax.rem(up, 2) + half) + x))

    alone = jnp.logical_not(chip_hosts).astype(jnp.int32)
    pl.semaphore_wait(barrier, jnp.where(is_host, 39, 22 + 24 * (1 - alone)))

    @pl.when(is_host)
    def _():
        def stage(h, carry):
            for side in range(2):
                j = NZ * side + lax.rem(h - z + NZ, NZ)
                dk = acc[j, 0] * FACTOR
                dv = acc[j, 1]
                for n in range(NU):
                    piece = jnp.concatenate([dk[8 * n:8 * n + 8], dv[8 * n:8 * n + 8]], axis=0)
                    kv_out[NU * side + n, h] = piece.astype(BF16)
            return carry

        def send_q(h, carry):
            for side in range(2):
                tile = dq_in.at[NZ * side + lax.rem(h - z + NZ, NZ)]
                there = passer(h, u, side)
                remote(tile, r_q.at[side, mine], p1q_send, rq_sem.at[side], there).start()
            return carry

        lax.fori_loop(0, NZ, send_q, 0)
        lax.fori_loop(0, NZ, greet_line, 0)
        lax.fori_loop(1, NU, greet_plane, 0)
        for part in range(2):
            heights = pl.ds(4 * part, 4)

            def send_k(to, carry):
                for side in range(2):
                    remote(
                        kv_out.at[NU * side + to, heights], r_kv.at[side, seat, heights],
                        p1k_send, rkv_sem.at[part, side], passer(z, to, side),
                    ).start()
                return carry

            lax.fori_loop(4 * part, 4 * part + 4, stage, 0)
            lax.fori_loop(0, NU, send_k, 0)

    def pass_q(side):
        arrived(r_q.at[side], rq_sem.at[side])
        heads = [r_q[side, l].astype(F32) for l in range(3)]
        for n in range(NU):
            rows = slice(8 * n, 8 * n + 8)
            both = jnp.concatenate([heads[0][rows], heads[1][rows]], axis=0)
            t_q[side, n, :16] = both.astype(BF16)
            both = jnp.concatenate([heads[2][rows], heads[2][rows]], axis=0)
            t_q[side, n, 16:] = both.astype(BF16)

        def one(to, carry):
            @pl.when(jnp.logical_or(to != u, c != side))
            def _():
                there = (2 * z + side, to)
                remote(t_q.at[side, to], f_q.at[u], p2q_send.at[side], fq_sem, there).start()

            @pl.when(jnp.logical_and(to == u, c == side))
            def _():
                pltpu.make_async_copy(t_q.at[side, to], f_q.at[u], fq_sem).start()

            return carry

        lax.fori_loop(0, NU, one, 0)

    def pass_k(part, side):
        arrived(r_kv.at[side, :, pl.ds(4 * part, 4)], rkv_sem.at[part, side])

        def one(h, carry):
            src = r_kv.at[side, :, h]

            @pl.when(jnp.logical_or(h != z, c != side))
            def _():
                there = (2 * h + side, u)
                remote(src, f_kv.at[z], p2k_send.at[side], fkv_sem, there).start()

            @pl.when(jnp.logical_and(h == z, c == side))
            def _():
                pltpu.make_async_copy(src, f_kv.at[z], fkv_sem).start()

            return carry

        lax.fori_loop(4 * part, 4 * part + 4, one, 0)

    low = z < 2
    for side in range(2):
        on = jnp.logical_and(passes[side], jnp.logical_not(low))
        pl.when(on)(functools.partial(pass_k, 0, side))
    for side in range(2):
        pl.when(passes[side])(functools.partial(pass_q, side))
    for side in range(2):
        pl.when(jnp.logical_and(passes[side], low))(functools.partial(pass_k, 0, side))
    for side in range(2):
        pl.when(passes[side])(functools.partial(pass_k, 1, side))

    @pl.when(is_host)
    def _():
        arrived(dq_in, p1q_send)
        arrived(kv_out, p1k_send)

    for side in range(2):

        @pl.when(jnp.logical_and(passes[side], c == side))
        def _():
            arrived(t_q.at[side, pl.ds(0, NU - 1)], p2q_send.at[side])
            arrived(r_kv.at[side, :, pl.ds(0, NZ - 1)], p2k_send.at[side])

        @pl.when(jnp.logical_and(passes[side], c != side))
        def _():
            arrived(t_q.at[side], p2q_send.at[side])
            arrived(r_kv.at[side], p2k_send.at[side])

    arrived(f_q, fq_sem)
    arrived(f_kv, fkv_sem)


def assemble(f_q, f_kv, q_hbm, k_hbm, v_hbm, out_q, out_k, out_v, sems):
    def columns(head):
        return slice(head * DH, head * DH + DH)

    copies = [
        pltpu.make_async_copy(src, dst, sems.at[n])
        for n, (src, dst) in enumerate(((out_q, q_hbm), (out_k, k_hbm), (out_v, v_hbm)))
    ]
    for n in range(NU):
        first = f_q[n, :16].astype(F32)
        out_q[:, columns(3 * n)] = first[:8].astype(BF16)
        out_q[:, columns(3 * n + 1)] = first[8:].astype(BF16)
        out_q[:, columns(3 * n + 2)] = f_q[n, 16:].astype(F32)[:8].astype(BF16)
    copies[0].start()
    for d in range(NZ):
        for l in range(3):
            for half in range(2):
                both = f_kv[d, 2 * l + half].astype(F32)
                up = (d - 3 * l) % NZ
                x = (up - up % 2 - 4 * half) % NZ // 2
                head = 3 * (4 * (2 * (up % 2) + half) + x) + l
                out_k[:, columns(head)] = both[:8].astype(BF16)
                out_v[:, columns(head)] = both[8:].astype(BF16)
    copies[1].start()
    copies[2].start()
    for copy in copies:
        copy.wait()


def local(query, key, value, grad_out, tile_mask, tile_order):
    anywhere = pl.BlockSpec(memory_space=pl.ANY)
    vmem = pl.BlockSpec(memory_space=pltpu.VMEM)
    smem = pl.BlockSpec(memory_space=pltpu.SMEM)
    dma = pltpu.SemaphoreType.DMA
    shape = jax.ShapeDtypeStruct
    most = 16 * 16 // SLOTS + WIDE
    operands = (query, key, value, grad_out, jnp.transpose(tile_mask, (1, 2, 0)), tile_order)
    kv, qg, picked = pl.pallas_call(
        collect,
        out_shape=(
            shape((2, NZ, 2, 128, 128), BF16),
            shape((2, NZ, 2, 128, 128), BF16),
            shape((16, 128), jnp.int32),
        ),
        in_specs=[anywhere] * 5 + [smem],
        out_specs=(vmem, vmem, vmem),
        scratch_shapes=[
            pltpu.VMEM((16, 16, H), jnp.int32),
            pltpu.VMEM((3, 3, 128, 128), BF16),
            dma, dma, dma, dma, dma((3, 3)), dma((3, 3)),
        ],
        compiler_params=pltpu.CompilerParams(
            collective_id=0, has_side_effects=True, vmem_limit_bytes=16 * 1024 * 1024
        ),
    )(*[pltpu.with_memory_space_constraint(a, pltpu.HBM) for a in operands])
    dq, acc = pl.pallas_call(
        gradients,
        out_shape=(
            shape((16, 128, 128), BF16),
            shape((16, 2, 128, 128), F32),
        ),
        in_specs=[vmem, vmem, anywhere],
        out_specs=(vmem, vmem),
        scratch_shapes=[
            pltpu.SMEM((16, 128), jnp.int32),
            pltpu.SMEM((most,), jnp.int32),
            pltpu.VMEM((most, 128 * SLOTS, 128), F32),
            pltpu.VMEM((most, 128 * SLOTS, 128), F32),
            pltpu.VMEM((most, 1, 128), F32),
            pltpu.VMEM((16, 1, 128), F32),
            pltpu.VMEM((16, 1, 128), F32),
            pltpu.VMEM((16, 1, 128), F32),
            pltpu.VMEM((16, 128, 128), F32),
            dma,
        ],
        compiler_params=pltpu.CompilerParams(vmem_limit_bytes=48 * 1024 * 1024),
    )(kv.reshape(16, 2, 128, 128), qg.reshape(16, 2, 128, 128), picked)
    f_q, f_kv = pl.pallas_call(
        give_back,
        out_shape=(shape((NU, 32, 128), BF16), shape((NZ, 6, 16, 128), BF16)),
        in_specs=[vmem] * 2,
        out_specs=(vmem, vmem),
        scratch_shapes=[
            pltpu.VMEM((2 * NU, NZ, 16, 128), BF16),
            pltpu.VMEM((2, 3, 128, 128), BF16),
            pltpu.VMEM((2, 6, NZ, 16, 128), BF16),
            pltpu.VMEM((2, NU, 32, 128), BF16),
            dma, dma, dma((2,)), dma((2, 2)), dma((2,)), dma((2,)), dma, dma,
        ],
        compiler_params=pltpu.CompilerParams(
            collective_id=1, has_side_effects=True, vmem_limit_bytes=16 * 1024 * 1024
        ),
    )(dq, acc)
    out = shape((8, H * DH), BF16)
    return pl.pallas_call(
        assemble,
        out_shape=(out, out, out),
        in_specs=[vmem] * 2,
        out_specs=(anywhere, anywhere, anywhere),
        scratch_shapes=[pltpu.VMEM((8, H * DH), BF16)] * 3 + [dma((3,))],
        compiler_params=pltpu.CompilerParams(vmem_limit_bytes=8 * 1024 * 1024),
    )(*[pltpu.with_memory_space_constraint(a, pltpu.VMEM) for a in (f_q, f_kv)])


def solution(mesh):
    placed = (P("blk", "uly"), P("blk", "uly"), P("blk", "uly"), P("blk", "uly"), P(), P())
    return jax.shard_map(
        local,
        mesh=mesh,
        in_specs=placed,
        out_specs=(P(("blk", "uly"), None), P(("blk", "uly"), None), P(("blk", "uly"), None)),
        check_vma=False,
    )
```

```python
import functools

import jax
import jax.numpy as jnp
from jax import lax
from jax.experimental import pallas as pl
from jax.experimental.pallas import tpu as pltpu
from jax.sharding import PartitionSpec as P

H = 48
DH = 128
TILE = 128
NZ = 8
NU = 16
SLOTS = 2
WIDE = 6
COUNT = 32
EMPTY = 40
MESH = pl.DeviceIdType.MESH
FACTOR = DH ** -0.5
LOG2E = 1.4426950408889634
F32 = jnp.float32
BF16 = jnp.bfloat16


def nt(a, b):
    return lax.dot_general(a, b, (((1,), (1,)), ((), ())), preferred_element_type=F32)


def nn(a, b):
    return lax.dot_general(a, b, (((1,), (0,)), ((), ())), preferred_element_type=F32)


def lift(u):
    x, y = lax.rem(u, 4), lax.div(u, 4)
    return lax.rem(2 * x + 4 * lax.rem(y, 2) + lax.div(y, 2), NZ)


def beside(u):
    x, y = lax.rem(u, 4), lax.div(u, 4)
    other = y + 1 - 2 * lax.rem(y, 2)
    return 4 * y + lax.rem(x + 1, 4), 4 * other + x, 4 * y + lax.rem(x + 3, 4)


def hosted(z, u):
    rel = lax.rem(z - lift(u) + NZ, NZ)
    yes = jnp.logical_or(rel == 0, jnp.logical_or(rel == 3, rel == 6))
    return yes, lax.div(rel, 3)


def remote(src, dst, send, recv, there):
    return pltpu.make_async_remote_copy(
        src_ref=src, dst_ref=dst, send_sem=send, recv_sem=recv,
        device_id=there, device_id_type=MESH,
    )


def arrived(ref, sem):
    pltpu.make_async_copy(ref, ref, sem).wait()


def place():
    blk = lax.axis_index("blk")
    u = lax.axis_index("uly")
    z = lax.div(blk, 2)
    c = lax.rem(blk, 2)
    yes, mine = hosted(z, u)
    return blk, u, z, c, jnp.logical_and(yes, c == lax.rem(mine, 2)), mine


def collect(
    q_in, k_in, v_in, g_in, mask_in, order_ref, kv, qg, picked,
    mask, passing, in_send, kv_sem, qg_sem, mask_sem, pass_sem, pass_send,
):
    blk, u, z, c, is_host, mine = place()
    via = beside(u)
    served = (via[2], via[1], via[0])
    barrier = pltpu.get_barrier_semaphore()

    def greet(there):
        pl.semaphore_signal(barrier, inc=1, device_id=there, device_id_type=MESH)

    get_mask = pltpu.make_async_copy(mask_in, mask, mask_sem)

    @pl.when(is_host)
    def _():
        get_mask.start()

        def greet_line(n, carry):
            greet((lax.rem(blk + n, 2 * NZ), u))
            return carry

        lax.fori_loop(1, 2 * NZ, greet_line, 0)

    for line in served:
        greet((blk, line))

    pl.semaphore_wait(barrier, 3 + 3 - is_host.astype(jnp.int32))

    def inputs(l):
        host = lax.rem(lift(u) + 3 * l, NZ)
        r = lax.rem(z - host + NZ, NZ)
        cols = pl.ds(pl.multiple_of(l * DH, DH), DH)
        there = (2 * host + lax.rem(l, 2), u)
        home = (
            (k_in, kv.at[c, r, 0], kv_sem),
            (v_in, kv.at[c, r, 1], kv_sem),
            (q_in, qg.at[c, r, 0], qg_sem),
            (g_in, qg.at[c, r, 1], qg_sem),
        )
        home = [(src.at[:, cols], dst, sem) for src, dst, sem in home]
        straight = [(src, dst, in_send, sem, there) for src, dst, sem in home]
        around = straight[:1] + [
            (home[n + 1][0], passing.at[n, l], in_send, pass_sem.at[n, l], (blk, via[n]))
            for n in range(3)
        ]
        return host, home, straight, around

    def nth(n, line):
        return lax.rem(z + line + n, 3)

    for part in (slice(0, 1), slice(1, 4)):
        for n in range(3):
            l = nth(n, u)
            host, home, straight, around = inputs(l)

            @pl.when(host != z)
            def _():
                for move in around[part]:
                    remote(*move).start()

            @pl.when(jnp.logical_and(host == z, c != lax.rem(l, 2)))
            def _():
                for move in straight[part]:
                    remote(*move).start()

            @pl.when(jnp.logical_and(host == z, c == lax.rem(l, 2)))
            def _():
                for move in home[part]:
                    pltpu.make_async_copy(*move).start()

    @pl.when(is_host)
    def _():
        row = lax.broadcasted_iota(jnp.int32, (16, 16), 0)
        lane = lax.broadcasted_iota(jnp.int32, (16, 16), 1)
        ident = jnp.zeros((16, 16), jnp.int32)
        for j in range(16):
            ident = jnp.where(row == j, order_ref[2 * lax.rem(z + j % NZ, NZ) + j // NZ], ident)
        hot = jnp.where(lane == ident, 1.0, 0.0).astype(BF16)
        wide = lax.broadcasted_iota(jnp.int32, (16, 128), 1)
        hot_wide = jnp.where(wide == ident[:, :1], 1.0, 0.0).astype(BF16)
        get_mask.wait()
        flat = jnp.where(mask[...] > 0, 1.0, 0.0).reshape(256, H).astype(BF16)
        head = lax.broadcasted_iota(jnp.int32, (H, 128), 0) == 3 * u + mine
        picked_out = nn(flat, jnp.where(head, 1.0, 0.0).astype(BF16))
        tall = lax.broadcasted_iota(jnp.int32, (16, 16, 128), 1)
        across = lax.broadcasted_iota(jnp.int32, (16, 16, 128), 2)
        table = jnp.where(tall == across, picked_out.reshape(16, 16, 128), 0.0)
        table = jnp.sum(table, axis=1).astype(BF16)
        by_query = nn(hot, table).astype(BF16)
        allowed = nt(by_query, hot_wide)
        before = jnp.where(row < lane, 1.0, 0.0).astype(BF16)
        rank = nn(allowed.astype(BF16), before)
        listed = jnp.where(wide == COUNT, jnp.sum(allowed, axis=1, keepdims=True), 0.0)
        for n in range(16):
            here = jnp.logical_and(allowed > 0.5, jnp.abs(rank - n) < 0.5)
            one = jnp.sum(jnp.where(here, lane.astype(F32), 0.0), axis=1, keepdims=True)
            listed = jnp.where(wide == n, one, listed)
        picked[...] = listed.astype(jnp.int32)

    def passed(n, l):
        host = lax.rem(lift(served[n]) + 3 * l, NZ)
        r = lax.rem(z - host + NZ, NZ)
        dst, sem = (
            (kv.at[c, r, 1], kv_sem),
            (qg.at[c, r, 0], qg_sem),
            (qg.at[c, r, 1], qg_sem),
        )[n]
        there = (2 * host + lax.rem(l, 2), served[n])
        return host != z, remote(passing.at[n, l], dst, pass_send.at[n, l], sem, there)

    for i in range(3):
        for n in range(3):
            l = nth(i, served[n])
            on, move = passed(n, l)

            @pl.when(on)
            def _():
                arrived(passing.at[n, l], pass_sem.at[n, l])
                move.start()

    @pl.when(is_host)
    def _():
        arrived(kv, kv_sem)
        arrived(qg, qg_sem)
        arrived(kv.at[0, pl.ds(0, 4)], in_send)

    @pl.when(jnp.logical_not(is_host))
    def _():
        arrived(kv.at[0, pl.ds(0, 6)], in_send)

    for l in range(3):
        for n in range(3):
            on, move = passed(n, l)
            pl.when(on)(move.wait_send)


def gradients(
    kv, qg, picked_in, dq_out, acc,
    picked, item_code, e_buf, d_buf, top_buf, row_top, row_sum, row_mix, dq_acc, sem,
):
    blk, u, z, c, is_host, mine = place()

    @pl.when(is_host)
    def _():
        get = pltpu.make_async_copy(picked_in, picked, sem)
        get.start()
        acc[...] = jnp.zeros_like(acc)
        dq_acc[...] = jnp.zeros_like(dq_acc)
        row_top[...] = jnp.full_like(row_top, -1e30)
        row_sum[...] = jnp.zeros_like(row_sum)
        row_mix[...] = jnp.zeros_like(row_mix)
        get.wait()

        items = jnp.int32(0)
        for r in range(16):
            end = picked[r, COUNT]
            for base in range(0, 16, SLOTS):
                item_code[items] = r * 4096 + base * 64 + end
                items = items + (base < end).astype(jnp.int32)
        for m in range(WIDE - 1):
            item_code[items + m] = EMPTY * 64
        rounds = lax.div(items + WIDE - 1, WIDE)

        def item(i):
            code = item_code[i]
            base = lax.bitwise_and(lax.shift_right_logical(code, 6), 63)
            return lax.shift_right_logical(code, 12), base, lax.bitwise_and(code, 63)

        def tiles(ref, r, base, part):
            return jnp.concatenate(
                [ref[picked[r, base + m], part] for m in range(SLOTS)], axis=0
            )

        def weigh(t, carry):
            for w in range(WIDE):
                i = t * WIDE + w
                r, base, end = item(i)
                scores = nt(tiles(kv, r, base, 0), qg[r, 0]) * (FACTOR * LOG2E)
                scores = jnp.concatenate(
                    [
                        scores[128 * m:128 * m + 128]
                        + jnp.where(base + m < end, 0.0, -1e30)
                        for m in range(SLOTS)
                    ],
                    axis=0,
                )
                top = jnp.max(scores, axis=0, keepdims=True)
                e = jnp.exp2(scores - top)
                dprob = nt(tiles(kv, r, base, 1), qg[r, 1])
                e_buf[i] = e
                d_buf[i] = dprob
                top_buf[i] = top
                total = jnp.sum(e, axis=0, keepdims=True)
                mixed = jnp.sum(e * dprob, axis=0, keepdims=True)
                old = row_top[r]
                new = jnp.maximum(old, top)
                keep = jnp.exp2(old - new)
                part = jnp.exp2(top - new)
                row_top[r] = new
                row_sum[r] = row_sum[r] * keep + total * part
                row_mix[r] = row_mix[r] * keep + mixed * part
            return carry

        lax.fori_loop(0, rounds, weigh, 0)

        def spread(t, carry):
            for w in range(WIDE):
                i = t * WIDE + w
                r, base, _ = item(i)
                whole = 1.0 / row_sum[r]
                prob = e_buf[i] * (jnp.exp2(top_buf[i] - row_top[r]) * whole)
                dscore = (prob * (d_buf[i] - row_mix[r] * whole)).astype(BF16)
                dk = nn(dscore, qg[r, 0])
                dv = nn(prob.astype(BF16), qg[r, 1])
                dq_acc[r] += lax.dot_general(
                    dscore, tiles(kv, r, base, 0), (((0,), (0,)), ((), ())),
                    preferred_element_type=F32,
                )
                for m in range(SLOTS):
                    j = picked[r, base + m]
                    acc[j, 0] += dk[128 * m:128 * m + 128]
                    acc[j, 1] += dv[128 * m:128 * m + 128]
            return carry

        lax.fori_loop(0, rounds, spread, 0)
        dq_out[...] = (dq_acc[...] * FACTOR).astype(BF16)


def give_back(
    dq_in, acc, f_q, f_kv, kv_out, r_q, r_kv, t_q,
    p1q_send, p1k_send, rq_sem, rkv_sem, p2q_send, p2k_send, fq_sem, fkv_sem,
):
    blk, u, z, c, is_host, mine = place()
    seat = mine * 2 + lax.rem(lax.div(u, 4), 2)
    chip_hosts = hosted(z, u)[0]
    passes = [
        jnp.logical_and(jnp.logical_not(is_host), jnp.logical_or(chip_hosts, c == side))
        for side in range(2)
    ]
    barrier = pltpu.get_barrier_semaphore()

    def passer(h, line, side):
        yes, l = hosted(h, line)
        return 2 * h + jnp.where(yes, 1 - lax.rem(l, 2), side), line

    def greet(there):
        @pl.when(jnp.logical_or(there[0] != blk, there[1] != u))
        def _():
            pl.semaphore_signal(barrier, inc=1, device_id=there, device_id_type=MESH)

    def greet_line(h, carry):
        greet(passer(h, u, c))
        return carry

    def greet_plane(n, carry):
        greet(passer(z, lax.rem(u + n, NU), c))
        return carry

    greet_plane(0, 0)

    @pl.when(jnp.logical_not(is_host))
    def _():
        lax.fori_loop(0, NZ, greet_line, 0)
        lax.fori_loop(1, NU, greet_plane, 0)
        for l in range(3):
            greet((2 * lax.rem(lift(u) + 3 * l, NZ) + l % 2, u))
            up = lax.rem(z - 3 * l + 2 * NZ, NZ)
            for half in range(2):
                x = lax.div(lax.rem(up - lax.rem(up, 2) - 4 * half + NZ, NZ), 2)
                greet((2 * z + l % 2, 4 * (2 * lax.rem(up, 2) + half) + x))

    alone = jnp.logical_not(chip_hosts).astype(jnp.int32)
    pl.semaphore_wait(barrier, jnp.where(is_host, 39, 22 + 24 * (1 - alone)))

    @pl.when(is_host)
    def _():
        def stage(h, carry):
            for side in range(2):
                j = NZ * side + lax.rem(h - z + NZ, NZ)
                dk = acc[j, 0] * FACTOR
                dv = acc[j, 1]
                for n in range(NU):
                    piece = jnp.concatenate([dk[8 * n:8 * n + 8], dv[8 * n:8 * n + 8]], axis=0)
                    kv_out[NU * side + n, h] = piece.astype(BF16)
            return carry

        def send_q(h, carry):
            for side in range(2):
                tile = dq_in.at[NZ * side + lax.rem(h - z + NZ, NZ)]
                there = passer(h, u, side)
                remote(tile, r_q.at[side, mine], p1q_send, rq_sem.at[side], there).start()
            return carry

        for part in range(2):
            heights = pl.ds(4 * part, 4)
            lax.fori_loop(4 * part, 4 * part + 4, send_q, 0)
            if part == 0:
                lax.fori_loop(0, NZ, greet_line, 0)
                lax.fori_loop(1, NU, greet_plane, 0)

            def send_k(to, carry):
                for side in range(2):
                    remote(
                        kv_out.at[NU * side + to, heights], r_kv.at[side, seat, heights],
                        p1k_send, rkv_sem.at[part, side], passer(z, to, side),
                    ).start()
                return carry

            lax.fori_loop(4 * part, 4 * part + 4, stage, 0)
            lax.fori_loop(0, NU, send_k, 0)

    def pass_q(side):
        arrived(r_q.at[side], rq_sem.at[side])
        heads = [r_q[side, l].astype(F32) for l in range(3)]
        for n in range(NU):
            rows = slice(8 * n, 8 * n + 8)
            both = jnp.concatenate([heads[0][rows], heads[1][rows]], axis=0)
            t_q[side, n, :16] = both.astype(BF16)
            both = jnp.concatenate([heads[2][rows], heads[2][rows]], axis=0)
            t_q[side, n, 16:] = both.astype(BF16)

        def one(to, carry):
            @pl.when(jnp.logical_or(to != u, c != side))
            def _():
                there = (2 * z + side, to)
                remote(t_q.at[side, to], f_q.at[u], p2q_send.at[side], fq_sem, there).start()

            @pl.when(jnp.logical_and(to == u, c == side))
            def _():
                pltpu.make_async_copy(t_q.at[side, to], f_q.at[u], fq_sem).start()

            return carry

        lax.fori_loop(0, NU, one, 0)

    def pass_k(part, side):
        arrived(r_kv.at[side, :, pl.ds(4 * part, 4)], rkv_sem.at[part, side])

        def one(h, carry):
            src = r_kv.at[side, :, h]

            @pl.when(jnp.logical_or(h != z, c != side))
            def _():
                there = (2 * h + side, u)
                remote(src, f_kv.at[z], p2k_send.at[side], fkv_sem, there).start()

            @pl.when(jnp.logical_and(h == z, c == side))
            def _():
                pltpu.make_async_copy(src, f_kv.at[z], fkv_sem).start()

            return carry

        lax.fori_loop(4 * part, 4 * part + 4, one, 0)

    low = z < 2
    for side in range(2):
        on = jnp.logical_and(passes[side], jnp.logical_not(low))
        pl.when(on)(functools.partial(pass_k, 0, side))
    for side in range(2):
        pl.when(passes[side])(functools.partial(pass_q, side))
    for side in range(2):
        pl.when(jnp.logical_and(passes[side], low))(functools.partial(pass_k, 0, side))
    for side in range(2):
        pl.when(passes[side])(functools.partial(pass_k, 1, side))

    @pl.when(is_host)
    def _():
        arrived(dq_in, p1q_send)
        arrived(kv_out, p1k_send)

    for side in range(2):

        @pl.when(jnp.logical_and(passes[side], c == side))
        def _():
            arrived(t_q.at[side, pl.ds(0, NU - 1)], p2q_send.at[side])
            arrived(r_kv.at[side, :, pl.ds(0, NZ - 1)], p2k_send.at[side])

        @pl.when(jnp.logical_and(passes[side], c != side))
        def _():
            arrived(t_q.at[side], p2q_send.at[side])
            arrived(r_kv.at[side], p2k_send.at[side])

    arrived(f_q, fq_sem)
    arrived(f_kv, fkv_sem)


def assemble(f_q, f_kv, q_hbm, k_hbm, v_hbm, out_q, out_k, out_v, sems):
    def columns(head):
        return slice(head * DH, head * DH + DH)

    copies = [
        pltpu.make_async_copy(src, dst, sems.at[n])
        for n, (src, dst) in enumerate(((out_q, q_hbm), (out_k, k_hbm), (out_v, v_hbm)))
    ]
    for n in range(NU):
        first = f_q[n, :16].astype(F32)
        out_q[:, columns(3 * n)] = first[:8].astype(BF16)
        out_q[:, columns(3 * n + 1)] = first[8:].astype(BF16)
        out_q[:, columns(3 * n + 2)] = f_q[n, 16:].astype(F32)[:8].astype(BF16)
    copies[0].start()
    for d in range(NZ):
        for l in range(3):
            for half in range(2):
                both = f_kv[d, 2 * l + half].astype(F32)
                up = (d - 3 * l) % NZ
                x = (up - up % 2 - 4 * half) % NZ // 2
                head = 3 * (4 * (2 * (up % 2) + half) + x) + l
                out_k[:, columns(head)] = both[:8].astype(BF16)
                out_v[:, columns(head)] = both[8:].astype(BF16)
    copies[1].start()
    copies[2].start()
    for copy in copies:
        copy.wait()


def local(query, key, value, grad_out, tile_mask, tile_order):
    anywhere = pl.BlockSpec(memory_space=pl.ANY)
    vmem = pl.BlockSpec(memory_space=pltpu.VMEM)
    smem = pl.BlockSpec(memory_space=pltpu.SMEM)
    dma = pltpu.SemaphoreType.DMA
    shape = jax.ShapeDtypeStruct
    most = 16 * 16 // SLOTS + WIDE
    operands = (query, key, value, grad_out, jnp.transpose(tile_mask, (1, 2, 0)), tile_order)
    kv, qg, picked = pl.pallas_call(
        collect,
        out_shape=(
            shape((2, NZ, 2, 128, 128), BF16),
            shape((2, NZ, 2, 128, 128), BF16),
            shape((16, 128), jnp.int32),
        ),
        in_specs=[anywhere] * 5 + [smem],
        out_specs=(vmem, vmem, vmem),
        scratch_shapes=[
            pltpu.VMEM((16, 16, H), jnp.int32),
            pltpu.VMEM((3, 3, 128, 128), BF16),
            dma, dma, dma, dma, dma((3, 3)), dma((3, 3)),
        ],
        compiler_params=pltpu.CompilerParams(
            collective_id=0, has_side_effects=True, vmem_limit_bytes=16 * 1024 * 1024
        ),
    )(*[pltpu.with_memory_space_constraint(a, pltpu.HBM) for a in operands])
    dq, acc = pl.pallas_call(
        gradients,
        out_shape=(
            shape((16, 128, 128), BF16),
            shape((16, 2, 128, 128), F32),
        ),
        in_specs=[vmem, vmem, anywhere],
        out_specs=(vmem, vmem),
        scratch_shapes=[
            pltpu.SMEM((16, 128), jnp.int32),
            pltpu.SMEM((most,), jnp.int32),
            pltpu.VMEM((most, 128 * SLOTS, 128), F32),
            pltpu.VMEM((most, 128 * SLOTS, 128), F32),
            pltpu.VMEM((most, 1, 128), F32),
            pltpu.VMEM((16, 1, 128), F32),
            pltpu.VMEM((16, 1, 128), F32),
            pltpu.VMEM((16, 1, 128), F32),
            pltpu.VMEM((16, 128, 128), F32),
            dma,
        ],
        compiler_params=pltpu.CompilerParams(vmem_limit_bytes=48 * 1024 * 1024),
    )(kv.reshape(16, 2, 128, 128), qg.reshape(16, 2, 128, 128), picked)
    f_q, f_kv = pl.pallas_call(
        give_back,
        out_shape=(shape((NU, 32, 128), BF16), shape((NZ, 6, 16, 128), BF16)),
        in_specs=[vmem] * 2,
        out_specs=(vmem, vmem),
        scratch_shapes=[
            pltpu.VMEM((2 * NU, NZ, 16, 128), BF16),
            pltpu.VMEM((2, 3, 128, 128), BF16),
            pltpu.VMEM((2, 6, NZ, 16, 128), BF16),
            pltpu.VMEM((2, NU, 32, 128), BF16),
            dma, dma, dma((2,)), dma((2, 2)), dma((2,)), dma((2,)), dma, dma,
        ],
        compiler_params=pltpu.CompilerParams(
            collective_id=1, has_side_effects=True, vmem_limit_bytes=16 * 1024 * 1024
        ),
    )(dq, acc)
    out = shape((8, H * DH), BF16)
    return pl.pallas_call(
        assemble,
        out_shape=(out, out, out),
        in_specs=[vmem] * 2,
        out_specs=(anywhere, anywhere, anywhere),
        scratch_shapes=[pltpu.VMEM((8, H * DH), BF16)] * 3 + [dma((3,))],
        compiler_params=pltpu.CompilerParams(vmem_limit_bytes=8 * 1024 * 1024),
    )(*[pltpu.with_memory_space_constraint(a, pltpu.VMEM) for a in (f_q, f_kv)])


def solution(mesh):
    placed = (P("blk", "uly"), P("blk", "uly"), P("blk", "uly"), P("blk", "uly"), P(), P())
    return jax.shard_map(
        local,
        mesh=mesh,
        in_specs=placed,
        out_specs=(P(("blk", "uly"), None), P(("blk", "uly"), None), P(("blk", "uly"), None)),
        check_vma=False,
    )
```

```python
import functools

import jax
import jax.numpy as jnp
from jax import lax
from jax.experimental import pallas as pl
from jax.experimental.pallas import tpu as pltpu
from jax.sharding import PartitionSpec as P

H = 48
DH = 128
TILE = 128
NZ = 8
NU = 16
SLOTS = 2
WIDE = 4
COUNT = 32
EMPTY = 40
MESH = pl.DeviceIdType.MESH
FACTOR = DH ** -0.5
LOG2E = 1.4426950408889634
F32 = jnp.float32
BF16 = jnp.bfloat16


def nt(a, b):
    return lax.dot_general(a, b, (((1,), (1,)), ((), ())), preferred_element_type=F32)


def nn(a, b):
    return lax.dot_general(a, b, (((1,), (0,)), ((), ())), preferred_element_type=F32)


def lift(u):
    x, y = lax.rem(u, 4), lax.div(u, 4)
    return lax.rem(2 * x + 4 * lax.rem(y, 2) + lax.div(y, 2), NZ)


def beside(u):
    x, y = lax.rem(u, 4), lax.div(u, 4)
    other = y + 1 - 2 * lax.rem(y, 2)
    return 4 * y + lax.rem(x + 1, 4), 4 * other + x, 4 * y + lax.rem(x + 3, 4)


def hosted(z, u):
    rel = lax.rem(z - lift(u) + NZ, NZ)
    yes = jnp.logical_or(rel == 0, jnp.logical_or(rel == 3, rel == 6))
    return yes, lax.div(rel, 3)


def remote(src, dst, send, recv, there):
    return pltpu.make_async_remote_copy(
        src_ref=src, dst_ref=dst, send_sem=send, recv_sem=recv,
        device_id=there, device_id_type=MESH,
    )


def arrived(ref, sem):
    pltpu.make_async_copy(ref, ref, sem).wait()


def place():
    blk = lax.axis_index("blk")
    u = lax.axis_index("uly")
    z = lax.div(blk, 2)
    c = lax.rem(blk, 2)
    yes, mine = hosted(z, u)
    return blk, u, z, c, jnp.logical_and(yes, c == lax.rem(mine, 2)), mine


def collect(
    q_in, k_in, v_in, g_in, mask_in, order_ref, kv, qg, picked,
    mask, passing, in_send, kv_sem, qg_sem, mask_sem, pass_sem, pass_send,
):
    blk, u, z, c, is_host, mine = place()
    via = beside(u)
    served = (via[2], via[1], via[0])
    barrier = pltpu.get_barrier_semaphore()

    def greet(there):
        pl.semaphore_signal(barrier, inc=1, device_id=there, device_id_type=MESH)

    get_mask = pltpu.make_async_copy(mask_in, mask, mask_sem)

    @pl.when(is_host)
    def _():
        get_mask.start()

        def greet_line(n, carry):
            greet((lax.rem(blk + n, 2 * NZ), u))
            return carry

        lax.fori_loop(1, 2 * NZ, greet_line, 0)

    for line in served:
        greet((blk, line))

    pl.semaphore_wait(barrier, 3 + 3 - is_host.astype(jnp.int32))

    def inputs(l):
        host = lax.rem(lift(u) + 3 * l, NZ)
        r = lax.rem(z - host + NZ, NZ)
        cols = pl.ds(pl.multiple_of(l * DH, DH), DH)
        there = (2 * host + lax.rem(l, 2), u)
        home = (
            (k_in, kv.at[c, r, 0], kv_sem),
            (v_in, kv.at[c, r, 1], kv_sem),
            (q_in, qg.at[c, r, 0], qg_sem),
            (g_in, qg.at[c, r, 1], qg_sem),
        )
        home = [(src.at[:, cols], dst, sem) for src, dst, sem in home]
        straight = [(src, dst, in_send, sem, there) for src, dst, sem in home]
        around = straight[:1] + [
            (home[n + 1][0], passing.at[n, l], in_send, pass_sem.at[n, l], (blk, via[n]))
            for n in range(3)
        ]
        return host, home, straight, around

    def nth(n, line):
        return lax.rem(z + line + n, 3)

    for part in (slice(0, 1), slice(1, 4)):
        for n in range(3):
            l = nth(n, u)
            host, home, straight, around = inputs(l)

            @pl.when(host != z)
            def _():
                for move in around[part]:
                    remote(*move).start()

            @pl.when(jnp.logical_and(host == z, c != lax.rem(l, 2)))
            def _():
                for move in straight[part]:
                    remote(*move).start()

            @pl.when(jnp.logical_and(host == z, c == lax.rem(l, 2)))
            def _():
                for move in home[part]:
                    pltpu.make_async_copy(*move).start()

    @pl.when(is_host)
    def _():
        row = lax.broadcasted_iota(jnp.int32, (16, 16), 0)
        lane = lax.broadcasted_iota(jnp.int32, (16, 16), 1)
        ident = jnp.zeros((16, 16), jnp.int32)
        for j in range(16):
            ident = jnp.where(row == j, order_ref[2 * lax.rem(z + j % NZ, NZ) + j // NZ], ident)
        hot = jnp.where(lane == ident, 1.0, 0.0).astype(BF16)
        wide = lax.broadcasted_iota(jnp.int32, (16, 128), 1)
        hot_wide = jnp.where(wide == ident[:, :1], 1.0, 0.0).astype(BF16)
        get_mask.wait()
        flat = jnp.where(mask[...] > 0, 1.0, 0.0).reshape(256, H).astype(BF16)
        head = lax.broadcasted_iota(jnp.int32, (H, 128), 0) == 3 * u + mine
        picked_out = nn(flat, jnp.where(head, 1.0, 0.0).astype(BF16))
        tall = lax.broadcasted_iota(jnp.int32, (16, 16, 128), 1)
        across = lax.broadcasted_iota(jnp.int32, (16, 16, 128), 2)
        table = jnp.where(tall == across, picked_out.reshape(16, 16, 128), 0.0)
        table = jnp.sum(table, axis=1).astype(BF16)
        by_query = nn(hot, table).astype(BF16)
        allowed = nt(by_query, hot_wide)
        before = jnp.where(row < lane, 1.0, 0.0).astype(BF16)
        rank = nn(allowed.astype(BF16), before)
        listed = jnp.where(wide == COUNT, jnp.sum(allowed, axis=1, keepdims=True), 0.0)
        for n in range(16):
            here = jnp.logical_and(allowed > 0.5, jnp.abs(rank - n) < 0.5)
            one = jnp.sum(jnp.where(here, lane.astype(F32), 0.0), axis=1, keepdims=True)
            listed = jnp.where(wide == n, one, listed)
        picked[...] = listed.astype(jnp.int32)

    def passed(n, l):
        host = lax.rem(lift(served[n]) + 3 * l, NZ)
        r = lax.rem(z - host + NZ, NZ)
        dst, sem = (
            (kv.at[c, r, 1], kv_sem),
            (qg.at[c, r, 0], qg_sem),
            (qg.at[c, r, 1], qg_sem),
        )[n]
        there = (2 * host + lax.rem(l, 2), served[n])
        return host != z, remote(passing.at[n, l], dst, pass_send.at[n, l], sem, there)

    for i in range(3):
        for n in range(3):
            l = nth(i, served[n])
            on, move = passed(n, l)

            @pl.when(on)
            def _():
                arrived(passing.at[n, l], pass_sem.at[n, l])
                move.start()

    @pl.when(is_host)
    def _():
        arrived(kv, kv_sem)
        arrived(qg, qg_sem)
        arrived(kv.at[0, pl.ds(0, 4)], in_send)

    @pl.when(jnp.logical_not(is_host))
    def _():
        arrived(kv.at[0, pl.ds(0, 6)], in_send)

    for l in range(3):
        for n in range(3):
            on, move = passed(n, l)
            pl.when(on)(move.wait_send)


def gradients(
    kv, qg, picked_in, dq_out, acc,
    picked, item_code, e_buf, d_buf, top_buf, row_top, row_sum, row_mix, dq_acc, sem,
):
    blk, u, z, c, is_host, mine = place()

    @pl.when(is_host)
    def _():
        get = pltpu.make_async_copy(picked_in, picked, sem)
        get.start()
        acc[...] = jnp.zeros_like(acc)
        dq_acc[...] = jnp.zeros_like(dq_acc)
        row_top[...] = jnp.full_like(row_top, -1e30)
        row_sum[...] = jnp.zeros_like(row_sum)
        row_mix[...] = jnp.zeros_like(row_mix)
        get.wait()

        items = jnp.int32(0)
        for r in range(16):
            end = picked[r, COUNT]
            for base in range(0, 16, SLOTS):
                item_code[items] = r * 4096 + base * 64 + end
                items = items + (base < end).astype(jnp.int32)
        for m in range(WIDE - 1):
            item_code[items + m] = EMPTY * 64
        rounds = lax.div(items + WIDE - 1, WIDE)

        def item(i):
            code = item_code[i]
            base = lax.bitwise_and(lax.shift_right_logical(code, 6), 63)
            return lax.shift_right_logical(code, 12), base, lax.bitwise_and(code, 63)

        def tiles(ref, r, base, part):
            return jnp.concatenate(
                [ref[picked[r, base + m], part] for m in range(SLOTS)], axis=0
            )

        def weigh(t, carry):
            for w in range(WIDE):
                i = t * WIDE + w
                r, base, end = item(i)
                scores = nt(tiles(kv, r, base, 0), qg[r, 0]) * (FACTOR * LOG2E)
                scores = jnp.concatenate(
                    [
                        scores[128 * m:128 * m + 128]
                        + jnp.where(base + m < end, 0.0, -1e30)
                        for m in range(SLOTS)
                    ],
                    axis=0,
                )
                top = jnp.max(scores, axis=0, keepdims=True)
                e = jnp.exp2(scores - top)
                dprob = nt(tiles(kv, r, base, 1), qg[r, 1])
                e_buf[i] = e
                d_buf[i] = dprob
                top_buf[i] = top
                total = jnp.sum(e, axis=0, keepdims=True)
                mixed = jnp.sum(e * dprob, axis=0, keepdims=True)
                old = row_top[r]
                new = jnp.maximum(old, top)
                keep = jnp.exp2(old - new)
                part = jnp.exp2(top - new)
                row_top[r] = new
                row_sum[r] = row_sum[r] * keep + total * part
                row_mix[r] = row_mix[r] * keep + mixed * part
            return carry

        lax.fori_loop(0, rounds, weigh, 0)

        def spread(t, carry):
            for w in range(WIDE):
                i = t * WIDE + w
                r, base, _ = item(i)
                whole = 1.0 / row_sum[r]
                prob = e_buf[i] * (jnp.exp2(top_buf[i] - row_top[r]) * whole)
                dscore = (prob * (d_buf[i] - row_mix[r] * whole)).astype(BF16)
                dk = nn(dscore, qg[r, 0])
                dv = nn(prob.astype(BF16), qg[r, 1])
                dq_acc[r] += lax.dot_general(
                    dscore, tiles(kv, r, base, 0), (((0,), (0,)), ((), ())),
                    preferred_element_type=F32,
                )
                for m in range(SLOTS):
                    j = picked[r, base + m]
                    acc[j, 0] += dk[128 * m:128 * m + 128]
                    acc[j, 1] += dv[128 * m:128 * m + 128]
            return carry

        lax.fori_loop(0, rounds, spread, 0)
        dq_out[...] = (dq_acc[...] * FACTOR).astype(BF16)


def give_back(
    dq_in, acc, f_q, f_kv, kv_out, r_q, r_kv, t_q,
    p1q_send, p1k_send, rq_sem, rkv_sem, p2q_send, p2k_send, fq_sem, fkv_sem,
):
    blk, u, z, c, is_host, mine = place()
    seat = mine * 2 + lax.rem(lax.div(u, 4), 2)
    chip_hosts = hosted(z, u)[0]
    passes = [
        jnp.logical_and(jnp.logical_not(is_host), jnp.logical_or(chip_hosts, c == side))
        for side in range(2)
    ]
    barrier = pltpu.get_barrier_semaphore()

    def passer(h, line, side):
        yes, l = hosted(h, line)
        return 2 * h + jnp.where(yes, 1 - lax.rem(l, 2), side), line

    def greet(there):
        @pl.when(jnp.logical_or(there[0] != blk, there[1] != u))
        def _():
            pl.semaphore_signal(barrier, inc=1, device_id=there, device_id_type=MESH)

    def greet_line(h, carry):
        greet(passer(h, u, c))
        return carry

    def greet_plane(n, carry):
        greet(passer(z, lax.rem(u + n, NU), c))
        return carry

    greet_plane(0, 0)

    @pl.when(jnp.logical_not(is_host))
    def _():
        lax.fori_loop(0, NZ, greet_line, 0)
        lax.fori_loop(1, NU, greet_plane, 0)
        for l in range(3):
            greet((2 * lax.rem(lift(u) + 3 * l, NZ) + l % 2, u))
            up = lax.rem(z - 3 * l + 2 * NZ, NZ)
            for half in range(2):
                x = lax.div(lax.rem(up - lax.rem(up, 2) - 4 * half + NZ, NZ), 2)
                greet((2 * z + l % 2, 4 * (2 * lax.rem(up, 2) + half) + x))

    alone = jnp.logical_not(chip_hosts).astype(jnp.int32)
    pl.semaphore_wait(barrier, jnp.where(is_host, 39, 22 + 24 * (1 - alone)))

    @pl.when(is_host)
    def _():
        def stage(h, carry):
            for side in range(2):
                j = NZ * side + lax.rem(h - z + NZ, NZ)
                dk = acc[j, 0] * FACTOR
                dv = acc[j, 1]
                for n in range(NU):
                    piece = jnp.concatenate([dk[8 * n:8 * n + 8], dv[8 * n:8 * n + 8]], axis=0)
                    kv_out[NU * side + n, h] = piece.astype(BF16)
            return carry

        def send_q(h, carry):
            for side in range(2):
                tile = dq_in.at[NZ * side + lax.rem(h - z + NZ, NZ)]
                there = passer(h, u, side)
                remote(tile, r_q.at[side, mine], p1q_send, rq_sem.at[side], there).start()
            return carry

        for part in range(2):
            heights = pl.ds(4 * part, 4)
            lax.fori_loop(4 * part, 4 * part + 4, send_q, 0)
            if part == 0:
                lax.fori_loop(0, NZ, greet_line, 0)
                lax.fori_loop(1, NU, greet_plane, 0)

            def send_k(to, carry):
                for side in range(2):
                    remote(
                        kv_out.at[NU * side + to, heights], r_kv.at[side, seat, heights],
                        p1k_send, rkv_sem.at[part, side], passer(z, to, side),
                    ).start()
                return carry

            lax.fori_loop(4 * part, 4 * part + 4, stage, 0)
            lax.fori_loop(0, NU, send_k, 0)

    def pass_q(side):
        arrived(r_q.at[side], rq_sem.at[side])
        heads = [r_q[side, l].astype(F32) for l in range(3)]
        for n in range(NU):
            rows = slice(8 * n, 8 * n + 8)
            both = jnp.concatenate([heads[0][rows], heads[1][rows]], axis=0)
            t_q[side, n, :16] = both.astype(BF16)
            both = jnp.concatenate([heads[2][rows], heads[2][rows]], axis=0)
            t_q[side, n, 16:] = both.astype(BF16)

        def one(to, carry):
            @pl.when(jnp.logical_or(to != u, c != side))
            def _():
                there = (2 * z + side, to)
                remote(t_q.at[side, to], f_q.at[u], p2q_send.at[side], fq_sem, there).start()

            @pl.when(jnp.logical_and(to == u, c == side))
            def _():
                pltpu.make_async_copy(t_q.at[side, to], f_q.at[u], fq_sem).start()

            return carry

        lax.fori_loop(0, NU, one, 0)

    def pass_k(part, side):
        arrived(r_kv.at[side, :, pl.ds(4 * part, 4)], rkv_sem.at[part, side])

        def one(h, carry):
            src = r_kv.at[side, :, h]

            @pl.when(jnp.logical_or(h != z, c != side))
            def _():
                there = (2 * h + side, u)
                remote(src, f_kv.at[z], p2k_send.at[side], fkv_sem, there).start()

            @pl.when(jnp.logical_and(h == z, c == side))
            def _():
                pltpu.make_async_copy(src, f_kv.at[z], fkv_sem).start()

            return carry

        lax.fori_loop(4 * part, 4 * part + 4, one, 0)

    low = z < 2
    for side in range(2):
        on = jnp.logical_and(passes[side], jnp.logical_not(low))
        pl.when(on)(functools.partial(pass_k, 0, side))
    for side in range(2):
        pl.when(passes[side])(functools.partial(pass_q, side))
    for side in range(2):
        pl.when(jnp.logical_and(passes[side], low))(functools.partial(pass_k, 0, side))
    for side in range(2):
        pl.when(passes[side])(functools.partial(pass_k, 1, side))

    @pl.when(is_host)
    def _():
        arrived(dq_in, p1q_send)
        arrived(kv_out, p1k_send)

    for side in range(2):

        @pl.when(jnp.logical_and(passes[side], c == side))
        def _():
            arrived(t_q.at[side, pl.ds(0, NU - 1)], p2q_send.at[side])
            arrived(r_kv.at[side, :, pl.ds(0, NZ - 1)], p2k_send.at[side])

        @pl.when(jnp.logical_and(passes[side], c != side))
        def _():
            arrived(t_q.at[side], p2q_send.at[side])
            arrived(r_kv.at[side], p2k_send.at[side])

    arrived(f_q, fq_sem)
    arrived(f_kv, fkv_sem)


def assemble(f_q, f_kv, q_hbm, k_hbm, v_hbm, out_q, out_k, out_v, sems):
    def columns(head):
        return slice(head * DH, head * DH + DH)

    copies = [
        pltpu.make_async_copy(src, dst, sems.at[n])
        for n, (src, dst) in enumerate(((out_q, q_hbm), (out_k, k_hbm), (out_v, v_hbm)))
    ]
    for n in range(NU):
        first = f_q[n, :16].astype(F32)
        out_q[:, columns(3 * n)] = first[:8].astype(BF16)
        out_q[:, columns(3 * n + 1)] = first[8:].astype(BF16)
        out_q[:, columns(3 * n + 2)] = f_q[n, 16:].astype(F32)[:8].astype(BF16)
    copies[0].start()
    for d in range(NZ):
        for l in range(3):
            for half in range(2):
                both = f_kv[d, 2 * l + half].astype(F32)
                up = (d - 3 * l) % NZ
                x = (up - up % 2 - 4 * half) % NZ // 2
                head = 3 * (4 * (2 * (up % 2) + half) + x) + l
                out_k[:, columns(head)] = both[:8].astype(BF16)
                out_v[:, columns(head)] = both[8:].astype(BF16)
    copies[1].start()
    copies[2].start()
    for copy in copies:
        copy.wait()


def local(query, key, value, grad_out, tile_mask, tile_order):
    anywhere = pl.BlockSpec(memory_space=pl.ANY)
    vmem = pl.BlockSpec(memory_space=pltpu.VMEM)
    smem = pl.BlockSpec(memory_space=pltpu.SMEM)
    dma = pltpu.SemaphoreType.DMA
    shape = jax.ShapeDtypeStruct
    most = 16 * 16 // SLOTS + WIDE
    operands = (query, key, value, grad_out, jnp.transpose(tile_mask, (1, 2, 0)), tile_order)
    kv, qg, picked = pl.pallas_call(
        collect,
        out_shape=(
            shape((2, NZ, 2, 128, 128), BF16),
            shape((2, NZ, 2, 128, 128), BF16),
            shape((16, 128), jnp.int32),
        ),
        in_specs=[anywhere] * 5 + [smem],
        out_specs=(vmem, vmem, vmem),
        scratch_shapes=[
            pltpu.VMEM((16, 16, H), jnp.int32),
            pltpu.VMEM((3, 3, 128, 128), BF16),
            dma, dma, dma, dma, dma((3, 3)), dma((3, 3)),
        ],
        compiler_params=pltpu.CompilerParams(
            collective_id=0, has_side_effects=True, vmem_limit_bytes=16 * 1024 * 1024
        ),
    )(*[pltpu.with_memory_space_constraint(a, pltpu.HBM) for a in operands])
    dq, acc = pl.pallas_call(
        gradients,
        out_shape=(
            shape((16, 128, 128), BF16),
            shape((16, 2, 128, 128), F32),
        ),
        in_specs=[vmem, vmem, anywhere],
        out_specs=(vmem, vmem),
        scratch_shapes=[
            pltpu.SMEM((16, 128), jnp.int32),
            pltpu.SMEM((most,), jnp.int32),
            pltpu.VMEM((most, 128 * SLOTS, 128), F32),
            pltpu.VMEM((most, 128 * SLOTS, 128), F32),
            pltpu.VMEM((most, 1, 128), F32),
            pltpu.VMEM((16, 1, 128), F32),
            pltpu.VMEM((16, 1, 128), F32),
            pltpu.VMEM((16, 1, 128), F32),
            pltpu.VMEM((16, 128, 128), F32),
            dma,
        ],
        compiler_params=pltpu.CompilerParams(vmem_limit_bytes=48 * 1024 * 1024),
    )(kv.reshape(16, 2, 128, 128), qg.reshape(16, 2, 128, 128), picked)
    f_q, f_kv = pl.pallas_call(
        give_back,
        out_shape=(shape((NU, 32, 128), BF16), shape((NZ, 6, 16, 128), BF16)),
        in_specs=[vmem] * 2,
        out_specs=(vmem, vmem),
        scratch_shapes=[
            pltpu.VMEM((2 * NU, NZ, 16, 128), BF16),
            pltpu.VMEM((2, 3, 128, 128), BF16),
            pltpu.VMEM((2, 6, NZ, 16, 128), BF16),
            pltpu.VMEM((2, NU, 32, 128), BF16),
            dma, dma, dma((2,)), dma((2, 2)), dma((2,)), dma((2,)), dma, dma,
        ],
        compiler_params=pltpu.CompilerParams(
            collective_id=1, has_side_effects=True, vmem_limit_bytes=16 * 1024 * 1024
        ),
    )(dq, acc)
    out = shape((8, H * DH), BF16)
    return pl.pallas_call(
        assemble,
        out_shape=(out, out, out),
        in_specs=[vmem] * 2,
        out_specs=(anywhere, anywhere, anywhere),
        scratch_shapes=[pltpu.VMEM((8, H * DH), BF16)] * 3 + [dma((3,))],
        compiler_params=pltpu.CompilerParams(vmem_limit_bytes=8 * 1024 * 1024),
    )(*[pltpu.with_memory_space_constraint(a, pltpu.VMEM) for a in (f_q, f_kv)])


def solution(mesh):
    placed = (P("blk", "uly"), P("blk", "uly"), P("blk", "uly"), P("blk", "uly"), P(), P())
    return jax.shard_map(
        local,
        mesh=mesh,
        in_specs=placed,
        out_specs=(P(("blk", "uly"), None), P(("blk", "uly"), None), P(("blk", "uly"), None)),
        check_vma=False,
    )
```
